128 devices in a mesh: inst: 8 (over x_hi, z), dom: 16 (over y, x_lo, core).
Axes of the slice: x: 4 (x_hi: 2, x_lo: 2; x = x_hi * 2 + x_lo), y: 4, z: 4, core: 2. Of those that a mesh axis runs over, the one named last changes fastest.
Arguments:
- flow_state: float32 [8, 6, 4, 1024, 128], P('inst', None, None, 'dom'), may hold values from -0.5 to 3, as said below
- donor_index: int32 [8, 2, 1024], P('inst', None, 'dom'), may hold values from 0 to 1023, as said below
- donor_weight: float32 [8, 2, 1024], P('inst', None, 'dom'), may hold values from 0 to 1
- span_count: int32 [16], P('dom'), may hold values from 64 to 128
Outputs:
- new_state: float32 [8, 6, 4, 1024, 128], P('inst', None, None, 'dom')
- last_update: float32 [8, 6, 4, 1024, 128], P('inst', None, None, 'dom')
The draws below stay inside these ranges and needn't reach their ends.
Inputs may be any that keep to these rules, and one draw needn't show every extreme that they name: `flow_state`: row 0 (density) lies in 0.8 to 1.2, rows 1 to 3 (momenta) in -0.5 to 0.5, row 4 (energy) in 2 to 3, row 5 (turbulence variable) in 0 to 0.4. For each instance n there is an offset o_n of 0 to 64 - 3 (the rotor's position at that instance), and for each instance, side and cell t a step e of 0 or 1, with donor_index[n, 0, t] = (t + o_n + e) mod 1024 and donor_index[n, 1, t] = (t - o_n - e - 1) mod 1024; o_n + e reaches 62 for some instance and cell on both sides.
All inputs are finite; a program needn't handle non-finite values.
Results may differ from the reference program's by a relative error of at most 0.0003.
Values sent between devices are 32-bit elements; how exact they have to be, the bound alone decides.
A program may use at most 64 MiB of HBM per device.

```python
import math
import jax
import jax.numpy as jnp
from jax import lax

AX = 4
S = 128
TD = 64
ITERS = 2
NI = 8
NT = 1024
NB = 16


def draw_flow_state(key, part):
    key = jax.random.fold_in(key, 11)
    subkeys = jax.random.split(key, 4)
    grid_shape = (NI, AX, NT, S)
    density = 1.0 + 0.08 * jnp.clip(jax.random.normal(subkeys[0], grid_shape, jnp.float32), -2.5, 2.5)
    momentum = 0.2 * jnp.clip(jax.random.normal(subkeys[1], (3,) + grid_shape, jnp.float32), -2.5, 2.5)
    energy = 2.5 + 0.2 * jnp.clip(jax.random.normal(subkeys[2], grid_shape, jnp.float32), -2.5, 2.5)
    turbulence = 0.2 + 0.08 * jnp.clip(jax.random.normal(subkeys[3], grid_shape, jnp.float32), -2.5, 2.5)
    momentum = jnp.transpose(momentum, (1, 0, 2, 3, 4))
    return jnp.concatenate([density[:, None], momentum, energy[:, None], turbulence[:, None]], axis=1).astype(jnp.float32)


def draw_donor_index(key, part):
    key = jax.random.fold_in(key, 21)
    subkeys = jax.random.split(key, 3)
    offsets = jax.random.randint(subkeys[0], (NI,), 0, TD - 2)
    top_instance = jax.random.randint(subkeys[1], (), 0, NI)
    instance_ids = jnp.arange(NI, dtype=jnp.int32)
    offsets = jnp.where(instance_ids == top_instance, TD - 3, offsets).astype(jnp.int32)
    extra = jax.random.randint(subkeys[2], (NI, 2, NT), 0, 2)
    cell_ids = jnp.arange(NT, dtype=jnp.int32)
    forced = (instance_ids[:, None, None] == top_instance) & (cell_ids[None, None, :] == 0)
    extra = jnp.where(forced, 1, extra).astype(jnp.int32)
    after_rows = (cell_ids[None, :] + offsets[:, None] + extra[:, 0]) % NT
    before_rows = (cell_ids[None, :] - offsets[:, None] - extra[:, 1] - 1) % NT
    return jnp.stack([after_rows, before_rows], axis=1).astype(jnp.int32)


def draw_donor_weight(key, part):
    key = jax.random.fold_in(key, 22)
    subkeys = jax.random.split(key, 2)
    base = jax.random.uniform(subkeys[0], (NI, 2, 1), jnp.float32, 0.2, 0.8)
    jitter = 0.15 * jax.random.uniform(subkeys[1], (NI, 2, NT), jnp.float32, -1.0, 1.0)
    return jnp.clip(base + jitter, 0.0, 1.0).astype(jnp.float32)


def touch_ends(values, own_key, smallest, largest):
    longest = values.shape.index(max(values.shape))
    spots = []
    for shift in (0, 1):
        where = [jax.random.randint(jax.random.fold_in(own_key, axis), (), 0, length) for axis, length in enumerate(values.shape)]
        where[longest] = (where[longest] + shift) % values.shape[longest]
        spots.append(tuple(where))
    return values.at[spots[0]].set(smallest).at[spots[1]].set(largest)


def setup_inputs(seed: int = 0) -> dict:
    splits = jax.random.split(jax.random.key(seed), 5)
    flow_state = draw_flow_state(jax.random.fold_in(splits[4], 71), 0)
    donor_index = draw_donor_index(jax.random.fold_in(splits[4], 71), 0)
    donor_weight = draw_donor_weight(jax.random.fold_in(splits[4], 71), 0)
    span_count = touch_ends(jax.random.randint(splits[3], (NB,), S // 2, S + 1), jax.random.fold_in(splits[3], 1), S // 2, S).astype(jnp.int32)
    return {"flow_state": flow_state, "donor_index": donor_index, "donor_weight": donor_weight, "span_count": span_count}


gamma_less = 0.4
dissip_coef = 0.1
visc_coef = 0.02
smooth_coef = 0.5
pseudo_step = 0.05
frequency = 1.0
spectral_visc = 0.1


def spectral_coefficients(row_ids, column_ids, instances):
    offset = row_ids - column_ids
    phase_angle = math.pi * offset.astype(jnp.float32) / instances
    parity = jnp.where(offset % 2 == 0, 1.0, -1.0)
    safe_sin = jnp.where(offset == 0, 1.0, jnp.sin(phase_angle))
    return jnp.where(offset == 0, 0.0, 0.5 * frequency * parity * jnp.cos(phase_angle) / safe_sin).astype(jnp.float32)


def spectral_operator(instances):
    row_ids = jnp.arange(instances, dtype=jnp.int32)
    derivative = spectral_coefficients(row_ids[:, None], row_ids[None, :], instances)
    return derivative - spectral_visc * jnp.dot(derivative, derivative, precision=lax.Precision.HIGHEST)


def cell_fluxes(current):
    density = current[0]
    velocity = current[1:4] / density
    turbulence = current[5] / density
    pressure = gamma_less * (current[4] - 0.5 * jnp.sum(current[1:4] * velocity, axis=0))
    fluxes = []
    for direction in range(3):
        speed_dir = velocity[direction]
        flux_rows = current * speed_dir
        flux_rows = flux_rows.at[1 + direction].add(pressure)
        flux_rows = flux_rows.at[4].add(pressure * speed_dir)
        fluxes.append(flux_rows)
    primitive = jnp.concatenate([velocity, turbulence[None]], axis=0)
    return fluxes, primitive


def spread_viscous(second_prim):
    zero_row = jnp.zeros_like(second_prim[0:1])
    return jnp.concatenate([zero_row, second_prim[0:3], zero_row, second_prim[3:4]], axis=0)


def axial_after(values, ghost):
    half_axial = values.shape[1] // 2
    return jnp.concatenate([values[:, 1:half_axial], ghost, values[:, half_axial + 1:], values[:, -1:]], axis=1)


def axial_before(values, ghost):
    half_axial = values.shape[1] // 2
    return jnp.concatenate([values[:, :1], values[:, :half_axial - 1], ghost, values[:, half_axial:-1]], axis=1)


def span_after(values):
    return jnp.concatenate([values[..., 1:], values[..., -1:]], axis=-1)


def span_before(values):
    return jnp.concatenate([values[..., :1], values[..., :-1]], axis=-1)


def residual_terms(padded, ghost_after, ghost_before):
    fluxes, primitive = cell_fluxes(padded)
    fluxes_after, prim_after = cell_fluxes(ghost_after)
    fluxes_before, prim_before = cell_fluxes(ghost_before)
    center = padded[:, :, 1:-1]
    prim_center = primitive[:, :, 1:-1]
    result = 0.5 * (fluxes[1][:, :, 2:] - fluxes[1][:, :, :-2])
    second_state = padded[:, :, 2:] - 2.0 * center + padded[:, :, :-2]
    second_prim = primitive[:, :, 2:] - 2.0 * prim_center + primitive[:, :, :-2]
    flux_axial = fluxes[0][:, :, 1:-1]
    result = result + 0.5 * (axial_after(flux_axial, fluxes_after[0]) - axial_before(flux_axial, fluxes_before[0]))
    second_state = second_state + axial_after(center, ghost_after) - 2.0 * center + axial_before(center, ghost_before)
    second_prim = second_prim + axial_after(prim_center, prim_after) - 2.0 * prim_center + axial_before(prim_center, prim_before)
    flux_span = fluxes[2][:, :, 1:-1]
    result = result + 0.5 * (span_after(flux_span) - span_before(flux_span))
    second_state = second_state + span_after(center) - 2.0 * center + span_before(center)
    second_prim = second_prim + span_after(prim_center) - 2.0 * prim_center + span_before(prim_center)
    return result - dissip_coef * second_state - visc_coef * spread_viscous(second_prim)


def interpolate(donor_plane, donor_rows, donor_share):
    cells_total = donor_plane.shape[1]
    near_take = jnp.take(donor_plane, donor_rows, axis=1)
    far_take = jnp.take(donor_plane, (donor_rows + 1) % cells_total, axis=1)
    share = donor_share[None, :, None]
    return (share * near_take + (1.0 - share) * far_take)[:, None]


def smooth_wrap(base, neighbour):
    return (base + smooth_coef * (jnp.roll(neighbour, 1, axis=3) + jnp.roll(neighbour, -1, axis=3))) / (1.0 + 2.0 * smooth_coef)


def reference(flow_state, donor_index, donor_weight, span_count):
    instances = flow_state.shape[0]
    half_axial = flow_state.shape[2] // 2
    cells_total = flow_state.shape[3]
    theta_block = cells_total // span_count.shape[0]
    matrix = spectral_operator(instances)
    span_pos = jnp.arange(flow_state.shape[4], dtype=jnp.int32)
    active_mask = (span_pos[None, :] < jnp.repeat(span_count, theta_block)[:, None]).astype(jnp.float32)
    current = flow_state
    update = jnp.zeros_like(flow_state)
    for sweep_index in range(ITERS):
        source = jnp.einsum("nm,mvats->nvats", matrix, current, precision=lax.Precision.HIGHEST)

        def instance_residual(inputs_tuple):
            member, member_source, donor_rows, donor_share = inputs_tuple
            padded = jnp.concatenate([member[:, :, -1:], member, member[:, :, :1]], axis=2)
            ghost_after = interpolate(member[:, half_axial], donor_rows[0], donor_share[0])
            ghost_before = interpolate(member[:, half_axial - 1], donor_rows[1], donor_share[1])
            return member_source + residual_terms(padded, ghost_after, ghost_before)

        result = lax.map(instance_residual, (current, source, donor_index, donor_weight))
        first_pass = smooth_wrap(result, result)
        smoothed = smooth_wrap(result, first_pass)
        update = active_mask * smoothed
        current = current - pseudo_step * update
    return current, update
```

```python
import functools
import math

import jax
import jax.numpy as jnp
import numpy as np
from jax import lax
from jax.experimental import pallas as pl
from jax.experimental.pallas import tpu as pltpu
from jax.sharding import PartitionSpec as P

ITERS = 2
NI = 8
NV = 6
AX = 4
PL = NV * AX
PER = PL // NI
T = 64
S = 128
PARTS = ((0, 16), (T - 16, 16), (16, T - 32))
MESH = pl.DeviceIdType.MESH


def spectral_row():
    k = np.arange(NI)[:, None] - np.arange(NI)[None, :]
    safe = np.where(k == 0, 1.0, np.sin(math.pi * k / NI))
    deriv = np.where(k == 0, 0.0, 0.5 * (-1.0) ** k * np.cos(math.pi * k / NI) / safe)
    return (deriv - 0.1 * deriv @ deriv)[:, 0]


def spectral_apply(x):
    row = spectral_row()
    even = [float(row[j] + row[j + 4]) / 2 for j in range(4)]
    odd = [float(row[j] - row[j + 4]) / 2 for j in range(4)]
    s = [x[z] + x[z + 4] for z in range(4)]
    d = [x[z] - x[z + 4] for z in range(4)]
    q0, q1 = s[0] - s[2], s[1] - s[3]
    s0 = even[0] * q0 + even[3] * q1
    s1 = even[1] * q0 + even[0] * q1
    sym = [s0, s1, -s0, -s1]
    out = [None] * NI
    for z in range(4):
        acc = None
        for y in range(4):
            coef = odd[z - y] if y <= z else -odd[4 + z - y]
            term = coef * d[y]
            acc = term if acc is None else acc + term
        out[z] = sym[z] + acc
        out[z + 4] = sym[z] - acc
    return out


def primitives(u):
    inv = 1.0 / u[0]
    vel = [u[1] * inv, u[2] * inv, u[3] * inv]
    nu = u[5] * inv
    pres = 0.4 * (u[4] - 0.5 * (u[1] * vel[0] + u[2] * vel[1] + u[3] * vel[2]))
    return vel, nu, pres


def centre_terms(u, vel, nu):
    return [
        0.1 * u[0],
        0.1 * u[1] + 0.02 * vel[0],
        0.1 * u[2] + 0.02 * vel[1],
        0.1 * u[3] + 0.02 * vel[2],
        0.1 * u[4],
        0.1 * u[5] + 0.02 * nu,
    ]


def half_flux(u, vel, pres, k):
    h = 0.5 * vel[k]
    f = [0.5 * u[1 + k], u[1] * h, u[2] * h, u[3] * h, (u[4] + pres) * h, u[5] * h]
    f[1 + k] = f[1 + k] + 0.5 * pres
    return f


def next_terms(u, k):
    vel, nu, pres = primitives(u)
    c = centre_terms(u, vel, nu)
    return [f - g for f, g in zip(half_flux(u, vel, pres, k), c)]


def prev_terms(u, k):
    vel, nu, pres = primitives(u)
    c = centre_terms(u, vel, nu)
    return [-(f + g) for f, g in zip(half_flux(u, vel, pres, k), c)]


def kernel(
    n_dom,
    n_cells,
    flow,
    idx,
    wgt,
    count,
    new_state,
    last_update,
    idx_s,
    count_s,
    idx_v,
    wgt_v,
    cur,
    in_u,
    in_n,
    w1,
    w2,
    ss,
    ww,
    n0,
    n1,
    rr,
    a2,
    b2,
    coef,
    win,
    edge,
    halo,
    redge,
    rhalo,
    qedge,
    qhalo,
    r2,
    wedge,
    whalo,
    load_sem,
    p_send,
    p_recv,
    d_send,
    d_recv,
):
    inst = lax.axis_index("inst")
    dom = lax.axis_index("dom")
    left = lax.rem(dom + n_dom - 1, n_dom)
    right = lax.rem(dom + 1, n_dom)
    work = dom + 2 - 4 * lax.rem(dom // 2, 2)

    loads = [
        pltpu.make_async_copy(source, target, load_sem.at[n])
        for n, (source, target) in enumerate(
            ((flow, cur), (idx, idx_s), (idx, idx_v), (wgt, wgt_v), (count, count_s))
        )
    ]
    for c in loads:
        c.start()
    barrier = pltpu.get_barrier_semaphore()
    for j in range(NI):
        pl.semaphore_signal(barrier, inc=1, device_id=(j, work), device_id_type=MESH)
    for d in (left, right):
        pl.semaphore_signal(barrier, inc=1, device_id=(inst, d), device_id_type=MESH)

    def cut(unit, part):
        if unit == 3 and part >= 2:
            return PARTS[2] + (part - 2, 1)
        return PARTS[part] + (0, PER)

    def piece(unit, partner, part, slot):
        at, size, k0, kn = cut(unit, part)
        rows = pl.ds(at, size)
        some = pl.ds(k0, kn)
        mine = pl.ds(PER * partner + k0, kn)
        theirs = pl.ds(PER * slot + k0, kn)
        if unit == 0:
            source, target = flow.at[mine, rows], in_u.at[slot, some, rows]
        elif unit == 1:
            source, target = w1.at[partner, some, rows], ss.at[theirs, rows]
        elif unit == 2:
            source, target = n0.at[mine, rows], in_n.at[slot, some, rows]
        else:
            source, target = w2.at[partner, some, rows], ww.at[slot, some, pl.ds(8 + at, size)]
        return pltpu.make_async_remote_copy(
            src_ref=source,
            dst_ref=target,
            send_sem=p_send.at[unit],
            recv_sem=p_recv.at[unit, part],
            device_id=(partner, work),
            device_id_type=MESH,
        )

    order = [lax.rem(inst + n, NI) for n in range(NI)]

    def send(unit, part):
        for j in order:
            piece(unit, j, part, inst).start()

    def arrive(unit, part):
        at, size, k0, kn = cut(unit, part)
        rows = pl.ds(at, size)
        if unit == 3:
            ref = ww.at[:, pl.ds(k0, kn), pl.ds(8 + at, size)]
        else:
            ref = (in_u.at[:, :, rows], ss.at[:, rows], in_n.at[:, :, rows])[unit]
        pltpu.make_async_copy(ref, ref, p_recv.at[unit, part]).wait()

    def gone(unit):
        ref = (flow, w1, n0, w2)[unit]
        pltpu.make_async_copy(ref, ref, p_send.at[unit]).wait()

    def planes(n, group, body):
        def step(i, _):
            for k in range(group):
                body(group * i + k)
            return 0

        lax.fori_loop(0, n // group, step, 0)

    def near(slot, source, target, device):
        return pltpu.make_async_remote_copy(
            src_ref=source,
            dst_ref=target,
            send_sem=d_send.at[slot],
            recv_sem=d_recv.at[slot],
            device_id=(inst, device),
            device_id_type=MESH,
        )

    def both(slot, out, back):
        return [
            near(slot, out.at[0], back.at[1], left),
            near(slot + 1, out.at[1], back.at[0], right),
        ]

    def spectral(part, source, target, extra=None, k0=0, kn=PER):
        at, size = PARTS[part]

        def step(n, _):
            k = k0 + n // (size // 16)
            t0 = pl.multiple_of(at + 16 * lax.rem(n, size // 16), 16)
            x = [source[m, k, pl.ds(t0, 16), :] for m in range(NI)]
            if extra is not None:
                x = [g + extra[m, k, pl.ds(t0, 16), :] for m, g in enumerate(x)]
            got = spectral_apply(x)
            for m in range(NI):
                target[m, k, pl.ds(t0, 16), :] = got[m]
            return 0

        lax.fori_loop(0, kn * size // 16, step, 0)

    lane = lax.broadcasted_iota(jnp.int32, (8, S), 1)
    first_lane = lane == 0
    last_lane = lane == S - 1

    def inside(out, start, stop):
        def tile(i, _):
            t0 = pl.multiple_of(8 * i, 8)
            total = []
            first = []
            second = []
            for a in range(AX):
                u = [cur[v * AX + a, pl.ds(t0, 8), :] for v in range(NV)]
                vel, nu, pres = primitives(u)
                c = centre_terms(u, vel, nu)
                f1 = half_flux(u, vel, pres, 0)
                first.append([f - g for f, g in zip(f1, c)])
                second.append([f + g for f, g in zip(f1, c)])
                f2 = half_flux(u, vel, pres, 1)
                f3 = half_flux(u, vel, pres, 2)
                mine = []
                for v in range(NV):
                    a2[v * AX + a, pl.ds(t0 + 8, 8), :] = f2[v] - c[v]
                    b2[v * AX + a, pl.ds(t0 + 8, 8), :] = f2[v] + c[v]
                    up = f3[v] - c[v]
                    down = f3[v] + c[v]
                    after = jnp.where(last_lane, up, pltpu.roll(up, S - 1, 1))
                    before = jnp.where(first_lane, down, pltpu.roll(down, 1, 1))
                    mine.append(6.0 * c[v] + (after - before))
                total.append(mine)
            for a in range(AX):
                for v in range(NV):
                    r = total[a][v]
                    if a == AX - 1:
                        r = r + first[a][v]
                    elif a != AX // 2 - 1:
                        r = r + first[a + 1][v]
                    if a == 0:
                        r = r - second[a][v]
                    elif a != AX // 2:
                        r = r - second[a - 1][v]
                    out[v * AX + a, pl.ds(t0, 8), :] = r
            return 0

        lax.fori_loop(start, stop, tile, 0)

    def around(out, it, layers, windows, base):
        for c in layers:
            c.wait_recv()
        low = prev_terms([halo[it, 0, AX * v : AX * v + AX, :] for v in range(NV)], 1)
        high = next_terms([halo[it, 1, AX * v : AX * v + AX, :] for v in range(NV)], 1)
        for v in range(NV):
            for a in range(AX):
                b2[v * AX + a, 7:8, :] = -low[v][a : a + 1]
                a2[v * AX + a, T + 8 : T + 9, :] = high[v][a : a + 1]

        def plane(p):
            out[p] += a2[p, 9 : T + 9] - b2[p, 7 : T + 7]

        planes(PL, 3, plane)
        for c in windows:
            c.wait_recv()

        def ghosts(i, _):
            t0 = pl.multiple_of(8 * i, 8)
            for side in range(2):
                taps = [coef[side, n, pl.ds(t0, 8), :] for n in range(3)]
                u = []
                for v in range(NV):
                    g = taps[0] * win[it, side, v, pl.ds(base[side] + t0, 8), :]
                    g = g + taps[1] * win[it, side, v, pl.ds(base[side] + t0 + 1, 8), :]
                    g = g + taps[2] * win[it, side, v, pl.ds(base[side] + t0 + 2, 8), :]
                    u.append(g)
                terms = next_terms(u, 0) if side == 0 else prev_terms(u, 0)
                for v in range(NV):
                    out[v * AX + 1 + side, pl.ds(t0, 8), :] += terms[v]
            return 0

        lax.fori_loop(0, T // 8, ghosts, 0)

    def rims(it):
        edge[it, 0, 0:PL] = cur[:, 0, :]
        edge[it, 1, 0:PL] = cur[:, T - 1, :]
        for side in range(2):
            edge[it, side, PL : PL + 8] = jnp.broadcast_to(active, (8, S))
        for v in range(NV):
            win[it, 0, v, 0:T] = cur[v * AX + 2]
            win[it, 1, v, T : 2 * T] = cur[v * AX + 1]
        layers = both(10 * it, edge.at[it], halo.at[it])
        windows = [
            near(10 * it + 2, win.at[it, 0, :, 0:T], win.at[it, 0, :, T : 2 * T], left),
            near(10 * it + 3, win.at[it, 1, :, T : 2 * T], win.at[it, 1, :, 0:T], right),
        ]
        return layers, windows

    pl.semaphore_wait(barrier, NI + 2)
    send(0, 0)
    send(0, 1)
    for c in loads:
        c.wait()
    active = jnp.where(lax.broadcasted_iota(jnp.int32, (1, S), 1) < count_s[0], 1.0, 0.0)
    layers, windows = rims(0)
    for c in layers + windows:
        c.start()
    send(0, 2)

    def least(t, low):
        cell = dom * T + t
        gaps = (idx_s[0, t] - cell, cell - 1 - idx_s[1, t])
        gaps = [jnp.where(g < 0, g + n_cells, g) for g in gaps]
        return jnp.minimum(low[0], gaps[0]), jnp.minimum(low[1], gaps[1])

    start = (jnp.int32(n_cells), jnp.int32(n_cells))
    offset = [jnp.clip(x, 0, T - 2) for x in lax.fori_loop(0, T, least, start)]
    base = [offset[0], T - 2 - offset[1]]
    eye = lax.broadcasted_iota(jnp.int32, (T, T), 0) == lax.broadcasted_iota(
        jnp.int32, (T, T), 1
    )
    for side in range(2):
        cell = dom * T + lax.broadcasted_iota(jnp.int32, (1, T), 1)
        row = idx_v[side : side + 1, :]
        gap = row - cell if side == 0 else cell - 1 - row
        gap = jnp.where(gap < 0, gap + n_cells, gap)
        step = jnp.where(gap > offset[side], 1.0, 0.0)
        w = wgt_v[side : side + 1, :]
        taps = [(1.0 - step) * w, step * w + (1.0 - step) * (1.0 - w), step * (1.0 - w)]
        if side == 1:
            taps = [step * w, (1.0 - step) * w + step * (1.0 - w), (1.0 - step) * (1.0 - w)]
        for i, tap in enumerate(taps):
            column = jnp.sum(jnp.where(eye, tap, 0.0), axis=1, keepdims=True)
            coef[side, i] = jnp.broadcast_to(column, (T, S))

    half = T // 16
    inside(n0, 0, half)
    for part in (0, 1):
        arrive(0, part)
        spectral(part, in_u, w1)
        send(1, part)
    inside(n0, half, 2 * half)
    arrive(0, 2)
    spectral(2, in_u, w1)
    send(1, 2)
    around(n0, 0, layers, windows, base)
    for part in (0, 1, 2):
        send(2, part)

    arrive(1, 0)
    arrive(1, 1)
    for n, t in enumerate((0, 1, T - 2, T - 1)):
        redge[0, n // 2, n % 2] = n0[:, t, :] + ss[:, t, :]
    rim = both(4, redge.at[0], rhalo.at[0])
    for c in rim:
        c.start()
    arrive(1, 2)

    def add_source(p):
        rr[p, 8 : T + 8] = n0[p] + ss[p]

    planes(PL, 3, add_source)
    for c in rim:
        c.wait()
    for n, t in enumerate((-2, -1, T, T + 1)):
        rr[:, 8 + t, :] = rhalo[0, n // 2, n % 2]
    gone(0)
    for c in layers + windows:
        c.wait_send()

    def smoothed(ref, p):
        return (
            0.625 * ref[p, 8 : T + 8]
            + 0.125 * (ref[p, 7 : T + 7] + ref[p, 9 : T + 9])
            + 0.0625 * (ref[p, 6 : T + 6] + ref[p, 10 : T + 10])
        )

    def first_update(p):
        cur[p] = cur[p] - 0.05 * (smoothed(rr, p) * active)

    planes(PL, 2, first_update)
    layers, windows = rims(1)
    for c in layers + windows:
        c.start()

    for part in (0, 1):
        arrive(2, part)
        spectral(part, in_n, w2, w1)
        send(3, part)
    inside(n1, 0, half)
    arrive(2, 2)
    for k in range(PER):
        spectral(2, in_n, w2, w1, k, 1)
        send(3, 2 + k)
    inside(n1, half, 2 * half)
    around(n1, 1, layers, windows, base)
    for n, t in enumerate((0, 1, T - 2, T - 1)):
        for k in range(PER):
            rows = [n1[PER * j + k, t : t + 1, :] + ss[PER * j + k, t : t + 1, :] for j in range(NI)]
            qedge[n // 2, n % 2, k] = jnp.concatenate(rows, axis=0)
    rim = both(6, qedge, qhalo)
    for c in rim:
        c.start()

    arrive(3, 0)
    arrive(3, 1)
    for n in range(4):
        for k in range(PER):
            wedge[0, n, k] = ww[:, k, 8 + n, :]
            wedge[1, n, k] = ww[:, k, T + 4 + n, :]
    far = both(8, wedge, whalo)
    for c in far:
        c.start()
    for c in rim + far:
        c.wait()
    for n in range(2):
        for k in range(PER):
            ww[:, k, 6 + n, :] = whalo[0, 2 + n, k]
            ww[:, k, T + 8 + n, :] = whalo[1, n, k]
    for side in range(2):
        h = [whalo[side, n] for n in range(4)]
        e = [wedge[side, n] for n in range(4)]
        line = h + e[:2] if side == 0 else e[2:] + h
        mask = halo[0, side, PL : PL + 1, :]
        for n in range(2):
            x = line[n : n + 5]
            z = 0.625 * x[2] + 0.125 * (x[1] + x[3]) + 0.0625 * (x[0] + x[4])
            t = n - 2 if side == 0 else T + n
            r = qhalo[side, n] - 0.05 * (z * mask)
            for k in range(PER):
                r2[:, k, 8 + t, :] = r[k]

    for k in range(PER):
        arrive(3, 2 + k)

        def second_update(j, k=k):
            p = PER * j + k
            z = (
                0.625 * ww[j, k, 8 : T + 8]
                + 0.125 * (ww[j, k, 7 : T + 7] + ww[j, k, 9 : T + 9])
                + 0.0625 * (ww[j, k, 6 : T + 6] + ww[j, k, 10 : T + 10])
            )
            r2[j, k, 8 : T + 8] = n1[p] + ss[p] - 0.05 * (z * active)
            y = (
                0.625 * r2[j, k, 8 : T + 8]
                + 0.125 * (r2[j, k, 7 : T + 7] + r2[j, k, 9 : T + 9])
                + 0.0625 * (r2[j, k, 6 : T + 6] + r2[j, k, 10 : T + 10])
            )
            update = y * active
            last_update[p] = update
            new_state[p] = cur[p] - 0.05 * update

        planes(NI, 2, second_update)

    for c in layers + windows:
        c.wait_send()
    for unit in (1, 2, 3):
        gone(unit)


def local(n_dom, flow_state, donor_index, donor_weight, span_count):
    shape = (PL, T, S)
    padded = (PL, T + 16, S)
    pieces = (NI, PER, T, S)
    f32 = jnp.float32
    vmem = pl.BlockSpec(memory_space=pltpu.VMEM)
    anywhere = pl.BlockSpec(memory_space=pltpu.HBM)
    new_state, last_update = pl.pallas_call(
        functools.partial(kernel, n_dom, n_dom * T),
        out_shape=[jax.ShapeDtypeStruct(shape, f32)] * 2,
        in_specs=[anywhere] * 4,
        out_specs=[vmem, vmem],
        scratch_shapes=[
            pltpu.SMEM((2, T), jnp.int32),
            pltpu.SMEM((1,), jnp.int32),
            pltpu.VMEM((2, T), jnp.int32),
            pltpu.VMEM((2, T), f32),
            pltpu.VMEM(shape, f32),
            pltpu.VMEM(pieces, f32),
            pltpu.VMEM(pieces, f32),
            pltpu.VMEM(pieces, f32),
            pltpu.VMEM(pieces, f32),
            pltpu.VMEM(shape, f32),
            pltpu.VMEM((NI, PER, T + 16, S), f32),
            pltpu.VMEM(shape, f32),
            pltpu.VMEM(shape, f32),
            pltpu.VMEM(padded, f32),
            pltpu.VMEM(padded, f32),
            pltpu.VMEM(padded, f32),
            pltpu.VMEM((2, 3, T, S), f32),
            pltpu.VMEM((ITERS, 2, NV, 2 * T, S), f32),
            pltpu.VMEM((ITERS, 2, PL + 8, S), f32),
            pltpu.VMEM((ITERS, 2, PL + 8, S), f32),
            pltpu.VMEM((1, 2, 2, PL, S), f32),
            pltpu.VMEM((1, 2, 2, PL, S), f32),
            pltpu.VMEM((2, 2, PER, NI, S), f32),
            pltpu.VMEM((2, 2, PER, NI, S), f32),
            pltpu.VMEM((NI, PER, T + 16, S), f32),
            pltpu.VMEM((2, 4, PER, NI, S), f32),
            pltpu.VMEM((2, 4, PER, NI, S), f32),
            pltpu.SemaphoreType.DMA((5,)),
            pltpu.SemaphoreType.DMA((4,)),
            pltpu.SemaphoreType.DMA((4, 2 + PER)),
            pltpu.SemaphoreType.DMA((20,)),
            pltpu.SemaphoreType.DMA((20,)),
        ],
        compiler_params=pltpu.CompilerParams(
            collective_id=0, has_side_effects=True, vmem_limit_bytes=52 * 1024 * 1024
        ),
        cost_estimate=pl.CostEstimate(
            flops=20_000_000, bytes_accessed=3 * PL * T * S * 4, transcendentals=0
        ),
    )(flow_state.reshape(shape), donor_index[0], donor_weight[0], span_count)
    whole = (1, NV, AX, T, S)
    return new_state.reshape(whole), last_update.reshape(whole)


def solution(mesh):
    placed = (
        P("inst", None, None, "dom", None),
        P("inst", None, "dom"),
        P("inst", None, "dom"),
        P("dom"),
    )
    return jax.shard_map(
        functools.partial(local, mesh.shape["dom"]),
        mesh=mesh,
        in_specs=placed,
        out_specs=(P("inst", None, None, "dom", None), P("inst", None, None, "dom", None)),
        check_vma=False,
    )
```

```python
import functools
import math

import jax
import jax.numpy as jnp
import numpy as np
from jax import lax
from jax.experimental import pallas as pl
from jax.experimental.pallas import tpu as pltpu
from jax.sharding import PartitionSpec as P

ITERS = 2
NI = 8
NV = 6
AX = 4
PL = NV * AX
T = 64
S = 128
ZN = 4
SLAB = T // ZN
ORDER = (1, 2, 0, 3)
MESH = pl.DeviceIdType.MESH


def spectral_row():
    k = np.arange(NI)[:, None] - np.arange(NI)[None, :]
    safe = np.where(k == 0, 1.0, np.sin(math.pi * k / NI))
    deriv = np.where(k == 0, 0.0, 0.5 * (-1.0) ** k * np.cos(math.pi * k / NI) / safe)
    return (deriv - 0.1 * deriv @ deriv)[:, 0]


def spectral_apply(x):
    row = spectral_row()
    even = [float(row[j] + row[j + 4]) / 2 for j in range(4)]
    odd = [float(row[j] - row[j + 4]) / 2 for j in range(4)]
    s = [x[z] + x[z + 4] for z in range(4)]
    d = [x[z] - x[z + 4] for z in range(4)]
    q0, q1 = s[0] - s[2], s[1] - s[3]
    s0 = even[0] * q0 + even[3] * q1
    s1 = even[1] * q0 + even[0] * q1
    sym = [s0, s1, -s0, -s1]
    out = [None] * NI
    for z in range(4):
        acc = None
        for y in range(4):
            coef = odd[z - y] if y <= z else -odd[4 + z - y]
            term = coef * d[y]
            acc = term if acc is None else acc + term
        out[z] = sym[z] + acc
        out[z + 4] = sym[z] - acc
    return out


def primitives(u):
    inv = 1.0 / u[0]
    vel = [u[1] * inv, u[2] * inv, u[3] * inv]
    nu = u[5] * inv
    pres = 0.4 * (u[4] - 0.5 * (u[1] * vel[0] + u[2] * vel[1] + u[3] * vel[2]))
    return vel, nu, pres


def centre_terms(u, vel, nu):
    return [
        0.1 * u[0],
        0.1 * u[1] + 0.02 * vel[0],
        0.1 * u[2] + 0.02 * vel[1],
        0.1 * u[3] + 0.02 * vel[2],
        0.1 * u[4],
        0.1 * u[5] + 0.02 * nu,
    ]


def half_flux(u, vel, pres, k):
    h = 0.5 * vel[k]
    f = [0.5 * u[1 + k], u[1] * h, u[2] * h, u[3] * h, (u[4] + pres) * h, u[5] * h]
    f[1 + k] = f[1 + k] + 0.5 * pres
    return f


def next_terms(u, k):
    vel, nu, pres = primitives(u)
    c = centre_terms(u, vel, nu)
    return [f - g for f, g in zip(half_flux(u, vel, pres, k), c)]


def prev_terms(u, k):
    vel, nu, pres = primitives(u)
    c = centre_terms(u, vel, nu)
    return [-(f + g) for f, g in zip(half_flux(u, vel, pres, k), c)]


def kernel(
    n_dom,
    n_cells,
    flow,
    idx,
    wgt,
    count,
    new_state,
    last_update,
    idx_s,
    count_s,
    idx_v,
    wgt_v,
    cur,
    in_u,
    in_n,
    w1,
    w2,
    ss,
    ww,
    n0,
    n1,
    rr,
    a2,
    b2,
    coef,
    win,
    edge,
    halo,
    redge,
    rhalo,
    qedge,
    qhalo,
    wedge,
    whalo,
    slab_n,
    slab_a,
    slab_b,
    slab_out,
    slab_in,
    load_sem,
    p_send,
    p_recv,
    d_send,
    d_recv,
):
    inst = lax.axis_index("inst")
    dom = lax.axis_index("dom")
    left = lax.rem(dom + n_dom - 1, n_dom)
    right = lax.rem(dom + 1, n_dom)

    def flip(d):
        return d + 2 - 4 * lax.rem(d // 2, 2)

    work = flip(dom)
    body, place = inst // ZN, lax.rem(inst, ZN)
    at_start = jnp.where(place == 0, 1, 0)
    at_end = jnp.where(place == ZN - 1, 1, 0)
    before = flip(lax.rem(work + n_dom - at_start, n_dom))
    beyond = flip(lax.rem(work + at_end, n_dom))
    below = (body * ZN + lax.rem(place + ZN - 1, ZN), before)
    above = (body * ZN + lax.rem(place + 1, ZN), beyond)

    loads = [
        pltpu.make_async_copy(source, target, load_sem.at[n])
        for n, (source, target) in enumerate(
            ((flow, cur), (idx, idx_s), (idx, idx_v), (wgt, wgt_v), (count, count_s))
        )
    ]
    for c in loads:
        c.start()
    barrier = pltpu.get_barrier_semaphore()
    for j in range(NI):
        pl.semaphore_signal(barrier, inc=1, device_id=(j, work), device_id_type=MESH)
    for device in ((inst, left), (inst, right), below, above):
        pl.semaphore_signal(barrier, inc=1, device_id=device, device_id_type=MESH)

    def remote(source, target, send, recv, device):
        return pltpu.make_async_remote_copy(
            src_ref=source,
            dst_ref=target,
            send_sem=send,
            recv_sem=recv,
            device_id=device,
            device_id_type=MESH,
        )

    def piece(unit, partner, part, slot):
        side, slab = partner // ZN, lax.rem(partner, ZN)
        row = 1 + side if part == 0 else (AX - 1) * side
        mine = pl.ds(pl.multiple_of(SLAB * slab, SLAB), SLAB)
        spot = 2 * part + slot // ZN
        at = SLAB * lax.rem(slot, ZN)
        if unit == 0:
            source, target = flow.at[:, row, mine], in_u.at[part, slot]
        elif unit == 1:
            source = w1.at[part, partner]
            target = ss.at[spot, :, pl.ds(pl.multiple_of(at, SLAB), SLAB)]
        elif unit == 2:
            source, target = n0.at[:, row, mine], in_n.at[slot]
        else:
            source = w2.at[part, partner]
            target = ww.at[spot, :, pl.ds(pl.multiple_of(at + 8, 8), SLAB)]
        return remote(source, target, p_send.at[unit], p_recv.at[unit, part], (partner, work))

    order = [lax.rem(inst + n, NI) for n in range(NI)]

    def send(unit, part):
        for j in order:
            piece(unit, j, part, inst).start()

    def arrive(unit, part):
        spots = pl.ds(2 * part, 2)
        ref = (in_u.at[part], ss.at[spots], in_n, ww.at[spots, :, pl.ds(8, T)])[unit]
        pltpu.make_async_copy(ref, ref, p_recv.at[unit, part]).wait()

    def gone(unit):
        ref = (flow, w1, n0.at[:, 1:3], w2)[unit]
        pltpu.make_async_copy(ref, ref, p_send.at[unit]).wait()

    def near(slot, source, target, device):
        return remote(source, target, d_send.at[slot], d_recv.at[slot], (inst, device))

    def both(slot, out, back):
        return [near(slot, out(0), back(1), left), near(slot + 1, out(1), back(0), right)]

    def start(copies):
        for c in copies:
            c.start()
        return copies

    def over(n, body):
        def step(i, _):
            body(i)
            return 0

        lax.fori_loop(0, n, step, 0)

    lane = lax.broadcasted_iota(jnp.int32, (8, S), 1)
    first_lane = lane == 0
    last_lane = lane == S - 1

    def spanwise(f, c):
        out = []
        for g, h in zip(f, c):
            up, down = g - h, g + h
            after = jnp.where(last_lane, up, pltpu.roll(up, S - 1, 1))
            prior = jnp.where(first_lane, down, pltpu.roll(down, 1, 1))
            out.append(6.0 * h + (after - prior))
        return out

    def spectral(part, target, plus=None):
        def variable(v):
            for t0 in range(0, SLAB, 8):
                rows = slice(t0, t0 + 8)
                if plus is None:
                    x = [in_u[part, m, v, rows, :] for m in range(NI)]
                else:
                    x = [w1[part, m, v, rows, :] + plus(m, v, t0) for m in range(NI)]
                for m, g in enumerate(spectral_apply(x)):
                    target[part, m, v, rows, :] = g

        over(NV, variable)

    def inside(out, first_tile, last_tile):
        def tile(i, _):
            t0 = pl.multiple_of(8 * i, 8)
            total = []
            first = []
            second = []
            for a in range(AX):
                u = [cur[v, a, pl.ds(t0, 8), :] for v in range(NV)]
                vel, nu, pres = primitives(u)
                c = centre_terms(u, vel, nu)
                f1 = half_flux(u, vel, pres, 0)
                first.append([f - g for f, g in zip(f1, c)])
                second.append([f + g for f, g in zip(f1, c)])
                f2 = half_flux(u, vel, pres, 1)
                for v in range(NV):
                    a2[v, a, pl.ds(t0 + 8, 8), :] = f2[v] - c[v]
                    b2[v, a, pl.ds(t0 + 8, 8), :] = f2[v] + c[v]
                total.append(spanwise(half_flux(u, vel, pres, 2), c))
            for a in range(AX):
                for v in range(NV):
                    r = total[a][v]
                    if a == AX - 1:
                        r = r + first[a][v]
                    elif a != AX // 2 - 1:
                        r = r + first[a + 1][v]
                    if a == 0:
                        r = r - second[a][v]
                    elif a != AX // 2:
                        r = r - second[a - 1][v]
                    out[v, a, pl.ds(t0, 8), :] = r
            return 0

        lax.fori_loop(first_tile, last_tile, tile, 0)

    def around(out, it, layers, windows):
        for c in layers:
            c.wait_recv()
        low = prev_terms([halo[it, 0, v] for v in range(NV)], 1)
        high = next_terms([halo[it, 1, v] for v in range(NV)], 1)
        for v in range(NV):
            for a in range(AX):
                b2[v, a, 7:8, :] = -low[v][a : a + 1]
                a2[v, a, T + 8 : T + 9, :] = high[v][a : a + 1]

        def variable(v):
            for a in range(AX):
                out[v, a] += a2[v, a, 9 : T + 9] - b2[v, a, 7 : T + 7]

        over(NV, variable)
        for c in windows:
            c.wait_recv()

        def ghosts(i):
            t0 = pl.multiple_of(8 * i, 8)
            for side in range(2):
                taps = [coef[side, n, pl.ds(t0, 8), :] for n in range(3)]
                u = []
                for v in range(NV):
                    g = taps[0] * win[it, side, v, pl.ds(base[side] + t0, 8), :]
                    g = g + taps[1] * win[it, side, v, pl.ds(base[side] + t0 + 1, 8), :]
                    g = g + taps[2] * win[it, side, v, pl.ds(base[side] + t0 + 2, 8), :]
                    u.append(g)
                terms = next_terms(u, 0) if side == 0 else prev_terms(u, 0)
                for v in range(NV):
                    out[v, 1 + side, pl.ds(t0, 8), :] += terms[v]

        over(T // 8, ghosts)

    def outer_layers(it):
        for side, t in enumerate((0, T - 1)):
            for v in range(NV):
                edge[it, side, v] = cur[v, :, t, :]
            edge[it, side, NV] = jnp.broadcast_to(active, (AX, S))
        return start(
            both(10 * it, lambda side: edge.at[it, side], lambda side: halo.at[it, side])
        )

    def interface_rows(it):
        for v in range(NV):
            win[it, 0, v, 0:T] = cur[v, 2]
            win[it, 1, v, T : 2 * T] = cur[v, 1]
        return start(
            [
                near(10 * it + 2, win.at[it, 0, :, 0:T], win.at[it, 0, :, T : 2 * T], left),
                near(10 * it + 3, win.at[it, 1, :, T : 2 * T], win.at[it, 1, :, 0:T], right),
            ]
        )

    def rim_of(slot, out, back, spots):
        return start(
            both(slot, lambda side: out.at[side, :, spots], lambda side: back.at[side, :, spots])
        )

    FRONT, REST = pl.ds(0, 2), pl.ds(2, 2)

    pl.semaphore_wait(barrier, NI + 4)
    for part in range(2):
        send(0, part)
    for c in loads:
        c.wait()
    active = jnp.where(lax.broadcasted_iota(jnp.int32, (1, S), 1) < count_s[0], 1.0, 0.0)
    layers = outer_layers(0)
    windows = interface_rows(0)

    def least(t, low):
        cell = dom * T + t
        gaps = (idx_s[0, t] - cell, cell - 1 - idx_s[1, t])
        gaps = [jnp.where(g < 0, g + n_cells, g) for g in gaps]
        return jnp.minimum(low[0], gaps[0]), jnp.minimum(low[1], gaps[1])

    most = (jnp.int32(n_cells), jnp.int32(n_cells))
    offset = [jnp.clip(x, 0, T - 2) for x in lax.fori_loop(0, T, least, most)]
    base = [offset[0], T - 2 - offset[1]]
    eye = lax.broadcasted_iota(jnp.int32, (T, T), 0) == lax.broadcasted_iota(
        jnp.int32, (T, T), 1
    )
    for side in range(2):
        cell = dom * T + lax.broadcasted_iota(jnp.int32, (1, T), 1)
        row = idx_v[side : side + 1, :]
        gap = row - cell if side == 0 else cell - 1 - row
        gap = jnp.where(gap < 0, gap + n_cells, gap)
        step = jnp.where(gap > offset[side], 1.0, 0.0)
        w = wgt_v[side : side + 1, :]
        taps = [(1.0 - step) * w, step * w + (1.0 - step) * (1.0 - w), step * (1.0 - w)]
        if side == 1:
            taps = [step * w, (1.0 - step) * w + step * (1.0 - w), (1.0 - step) * (1.0 - w)]
        for i, tap in enumerate(taps):
            column = jnp.sum(jnp.where(eye, tap, 0.0), axis=1, keepdims=True)
            coef[side, i] = jnp.broadcast_to(column, (T, S))

    half = T // 16
    inside(n0, 0, half)
    arrive(0, 0)
    spectral(0, w1)
    send(1, 0)
    arrive(0, 1)
    for v in range(NV):
        slab_out[0, v] = in_u[1, :, v, 0, :]
        slab_out[1, v] = in_u[1, :, v, SLAB - 1, :]
    slabs = start(
        [
            remote(slab_out.at[0], slab_in.at[1], d_send.at[18], d_recv.at[18], below),
            remote(slab_out.at[1], slab_in.at[0], d_send.at[19], d_recv.at[19], above),
        ]
    )
    spectral(1, w1)
    send(1, 1)
    inside(n0, half, 2 * half)
    around(n0, 0, layers, windows)
    send(2, 0)

    toward = jnp.where(body == 0, 1.0, -1.0)

    def slab_inside(m):
        for t0 in range(0, SLAB, 8):
            rows = slice(t0, t0 + 8)
            u = [in_u[0, m, v, rows, :] for v in range(NV)]
            vel, nu, pres = primitives(u)
            c1 = centre_terms(u, vel, nu)
            f1 = half_flux(u, vel, pres, 0)
            u = [in_u[1, m, v, rows, :] for v in range(NV)]
            vel, nu, pres = primitives(u)
            c = centre_terms(u, vel, nu)
            f = half_flux(u, vel, pres, 0)
            f2 = half_flux(u, vel, pres, 1)
            r = spanwise(half_flux(u, vel, pres, 2), c)
            for v in range(NV):
                slab_a[m, v, t0 : t0 + 8, :] = f2[v] - c[v]
                slab_b[m, v, t0 + 8 : t0 + 16, :] = f2[v] + c[v]
                slab_n[m, v, rows, :] = r[v] + (toward * (f1[v] - f[v]) - (c1[v] + c[v]))

    over(NI, slab_inside)
    for c in slabs:
        c.wait()
    low = prev_terms([slab_in[0, v] for v in range(NV)], 1)
    high = next_terms([slab_in[1, v] for v in range(NV)], 1)
    for v in range(NV):
        slab_b[:, v, 7, :] = -low[v]
        slab_a[:, v, SLAB, :] = high[v]

    def outer(m, v, t0):
        return slab_n[m, v, t0 : t0 + 8, :] + (
            slab_a[m, v, t0 + 1 : t0 + 9, :] - slab_b[m, v, t0 + 7 : t0 + 15, :]
        )

    spectral(1, w2, outer)
    send(3, 1)

    def keep_rows(out, spots, times, value):
        for spot in spots:
            for n, t in enumerate(times):
                out[n // (len(times) // 2), n % (len(times) // 2), spot] = value(spot, t)

    def put_rows(back, spots, times):
        for spot in spots:
            for n, t in enumerate(times):
                rr[spot, :, 8 + t, :] = back[n // 2, n % 2, spot]

    ends = (0, 1, T - 2, T - 1)
    outside = (-2, -1, T, T + 1)

    def smoothed(ref, spot, v):
        return (
            0.625 * ref[spot, v, 8 : T + 8]
            + 0.125 * (ref[spot, v, 7 : T + 7] + ref[spot, v, 9 : T + 9])
            + 0.0625 * (ref[spot, v, 6 : T + 6] + ref[spot, v, 10 : T + 10])
        )

    def sums(spots):
        def variable(v):
            for spot in spots:
                rr[spot, v, 8 : T + 8] = n0[v, ORDER[spot]] + ss[spot, v]

        over(NV, variable)

    def first_update(spots):
        def variable(v):
            for spot in spots:
                a = ORDER[spot]
                cur[v, a] = cur[v, a] - 0.05 * (smoothed(rr, spot, v) * active)

        over(NV, variable)

    def first_sum(spot, t):
        return n0[:, ORDER[spot], t, :] + ss[spot, :, t, :]

    arrive(1, 0)
    keep_rows(redge, (0, 1), ends, first_sum)
    rim = rim_of(4, redge, rhalo, FRONT)
    sums((0, 1))
    arrive(1, 1)
    keep_rows(redge, (2, 3), ends, first_sum)
    rim2 = rim_of(6, redge, rhalo, REST)
    for c in rim:
        c.wait()
    put_rows(rhalo, (0, 1), outside)
    gone(0)
    for c in layers + windows:
        c.wait_send()
    first_update((0, 1))
    windows = interface_rows(1)
    sums((2, 3))
    for c in rim2:
        c.wait()
    put_rows(rhalo, (2, 3), outside)
    first_update((2, 3))
    layers = outer_layers(1)

    arrive(2, 0)
    spectral(0, w2, lambda m, v, t0: in_n[m, v, t0 : t0 + 8, :])
    send(3, 0)
    inside(n1, 0, 2 * half)
    around(n1, 1, layers, windows)
    keep_rows(qedge, range(4), ends, lambda spot, t: n1[:, ORDER[spot], t, :] + ss[spot, :, t, :])
    rim = start(both(8, lambda side: qedge.at[side], lambda side: qhalo.at[side]))

    far_rows = (0, 1, 2, 3, T - 4, T - 3, T - 2, T - 1)

    def last_source(spot, t):
        return ww[spot, :, 8 + t, :]

    arrive(3, 1)
    keep_rows(wedge, (2, 3), far_rows, last_source)
    far2 = rim_of(14, wedge, whalo, REST)
    arrive(3, 0)
    keep_rows(wedge, (0, 1), far_rows, last_source)
    far = rim_of(16, wedge, whalo, FRONT)
    for c in rim:
        c.wait()

    def second_update(spots):
        for spot in spots:
            for n in range(2):
                ww[spot, :, 6 + n, :] = whalo[0, 2 + n, spot]
                ww[spot, :, T + 8 + n, :] = whalo[1, n, spot]
            for side in range(2):
                h = [whalo[side, n, spot] for n in range(4)]
                e = [wedge[side, n, spot] for n in range(4)]
                line = h + e[:2] if side == 0 else e[2:] + h
                mask = halo[0, side, NV, 0:1, :]
                for n in range(2):
                    x = line[n : n + 5]
                    z = 0.625 * x[2] + 0.125 * (x[1] + x[3]) + 0.0625 * (x[0] + x[4])
                    t = n - 2 if side == 0 else T + n
                    rr[spot, :, 8 + t, :] = qhalo[side, n, spot] - 0.05 * (z * mask)

        def variable(v):
            for spot in spots:
                a = ORDER[spot]
                rr[spot, v, 8 : T + 8] = (
                    n1[v, a] + ss[spot, v] - 0.05 * (smoothed(ww, spot, v) * active)
                )
                update = smoothed(rr, spot, v) * active
                last_update[v, a] = update
                new_state[v, a] = cur[v, a] - 0.05 * update

        over(NV, variable)

    for c in far2:
        c.wait()
    second_update((2, 3))
    for c in far:
        c.wait()
    second_update((0, 1))

    for c in layers + windows:
        c.wait_send()
    for unit in (1, 2, 3):
        gone(unit)


def local(n_dom, flow_state, donor_index, donor_weight, span_count):
    shape = (NV, AX, T, S)
    padded = (NV, AX, T + 16, S)
    pieces = (2, NI, NV, SLAB, S)
    turned = (AX, NV, T + 16, S)
    f32 = jnp.float32
    anywhere = pl.BlockSpec(memory_space=pl.ANY)
    vmem = pl.BlockSpec(memory_space=pltpu.VMEM)
    new_state, last_update = pl.pallas_call(
        functools.partial(kernel, n_dom, n_dom * T),
        out_shape=[jax.ShapeDtypeStruct(shape, f32)] * 2,
        in_specs=[anywhere] * 4,
        out_specs=[vmem, vmem],
        scratch_shapes=[
            pltpu.SMEM((2, T), jnp.int32),
            pltpu.SMEM((1,), jnp.int32),
            pltpu.VMEM((2, T), jnp.int32),
            pltpu.VMEM((2, T), f32),
            pltpu.VMEM(shape, f32),
            pltpu.VMEM(pieces, f32),
            pltpu.VMEM((NI, NV, SLAB, S), f32),
            pltpu.VMEM(pieces, f32),
            pltpu.VMEM(pieces, f32),
            pltpu.VMEM((AX, NV, T, S), f32),
            pltpu.VMEM(turned, f32),
            pltpu.VMEM(shape, f32),
            pltpu.VMEM(shape, f32),
            pltpu.VMEM(turned, f32),
            pltpu.VMEM(padded, f32),
            pltpu.VMEM(padded, f32),
            pltpu.VMEM((2, 3, T, S), f32),
            pltpu.VMEM((ITERS, 2, NV, 2 * T, S), f32),
            pltpu.VMEM((ITERS, 2, NV + 1, AX, S), f32),
            pltpu.VMEM((ITERS, 2, NV + 1, AX, S), f32),
            pltpu.VMEM((2, 2, AX, NV, S), f32),
            pltpu.VMEM((2, 2, AX, NV, S), f32),
            pltpu.VMEM((2, 2, AX, NV, S), f32),
            pltpu.VMEM((2, 2, AX, NV, S), f32),
            pltpu.VMEM((2, 4, AX, NV, S), f32),
            pltpu.VMEM((2, 4, AX, NV, S), f32),
            pltpu.VMEM((NI, NV, SLAB, S), f32),
            pltpu.VMEM((NI, NV, SLAB + 8, S), f32),
            pltpu.VMEM((NI, NV, SLAB + 8, S), f32),
            pltpu.VMEM((2, NV, NI, S), f32),
            pltpu.VMEM((2, NV, NI, S), f32),
            pltpu.SemaphoreType.DMA((5,)),
            pltpu.SemaphoreType.DMA((4,)),
            pltpu.SemaphoreType.DMA((4, 2)),
            pltpu.SemaphoreType.DMA((20,)),
            pltpu.SemaphoreType.DMA((20,)),
        ],
        compiler_params=pltpu.CompilerParams(
            collective_id=0, has_side_effects=True, vmem_limit_bytes=52 * 1024 * 1024
        ),
        cost_estimate=pl.CostEstimate(
            flops=20_000_000, bytes_accessed=3 * PL * T * S * 4, transcendentals=0
        ),
    )(flow_state.reshape(shape), donor_index[0], donor_weight[0], span_count)
    whole = (1, NV, AX, T, S)
    return new_state.reshape(whole), last_update.reshape(whole)


def solution(mesh):
    placed = (
        P("inst", None, None, "dom", None),
        P("inst", None, "dom"),
        P("inst", None, "dom"),
        P("dom"),
    )
    return jax.shard_map(
        functools.partial(local, mesh.shape["dom"]),
        mesh=mesh,
        in_specs=placed,
        out_specs=(P("inst", None, None, "dom", None), P("inst", None, None, "dom", None)),
        check_vma=False,
    )
```

```python
import functools
import math

import jax
import jax.numpy as jnp
import numpy as np
from jax import lax
from jax.experimental import pallas as pl
from jax.experimental.pallas import tpu as pltpu
from jax.sharding import PartitionSpec as P

ITERS = 2
NI = 8
NV = 6
AX = 4
PL = NV * AX
T = 64
S = 128
ZN = 4
SLAB = T // ZN
ORDER = (1, 2, 0, 3)
MESH = pl.DeviceIdType.MESH


def spectral_row():
    k = np.arange(NI)[:, None] - np.arange(NI)[None, :]
    safe = np.where(k == 0, 1.0, np.sin(math.pi * k / NI))
    deriv = np.where(k == 0, 0.0, 0.5 * (-1.0) ** k * np.cos(math.pi * k / NI) / safe)
    return (deriv - 0.1 * deriv @ deriv)[:, 0]


def spectral_apply(x):
    row = spectral_row()
    even = [float(row[j] + row[j + 4]) / 2 for j in range(4)]
    odd = [float(row[j] - row[j + 4]) / 2 for j in range(4)]
    s = [x[z] + x[z + 4] for z in range(4)]
    d = [x[z] - x[z + 4] for z in range(4)]
    q0, q1 = s[0] - s[2], s[1] - s[3]
    s0 = even[0] * q0 + even[3] * q1
    s1 = even[1] * q0 + even[0] * q1
    sym = [s0, s1, -s0, -s1]
    out = [None] * NI
    for z in range(4):
        acc = None
        for y in range(4):
            coef = odd[z - y] if y <= z else -odd[4 + z - y]
            term = coef * d[y]
            acc = term if acc is None else acc + term
        out[z] = sym[z] + acc
        out[z + 4] = sym[z] - acc
    return out


def primitives(u):
    inv = 1.0 / u[0]
    vel = [u[1] * inv, u[2] * inv, u[3] * inv]
    nu = u[5] * inv
    pres = 0.4 * (u[4] - 0.5 * (u[1] * vel[0] + u[2] * vel[1] + u[3] * vel[2]))
    return vel, nu, pres


def centre_terms(u, vel, nu):
    return [
        0.1 * u[0],
        0.1 * u[1] + 0.02 * vel[0],
        0.1 * u[2] + 0.02 * vel[1],
        0.1 * u[3] + 0.02 * vel[2],
        0.1 * u[4],
        0.1 * u[5] + 0.02 * nu,
    ]


def half_flux(u, vel, pres, k):
    h = 0.5 * vel[k]
    f = [0.5 * u[1 + k], u[1] * h, u[2] * h, u[3] * h, (u[4] + pres) * h, u[5] * h]
    f[1 + k] = f[1 + k] + 0.5 * pres
    return f


def next_terms(u, k):
    vel, nu, pres = primitives(u)
    c = centre_terms(u, vel, nu)
    return [f - g for f, g in zip(half_flux(u, vel, pres, k), c)]


def prev_terms(u, k):
    vel, nu, pres = primitives(u)
    c = centre_terms(u, vel, nu)
    return [-(f + g) for f, g in zip(half_flux(u, vel, pres, k), c)]


def kernel(
    n_dom,
    n_cells,
    flow,
    idx,
    wgt,
    count,
    new_state,
    last_update,
    idx_s,
    count_s,
    idx_v,
    wgt_v,
    cur,
    in_u,
    in_n,
    w1,
    w2,
    ss,
    ww,
    n0,
    n1,
    rr,
    a2,
    b2,
    coef,
    win,
    edge,
    halo,
    redge,
    rhalo,
    qedge,
    qhalo,
    wedge,
    whalo,
    slab_n,
    slab_a,
    slab_b,
    slab_out,
    slab_in,
    load_sem,
    p_send,
    p_recv,
    h_send,
    h_recv,
    d_send,
    d_recv,
):
    inst = lax.axis_index("inst")
    dom = lax.axis_index("dom")
    left = lax.rem(dom + n_dom - 1, n_dom)
    right = lax.rem(dom + 1, n_dom)

    def flip(d):
        return d + 2 - 4 * lax.rem(d // 2, 2)

    work = flip(dom)
    body, place = inst // ZN, lax.rem(inst, ZN)
    at_start = jnp.where(place == 0, 1, 0)
    at_end = jnp.where(place == ZN - 1, 1, 0)
    before = flip(lax.rem(work + n_dom - at_start, n_dom))
    beyond = flip(lax.rem(work + at_end, n_dom))
    below = (body * ZN + lax.rem(place + ZN - 1, ZN), before)
    above = (body * ZN + lax.rem(place + 1, ZN), beyond)

    loads = [
        pltpu.make_async_copy(source, target, load_sem.at[n])
        for n, (source, target) in enumerate(
            ((flow, cur), (idx, idx_s), (idx, idx_v), (wgt, wgt_v), (count, count_s))
        )
    ]
    for c in loads:
        c.start()
    barrier = pltpu.get_barrier_semaphore()
    for j in range(NI):
        pl.semaphore_signal(barrier, inc=1, device_id=(j, work), device_id_type=MESH)
    friends = [(inst, left), (inst, right), below, above]
    for side in range(2):
        friends += [(side * ZN + ZN - 1, flip(left)), (side * ZN, flip(right))]
    for device in friends:
        pl.semaphore_signal(barrier, inc=1, device_id=device, device_id_type=MESH)

    def remote(source, target, send, recv, device):
        return pltpu.make_async_remote_copy(
            src_ref=source,
            dst_ref=target,
            send_sem=send,
            recv_sem=recv,
            device_id=device,
            device_id_type=MESH,
        )

    def piece(unit, partner, part, slot):
        side, slab = partner // ZN, lax.rem(partner, ZN)
        row = 1 + side if part == 0 else (AX - 1) * side
        mine = pl.ds(pl.multiple_of(SLAB * slab, SLAB), SLAB)
        spot = 2 * part + slot // ZN
        at = SLAB * lax.rem(slot, ZN)
        if unit == 0:
            source, target = flow.at[:, row, mine], in_u.at[part, slot]
        elif unit == 1:
            source = w1.at[part, partner]
            target = ss.at[spot, :, pl.ds(pl.multiple_of(at, SLAB), SLAB)]
        elif unit == 2:
            source, target = n0.at[:, row, mine], in_n.at[slot]
        else:
            source = w2.at[part, partner]
            target = ww.at[spot, :, pl.ds(pl.multiple_of(at + 8, 8), SLAB)]
        return remote(source, target, p_send.at[unit], p_recv.at[unit, part], (partner, work))

    order = [lax.rem(inst + n, NI) for n in range(NI)]

    def send(unit, part):
        for j in order:
            piece(unit, j, part, inst).start()

    def arrive(unit, part):
        spots = pl.ds(2 * part, 2)
        ref = (in_u.at[part], ss.at[spots], in_n, ww.at[spots, :, pl.ds(8, T)])[unit]
        pltpu.make_async_copy(ref, ref, p_recv.at[unit, part]).wait()

    def gone(unit):
        ref = (flow, w1, n0.at[:, 1:3], w2)[unit]
        pltpu.make_async_copy(ref, ref, p_send.at[unit]).wait()

    end_row = (SLAB - 4) * at_end

    def send_ends(part):
        def instance(m):
            for v in range(NV):
                wedge[part, m, v] = w2[part, m, v, pl.ds(end_row, 4), :]

        over(NI, instance)
        for at_edge, side, block in ((at_start, 1, before), (at_end, 0, beyond)):

            @pl.when(at_edge == 1)
            def _(side=side, block=block):
                for m in order:
                    remote(
                        wedge.at[part, m],
                        whalo.at[side, 2 * part + body],
                        h_send.at[part],
                        h_recv.at[part, side],
                        (m, flip(block)),
                    ).start()

    def ends_came(part):
        for side in range(2):
            ref = whalo.at[side, pl.ds(2 * part, 2)]
            pltpu.make_async_copy(ref, ref, h_recv.at[part, side]).wait()

    def ends_gone():
        @pl.when(at_start + at_end == 1)
        def _():
            for part in range(2):
                ref = wedge.at[part]
                pltpu.make_async_copy(ref, ref, h_send.at[part]).wait()

    def near(slot, source, target, device):
        return remote(source, target, d_send.at[slot], d_recv.at[slot], (inst, device))

    def both(slot, out, back):
        return [near(slot, out(0), back(1), left), near(slot + 1, out(1), back(0), right)]

    def start(copies):
        for c in copies:
            c.start()
        return copies

    def over(n, body):
        def step(i, _):
            body(i)
            return 0

        lax.fori_loop(0, n, step, 0)

    lane = lax.broadcasted_iota(jnp.int32, (8, S), 1)
    first_lane = lane == 0
    last_lane = lane == S - 1

    def spanwise(f, c):
        out = []
        for g, h in zip(f, c):
            up, down = g - h, g + h
            after = jnp.where(last_lane, up, pltpu.roll(up, S - 1, 1))
            prior = jnp.where(first_lane, down, pltpu.roll(down, 1, 1))
            out.append(6.0 * h + (after - prior))
        return out

    def spectral(part, target, plus=None):
        def variable(v):
            for t0 in range(0, SLAB, 8):
                rows = slice(t0, t0 + 8)
                if plus is None:
                    x = [in_u[part, m, v, rows, :] for m in range(NI)]
                else:
                    x = [w1[part, m, v, rows, :] + plus(m, v, t0) for m in range(NI)]
                for m, g in enumerate(spectral_apply(x)):
                    target[part, m, v, rows, :] = g

        over(NV, variable)

    def inside(out, first_tile, last_tile):
        def tile(i, _):
            t0 = pl.multiple_of(8 * i, 8)
            total = []
            first = []
            second = []
            for a in range(AX):
                u = [cur[v, a, pl.ds(t0, 8), :] for v in range(NV)]
                vel, nu, pres = primitives(u)
                c = centre_terms(u, vel, nu)
                f1 = half_flux(u, vel, pres, 0)
                first.append([f - g for f, g in zip(f1, c)])
                second.append([f + g for f, g in zip(f1, c)])
                f2 = half_flux(u, vel, pres, 1)
                for v in range(NV):
                    a2[v, a, pl.ds(t0 + 8, 8), :] = f2[v] - c[v]
                    b2[v, a, pl.ds(t0 + 8, 8), :] = f2[v] + c[v]
                total.append(spanwise(half_flux(u, vel, pres, 2), c))
            for a in range(AX):
                for v in range(NV):
                    r = total[a][v]
                    if a == AX - 1:
                        r = r + first[a][v]
                    elif a != AX // 2 - 1:
                        r = r + first[a + 1][v]
                    if a == 0:
                        r = r - second[a][v]
                    elif a != AX // 2:
                        r = r - second[a - 1][v]
                    out[v, a, pl.ds(t0, 8), :] = r
            return 0

        lax.fori_loop(first_tile, last_tile, tile, 0)

    def around(out, it, layers, windows):
        for c in layers:
            c.wait_recv()
        low = prev_terms([halo[it, 0, v] for v in range(NV)], 1)
        high = next_terms([halo[it, 1, v] for v in range(NV)], 1)
        for v in range(NV):
            for a in range(AX):
                b2[v, a, 7:8, :] = -low[v][a : a + 1]
                a2[v, a, T + 8 : T + 9, :] = high[v][a : a + 1]

        def variable(v):
            for a in range(AX):
                out[v, a] += a2[v, a, 9 : T + 9] - b2[v, a, 7 : T + 7]

        over(NV, variable)
        for c in windows:
            c.wait_recv()

        def ghosts(i):
            t0 = pl.multiple_of(8 * i, 8)
            for side in range(2):
                taps = [coef[side, n, pl.ds(t0, 8), :] for n in range(3)]
                u = []
                for v in range(NV):
                    g = taps[0] * win[it, side, v, pl.ds(base[side] + t0, 8), :]
                    g = g + taps[1] * win[it, side, v, pl.ds(base[side] + t0 + 1, 8), :]
                    g = g + taps[2] * win[it, side, v, pl.ds(base[side] + t0 + 2, 8), :]
                    u.append(g)
                terms = next_terms(u, 0) if side == 0 else prev_terms(u, 0)
                for v in range(NV):
                    out[v, 1 + side, pl.ds(t0, 8), :] += terms[v]

        over(T // 8, ghosts)

    def outer_layers(it):
        for side, t in enumerate((0, T - 1)):
            for v in range(NV):
                edge[it, side, v] = cur[v, :, t, :]
            edge[it, side, NV] = jnp.broadcast_to(active, (AX, S))
        return start(
            both(10 * it, lambda side: edge.at[it, side], lambda side: halo.at[it, side])
        )

    def interface_rows(it):
        for v in range(NV):
            win[it, 0, v, 0:T] = cur[v, 2]
            win[it, 1, v, T : 2 * T] = cur[v, 1]
        return start(
            [
                near(10 * it + 2, win.at[it, 0, :, 0:T], win.at[it, 0, :, T : 2 * T], left),
                near(10 * it + 3, win.at[it, 1, :, T : 2 * T], win.at[it, 1, :, 0:T], right),
            ]
        )

    def rim_of(slot, out, back, spots):
        return start(
            both(slot, lambda side: out.at[side, :, spots], lambda side: back.at[side, :, spots])
        )

    FRONT, REST = pl.ds(0, 2), pl.ds(2, 2)

    pl.semaphore_wait(barrier, NI + 4 + NI * (at_start + at_end))
    for part in range(2):
        send(0, part)
    for c in loads:
        c.wait()
    active = jnp.where(lax.broadcasted_iota(jnp.int32, (1, S), 1) < count_s[0], 1.0, 0.0)
    layers = outer_layers(0)
    windows = interface_rows(0)

    def least(t, low):
        cell = dom * T + t
        gaps = (idx_s[0, t] - cell, cell - 1 - idx_s[1, t])
        gaps = [jnp.where(g < 0, g + n_cells, g) for g in gaps]
        return jnp.minimum(low[0], gaps[0]), jnp.minimum(low[1], gaps[1])

    most = (jnp.int32(n_cells), jnp.int32(n_cells))
    offset = [jnp.clip(x, 0, T - 2) for x in lax.fori_loop(0, T, least, most)]
    base = [offset[0], T - 2 - offset[1]]
    eye = lax.broadcasted_iota(jnp.int32, (T, T), 0) == lax.broadcasted_iota(
        jnp.int32, (T, T), 1
    )
    for side in range(2):
        cell = dom * T + lax.broadcasted_iota(jnp.int32, (1, T), 1)
        row = idx_v[side : side + 1, :]
        gap = row - cell if side == 0 else cell - 1 - row
        gap = jnp.where(gap < 0, gap + n_cells, gap)
        step = jnp.where(gap > offset[side], 1.0, 0.0)
        w = wgt_v[side : side + 1, :]
        taps = [(1.0 - step) * w, step * w + (1.0 - step) * (1.0 - w), step * (1.0 - w)]
        if side == 1:
            taps = [step * w, (1.0 - step) * w + step * (1.0 - w), (1.0 - step) * (1.0 - w)]
        for i, tap in enumerate(taps):
            column = jnp.sum(jnp.where(eye, tap, 0.0), axis=1, keepdims=True)
            coef[side, i] = jnp.broadcast_to(column, (T, S))

    half = T // 16
    inside(n0, 0, half)
    arrive(0, 0)
    spectral(0, w1)
    send(1, 0)
    arrive(0, 1)
    for v in range(NV):
        slab_out[0, v] = in_u[1, :, v, 0, :]
        slab_out[1, v] = in_u[1, :, v, SLAB - 1, :]
    slabs = start(
        [
            remote(slab_out.at[0], slab_in.at[1], d_send.at[18], d_recv.at[18], below),
            remote(slab_out.at[1], slab_in.at[0], d_send.at[19], d_recv.at[19], above),
        ]
    )
    spectral(1, w1)
    send(1, 1)
    inside(n0, half, 2 * half)
    around(n0, 0, layers, windows)
    send(2, 0)

    toward = jnp.where(body == 0, 1.0, -1.0)

    def slab_inside(m):
        for t0 in range(0, SLAB, 8):
            rows = slice(t0, t0 + 8)
            u = [in_u[0, m, v, rows, :] for v in range(NV)]
            vel, nu, pres = primitives(u)
            c1 = centre_terms(u, vel, nu)
            f1 = half_flux(u, vel, pres, 0)
            u = [in_u[1, m, v, rows, :] for v in range(NV)]
            vel, nu, pres = primitives(u)
            c = centre_terms(u, vel, nu)
            f = half_flux(u, vel, pres, 0)
            f2 = half_flux(u, vel, pres, 1)
            r = spanwise(half_flux(u, vel, pres, 2), c)
            for v in range(NV):
                slab_a[m, v, t0 : t0 + 8, :] = f2[v] - c[v]
                slab_b[m, v, t0 + 8 : t0 + 16, :] = f2[v] + c[v]
                slab_n[m, v, rows, :] = r[v] + (toward * (f1[v] - f[v]) - (c1[v] + c[v]))

    over(NI, slab_inside)
    for c in slabs:
        c.wait()
    low = prev_terms([slab_in[0, v] for v in range(NV)], 1)
    high = next_terms([slab_in[1, v] for v in range(NV)], 1)
    for v in range(NV):
        slab_b[:, v, 7, :] = -low[v]
        slab_a[:, v, SLAB, :] = high[v]

    def outer(m, v, t0):
        return slab_n[m, v, t0 : t0 + 8, :] + (
            slab_a[m, v, t0 + 1 : t0 + 9, :] - slab_b[m, v, t0 + 7 : t0 + 15, :]
        )

    spectral(1, w2, outer)
    send_ends(1)
    send(3, 1)

    def keep_rows(out, spots, times, value):
        for spot in spots:
            for n, t in enumerate(times):
                out[n // (len(times) // 2), n % (len(times) // 2), spot] = value(spot, t)

    def put_rows(back, spots, times):
        for spot in spots:
            for n, t in enumerate(times):
                rr[spot, :, 8 + t, :] = back[n // 2, n % 2, spot]

    ends = (0, 1, T - 2, T - 1)
    outside = (-2, -1, T, T + 1)

    def smoothed(ref, spot, v):
        return (
            0.625 * ref[spot, v, 8 : T + 8]
            + 0.125 * (ref[spot, v, 7 : T + 7] + ref[spot, v, 9 : T + 9])
            + 0.0625 * (ref[spot, v, 6 : T + 6] + ref[spot, v, 10 : T + 10])
        )

    def sums(spots):
        def variable(v):
            for spot in spots:
                rr[spot, v, 8 : T + 8] = n0[v, ORDER[spot]] + ss[spot, v]

        over(NV, variable)

    def first_update(spots):
        def variable(v):
            for spot in spots:
                a = ORDER[spot]
                cur[v, a] = cur[v, a] - 0.05 * (smoothed(rr, spot, v) * active)

        over(NV, variable)

    def first_sum(spot, t):
        return n0[:, ORDER[spot], t, :] + ss[spot, :, t, :]

    arrive(1, 0)
    keep_rows(redge, (0, 1), ends, first_sum)
    rim = rim_of(4, redge, rhalo, FRONT)
    sums((0, 1))
    arrive(1, 1)
    keep_rows(redge, (2, 3), ends, first_sum)
    rim2 = rim_of(6, redge, rhalo, REST)
    for c in rim:
        c.wait()
    put_rows(rhalo, (0, 1), outside)
    gone(0)
    for c in layers + windows:
        c.wait_send()
    first_update((0, 1))
    windows = interface_rows(1)
    sums((2, 3))
    for c in rim2:
        c.wait()
    put_rows(rhalo, (2, 3), outside)
    first_update((2, 3))
    layers = outer_layers(1)

    arrive(2, 0)
    spectral(0, w2, lambda m, v, t0: in_n[m, v, t0 : t0 + 8, :])
    send_ends(0)
    send(3, 0)
    inside(n1, 0, 2 * half)
    around(n1, 1, layers, windows)
    keep_rows(qedge, range(4), ends, lambda spot, t: n1[:, ORDER[spot], t, :] + ss[spot, :, t, :])
    rim = start(both(8, lambda side: qedge.at[side], lambda side: qhalo.at[side]))

    for c in rim:
        c.wait()

    def second_update(spots):
        for spot in spots:
            for n in range(2):
                ww[spot, :, 6 + n, :] = whalo[0, spot, :, 2 + n, :]
                ww[spot, :, T + 8 + n, :] = whalo[1, spot, :, n, :]
            for side in range(2):
                h = [whalo[side, spot, :, n, :] for n in range(4)]
                e = [ww[spot, :, 8 + t, :] for t in ((0, 1), (T - 2, T - 1))[side]]
                line = h + e if side == 0 else e + h
                mask = halo[0, side, NV, 0:1, :]
                for n in range(2):
                    x = line[n : n + 5]
                    z = 0.625 * x[2] + 0.125 * (x[1] + x[3]) + 0.0625 * (x[0] + x[4])
                    t = n - 2 if side == 0 else T + n
                    rr[spot, :, 8 + t, :] = qhalo[side, n, spot] - 0.05 * (z * mask)

        def variable(v):
            for spot in spots:
                a = ORDER[spot]
                rr[spot, v, 8 : T + 8] = (
                    n1[v, a] + ss[spot, v] - 0.05 * (smoothed(ww, spot, v) * active)
                )
                update = smoothed(rr, spot, v) * active
                last_update[v, a] = update
                new_state[v, a] = cur[v, a] - 0.05 * update

        over(NV, variable)

    for part in (1, 0):
        arrive(3, part)
        ends_came(part)
        second_update((2 * part, 2 * part + 1))

    for c in layers + windows:
        c.wait_send()
    for unit in (1, 2, 3):
        gone(unit)
    ends_gone()


def local(n_dom, flow_state, donor_index, donor_weight, span_count):
    shape = (NV, AX, T, S)
    padded = (NV, AX, T + 16, S)
    pieces = (2, NI, NV, SLAB, S)
    turned = (AX, NV, T + 16, S)
    f32 = jnp.float32
    anywhere = pl.BlockSpec(memory_space=pl.ANY)
    vmem = pl.BlockSpec(memory_space=pltpu.VMEM)
    new_state, last_update = pl.pallas_call(
        functools.partial(kernel, n_dom, n_dom * T),
        out_shape=[jax.ShapeDtypeStruct(shape, f32)] * 2,
        in_specs=[anywhere] * 4,
        out_specs=[vmem, vmem],
        scratch_shapes=[
            pltpu.SMEM((2, T), jnp.int32),
            pltpu.SMEM((1,), jnp.int32),
            pltpu.VMEM((2, T), jnp.int32),
            pltpu.VMEM((2, T), f32),
            pltpu.VMEM(shape, f32),
            pltpu.VMEM(pieces, f32),
            pltpu.VMEM((NI, NV, SLAB, S), f32),
            pltpu.VMEM(pieces, f32),
            pltpu.VMEM(pieces, f32),
            pltpu.VMEM((AX, NV, T, S), f32),
            pltpu.VMEM(turned, f32),
            pltpu.VMEM(shape, f32),
            pltpu.VMEM(shape, f32),
            pltpu.VMEM(turned, f32),
            pltpu.VMEM(padded, f32),
            pltpu.VMEM(padded, f32),
            pltpu.VMEM((2, 3, T, S), f32),
            pltpu.VMEM((ITERS, 2, NV, 2 * T, S), f32),
            pltpu.VMEM((ITERS, 2, NV + 1, AX, S), f32),
            pltpu.VMEM((ITERS, 2, NV + 1, AX, S), f32),
            pltpu.VMEM((2, 2, AX, NV, S), f32),
            pltpu.VMEM((2, 2, AX, NV, S), f32),
            pltpu.VMEM((2, 2, AX, NV, S), f32),
            pltpu.VMEM((2, 2, AX, NV, S), f32),
            pltpu.VMEM((2, NI, NV, 4, S), f32),
            pltpu.VMEM((2, AX, NV, 4, S), f32),
            pltpu.VMEM((NI, NV, SLAB, S), f32),
            pltpu.VMEM((NI, NV, SLAB + 8, S), f32),
            pltpu.VMEM((NI, NV, SLAB + 8, S), f32),
            pltpu.VMEM((2, NV, NI, S), f32),
            pltpu.VMEM((2, NV, NI, S), f32),
            pltpu.SemaphoreType.DMA((5,)),
            pltpu.SemaphoreType.DMA((4,)),
            pltpu.SemaphoreType.DMA((4, 2)),
            pltpu.SemaphoreType.DMA((2,)),
            pltpu.SemaphoreType.DMA((2, 2)),
            pltpu.SemaphoreType.DMA((20,)),
            pltpu.SemaphoreType.DMA((20,)),
        ],
        compiler_params=pltpu.CompilerParams(
            collective_id=0, has_side_effects=True, vmem_limit_bytes=52 * 1024 * 1024
        ),
        cost_estimate=pl.CostEstimate(
            flops=20_000_000, bytes_accessed=3 * PL * T * S * 4, transcendentals=0
        ),
    )(flow_state.reshape(shape), donor_index[0], donor_weight[0], span_count)
    whole = (1, NV, AX, T, S)
    return new_state.reshape(whole), last_update.reshape(whole)


def solution(mesh):
    placed = (
        P("inst", None, None, "dom", None),
        P("inst", None, "dom"),
        P("inst", None, "dom"),
        P("dom"),
    )
    return jax.shard_map(
        functools.partial(local, mesh.shape["dom"]),
        mesh=mesh,
        in_specs=placed,
        out_specs=(P("inst", None, None, "dom", None), P("inst", None, None, "dom", None)),
        check_vma=False,
    )
```

```python
import functools
import math

import jax
import jax.numpy as jnp
import numpy as np
from jax import lax
from jax.experimental import pallas as pl
from jax.experimental.pallas import tpu as pltpu
from jax.sharding import PartitionSpec as P

ITERS = 2
NI = 8
NV = 6
AX = 4
PL = NV * AX
T = 64
S = 128
ZN = 4
SLAB = T // ZN
ORDER = (1, 2, 0, 3)
MESH = pl.DeviceIdType.MESH


def spectral_row():
    k = np.arange(NI)[:, None] - np.arange(NI)[None, :]
    safe = np.where(k == 0, 1.0, np.sin(math.pi * k / NI))
    deriv = np.where(k == 0, 0.0, 0.5 * (-1.0) ** k * np.cos(math.pi * k / NI) / safe)
    return (deriv - 0.1 * deriv @ deriv)[:, 0]


def spectral_apply(x):
    row = spectral_row()
    even = [float(row[j] + row[j + 4]) / 2 for j in range(4)]
    odd = [float(row[j] - row[j + 4]) / 2 for j in range(4)]
    s = [x[z] + x[z + 4] for z in range(4)]
    d = [x[z] - x[z + 4] for z in range(4)]
    q0, q1 = s[0] - s[2], s[1] - s[3]
    s0 = even[0] * q0 + even[3] * q1
    s1 = even[1] * q0 + even[0] * q1
    sym = [s0, s1, -s0, -s1]
    out = [None] * NI
    for z in range(4):
        acc = None
        for y in range(4):
            coef = odd[z - y] if y <= z else -odd[4 + z - y]
            term = coef * d[y]
            acc = term if acc is None else acc + term
        out[z] = sym[z] + acc
        out[z + 4] = sym[z] - acc
    return out


def primitives(u):
    inv = 1.0 / u[0]
    vel = [u[1] * inv, u[2] * inv, u[3] * inv]
    nu = u[5] * inv
    pres = 0.4 * (u[4] - 0.5 * (u[1] * vel[0] + u[2] * vel[1] + u[3] * vel[2]))
    return vel, nu, pres


def centre_terms(u, vel, nu):
    return [
        0.1 * u[0],
        0.1 * u[1] + 0.02 * vel[0],
        0.1 * u[2] + 0.02 * vel[1],
        0.1 * u[3] + 0.02 * vel[2],
        0.1 * u[4],
        0.1 * u[5] + 0.02 * nu,
    ]


def half_flux(u, vel, pres, k):
    h = 0.5 * vel[k]
    f = [0.5 * u[1 + k], u[1] * h, u[2] * h, u[3] * h, (u[4] + pres) * h, u[5] * h]
    f[1 + k] = f[1 + k] + 0.5 * pres
    return f


def next_terms(u, k):
    vel, nu, pres = primitives(u)
    c = centre_terms(u, vel, nu)
    return [f - g for f, g in zip(half_flux(u, vel, pres, k), c)]


def prev_terms(u, k):
    vel, nu, pres = primitives(u)
    c = centre_terms(u, vel, nu)
    return [-(f + g) for f, g in zip(half_flux(u, vel, pres, k), c)]


def kernel(
    n_dom,
    n_cells,
    flow,
    idx,
    wgt,
    count,
    new_state,
    last_update,
    idx_s,
    count_s,
    idx_v,
    wgt_v,
    cur,
    in_u,
    in_n,
    w1,
    w2,
    ss,
    ww,
    n0,
    n1,
    rr,
    a2,
    b2,
    coef,
    win,
    edge,
    halo,
    redge,
    rhalo,
    qedge,
    qhalo,
    wedge,
    whalo,
    slab_n,
    slab_a,
    slab_b,
    slab_out,
    slab_in,
    load_sem,
    p_send,
    p_recv,
    d_send,
    d_recv,
):
    inst = lax.axis_index("inst")
    dom = lax.axis_index("dom")
    left = lax.rem(dom + n_dom - 1, n_dom)
    right = lax.rem(dom + 1, n_dom)

    def flip(d):
        return d + 2 - 4 * lax.rem(d // 2, 2)

    work = flip(dom)
    body, place = inst // ZN, lax.rem(inst, ZN)
    at_start = jnp.where(place == 0, 1, 0)
    at_end = jnp.where(place == ZN - 1, 1, 0)
    before = flip(lax.rem(work + n_dom - at_start, n_dom))
    beyond = flip(lax.rem(work + at_end, n_dom))
    below = (body * ZN + lax.rem(place + ZN - 1, ZN), before)
    above = (body * ZN + lax.rem(place + 1, ZN), beyond)

    loads = [
        pltpu.make_async_copy(source, target, load_sem.at[n])
        for n, (source, target) in enumerate(
            ((flow, cur), (idx, idx_s), (idx, idx_v), (wgt, wgt_v), (count, count_s))
        )
    ]
    for c in loads:
        c.start()
    barrier = pltpu.get_barrier_semaphore()
    for j in range(NI):
        pl.semaphore_signal(barrier, inc=1, device_id=(j, work), device_id_type=MESH)
    for device in ((inst, left), (inst, right), below, above):
        pl.semaphore_signal(barrier, inc=1, device_id=device, device_id_type=MESH)

    def remote(source, target, send, recv, device):
        return pltpu.make_async_remote_copy(
            src_ref=source,
            dst_ref=target,
            send_sem=send,
            recv_sem=recv,
            device_id=device,
            device_id_type=MESH,
        )

    def piece(unit, partner, part, slot):
        side, slab = partner // ZN, lax.rem(partner, ZN)
        row = 1 + side if part == 0 else (AX - 1) * side
        mine = pl.ds(pl.multiple_of(SLAB * slab, SLAB), SLAB)
        spot = 2 * part + slot // ZN
        at = SLAB * lax.rem(slot, ZN)
        if unit == 0:
            source, target = flow.at[:, row, mine], in_u.at[part, slot]
        elif unit == 1:
            source = w1.at[part, partner]
            target = ss.at[spot, :, pl.ds(pl.multiple_of(at, SLAB), SLAB)]
        elif unit == 2:
            source, target = n0.at[:, row, mine], in_n.at[slot]
        else:
            source = w2.at[part, partner]
            target = ww.at[spot, :, pl.ds(pl.multiple_of(at + 8, 8), SLAB)]
        return remote(source, target, p_send.at[unit], p_recv.at[unit, part], (partner, work))

    order = [lax.rem(inst + n, NI) for n in range(NI)]

    def send(unit, part):
        for j in order:
            piece(unit, j, part, inst).start()

    def arrive(unit, part):
        spots = pl.ds(2 * part, 2)
        ref = (in_u.at[part], ss.at[spots], in_n, ww.at[spots, :, pl.ds(8, T)])[unit]
        pltpu.make_async_copy(ref, ref, p_recv.at[unit, part]).wait()

    def gone(unit):
        ref = (flow, w1, n0.at[:, 1:3], w2)[unit]
        pltpu.make_async_copy(ref, ref, p_send.at[unit]).wait()

    def near(slot, source, target, device):
        return remote(source, target, d_send.at[slot], d_recv.at[slot], (inst, device))

    def both(slot, out, back):
        return [near(slot, out(0), back(1), left), near(slot + 1, out(1), back(0), right)]

    def start(copies):
        for c in copies:
            c.start()
        return copies

    def over(n, body):
        def step(i, _):
            body(i)
            return 0

        lax.fori_loop(0, n, step, 0)

    lane = lax.broadcasted_iota(jnp.int32, (8, S), 1)
    first_lane = lane == 0
    last_lane = lane == S - 1

    def spanwise(f, c):
        out = []
        for g, h in zip(f, c):
            up, down = g - h, g + h
            after = jnp.where(last_lane, up, pltpu.roll(up, S - 1, 1))
            prior = jnp.where(first_lane, down, pltpu.roll(down, 1, 1))
            out.append(6.0 * h + (after - prior))
        return out

    def spectral(part, target, plus=None):
        def variable(v):
            for t0 in range(0, SLAB, 8):
                rows = slice(t0, t0 + 8)
                if plus is None:
                    x = [in_u[part, m, v, rows, :] for m in range(NI)]
                else:
                    x = [w1[part, m, v, rows, :] + plus(m, v, t0) for m in range(NI)]
                for m, g in enumerate(spectral_apply(x)):
                    target[part, m, v, rows, :] = g

        over(NV, variable)

    def inside(out, first_tile, last_tile):
        def tile(i, _):
            t0 = pl.multiple_of(8 * i, 8)
            total = []
            first = []
            second = []
            for a in range(AX):
                u = [cur[v, a, pl.ds(t0, 8), :] for v in range(NV)]
                vel, nu, pres = primitives(u)
                c = centre_terms(u, vel, nu)
                f1 = half_flux(u, vel, pres, 0)
                first.append([f - g for f, g in zip(f1, c)])
                second.append([f + g for f, g in zip(f1, c)])
                f2 = half_flux(u, vel, pres, 1)
                for v in range(NV):
                    a2[v, a, pl.ds(t0 + 8, 8), :] = f2[v] - c[v]
                    b2[v, a, pl.ds(t0 + 8, 8), :] = f2[v] + c[v]
                total.append(spanwise(half_flux(u, vel, pres, 2), c))
            for a in range(AX):
                for v in range(NV):
                    r = total[a][v]
                    if a == AX - 1:
                        r = r + first[a][v]
                    elif a != AX // 2 - 1:
                        r = r + first[a + 1][v]
                    if a == 0:
                        r = r - second[a][v]
                    elif a != AX // 2:
                        r = r - second[a - 1][v]
                    out[v, a, pl.ds(t0, 8), :] = r
            return 0

        lax.fori_loop(first_tile, last_tile, tile, 0)

    def around(out, it, layers):
        for c in layers:
            c.wait_recv()
        low = prev_terms([halo[it, 0, v] for v in range(NV)], 1)
        high = next_terms([halo[it, 1, v] for v in range(NV)], 1)
        for v in range(NV):
            for a in range(AX):
                b2[v, a, 7:8, :] = -low[v][a : a + 1]
                a2[v, a, T + 8 : T + 9, :] = high[v][a : a + 1]

        def variable(v):
            for a in range(AX):
                out[v, a] += a2[v, a, 9 : T + 9] - b2[v, a, 7 : T + 7]

        over(NV, variable)

    def interface(out, it, windows):
        for c in windows:
            c.wait_recv()

        def ghosts(i):
            t0 = pl.multiple_of(8 * i, 8)
            for side in range(2):
                taps = [coef[side, n, pl.ds(t0, 8), :] for n in range(3)]
                u = []
                for v in range(NV):
                    g = taps[0] * win[it, side, v, pl.ds(base[side] + t0, 8), :]
                    g = g + taps[1] * win[it, side, v, pl.ds(base[side] + t0 + 1, 8), :]
                    g = g + taps[2] * win[it, side, v, pl.ds(base[side] + t0 + 2, 8), :]
                    u.append(g)
                terms = next_terms(u, 0) if side == 0 else prev_terms(u, 0)
                for v in range(NV):
                    out[v, 1 + side, pl.ds(t0, 8), :] += terms[v]

        over(T // 8, ghosts)

    def outer_layers(it):
        for side, t in enumerate((0, T - 1)):
            for v in range(NV):
                edge[it, side, v] = cur[v, :, t, :]
            edge[it, side, NV] = jnp.broadcast_to(active, (AX, S))
        return start(
            both(10 * it, lambda side: edge.at[it, side], lambda side: halo.at[it, side])
        )

    def interface_rows(it):
        for v in range(NV):
            win[it, 0, v, 0:T] = cur[v, 2]
            win[it, 1, v, T : 2 * T] = cur[v, 1]
        return start(
            [
                near(10 * it + 2, win.at[it, 0, :, 0:T], win.at[it, 0, :, T : 2 * T], left),
                near(10 * it + 3, win.at[it, 1, :, T : 2 * T], win.at[it, 1, :, 0:T], right),
            ]
        )

    def rim_of(slot, out, back, spots):
        return start(
            both(slot, lambda side: out.at[side, :, spots], lambda side: back.at[side, :, spots])
        )

    FRONT, REST = pl.ds(0, 2), pl.ds(2, 2)

    pl.semaphore_wait(barrier, NI + 4)
    for part in range(2):
        send(0, part)
    for c in loads:
        c.wait()
    active = jnp.where(lax.broadcasted_iota(jnp.int32, (1, S), 1) < count_s[0], 1.0, 0.0)
    layers = outer_layers(0)
    windows = interface_rows(0)

    def least(t, low):
        cell = dom * T + t
        gaps = (idx_s[0, t] - cell, cell - 1 - idx_s[1, t])
        gaps = [jnp.where(g < 0, g + n_cells, g) for g in gaps]
        return jnp.minimum(low[0], gaps[0]), jnp.minimum(low[1], gaps[1])

    most = (jnp.int32(n_cells), jnp.int32(n_cells))
    offset = [jnp.clip(x, 0, T - 2) for x in lax.fori_loop(0, T, least, most)]
    base = [offset[0], T - 2 - offset[1]]
    eye = lax.broadcasted_iota(jnp.int32, (T, T), 0) == lax.broadcasted_iota(
        jnp.int32, (T, T), 1
    )
    for side in range(2):
        cell = dom * T + lax.broadcasted_iota(jnp.int32, (1, T), 1)
        row = idx_v[side : side + 1, :]
        gap = row - cell if side == 0 else cell - 1 - row
        gap = jnp.where(gap < 0, gap + n_cells, gap)
        step = jnp.where(gap > offset[side], 1.0, 0.0)
        w = wgt_v[side : side + 1, :]
        taps = [(1.0 - step) * w, step * w + (1.0 - step) * (1.0 - w), step * (1.0 - w)]
        if side == 1:
            taps = [step * w, (1.0 - step) * w + step * (1.0 - w), (1.0 - step) * (1.0 - w)]
        for i, tap in enumerate(taps):
            column = jnp.sum(jnp.where(eye, tap, 0.0), axis=1, keepdims=True)
            coef[side, i] = jnp.broadcast_to(column, (T, S))

    half = T // 16
    inside(n0, 0, half)
    arrive(0, 0)
    spectral(0, w1)
    send(1, 0)
    arrive(0, 1)
    for v in range(NV):
        slab_out[0, v] = in_u[1, :, v, 0, :]
        slab_out[1, v] = in_u[1, :, v, SLAB - 1, :]
    slabs = start(
        [
            remote(slab_out.at[0], slab_in.at[1], d_send.at[18], d_recv.at[18], below),
            remote(slab_out.at[1], slab_in.at[0], d_send.at[19], d_recv.at[19], above),
        ]
    )
    spectral(1, w1)
    send(1, 1)
    inside(n0, half, 2 * half)
    around(n0, 0, layers)
    interface(n0, 0, windows)
    send(2, 0)

    toward = jnp.where(body == 0, 1.0, -1.0)

    def slab_inside(m):
        for t0 in range(0, SLAB, 8):
            rows = slice(t0, t0 + 8)
            u = [in_u[0, m, v, rows, :] for v in range(NV)]
            vel, nu, pres = primitives(u)
            c1 = centre_terms(u, vel, nu)
            f1 = half_flux(u, vel, pres, 0)
            u = [in_u[1, m, v, rows, :] for v in range(NV)]
            vel, nu, pres = primitives(u)
            c = centre_terms(u, vel, nu)
            f = half_flux(u, vel, pres, 0)
            f2 = half_flux(u, vel, pres, 1)
            r = spanwise(half_flux(u, vel, pres, 2), c)
            for v in range(NV):
                slab_a[m, v, t0 : t0 + 8, :] = f2[v] - c[v]
                slab_b[m, v, t0 + 8 : t0 + 16, :] = f2[v] + c[v]
                slab_n[m, v, rows, :] = r[v] + (toward * (f1[v] - f[v]) - (c1[v] + c[v]))

    over(NI, slab_inside)
    for c in slabs:
        c.wait()
    low = prev_terms([slab_in[0, v] for v in range(NV)], 1)
    high = next_terms([slab_in[1, v] for v in range(NV)], 1)
    for v in range(NV):
        slab_b[:, v, 7, :] = -low[v]
        slab_a[:, v, SLAB, :] = high[v]

    def outer(m, v, t0):
        return slab_n[m, v, t0 : t0 + 8, :] + (
            slab_a[m, v, t0 + 1 : t0 + 9, :] - slab_b[m, v, t0 + 7 : t0 + 15, :]
        )

    spectral(1, w2, outer)

    def keep_rows(out, spots, times, value):
        for spot in spots:
            for n, t in enumerate(times):
                out[n // (len(times) // 2), n % (len(times) // 2), spot] = value(spot, t)

    def put_rows(back, spots, times):
        for spot in spots:
            for n, t in enumerate(times):
                rr[spot, :, 8 + t, :] = back[n // 2, n % 2, spot]

    ends = (0, 1, T - 2, T - 1)
    outside = (-2, -1, T, T + 1)

    def smoothed(ref, spot, v):
        return (
            0.625 * ref[spot, v, 8 : T + 8]
            + 0.125 * (ref[spot, v, 7 : T + 7] + ref[spot, v, 9 : T + 9])
            + 0.0625 * (ref[spot, v, 6 : T + 6] + ref[spot, v, 10 : T + 10])
        )

    def sums(spots):
        def variable(v):
            for spot in spots:
                rr[spot, v, 8 : T + 8] = n0[v, ORDER[spot]] + ss[spot, v]

        over(NV, variable)

    def first_update(spots):
        def variable(v):
            for spot in spots:
                a = ORDER[spot]
                cur[v, a] = cur[v, a] - 0.05 * (smoothed(rr, spot, v) * active)

        over(NV, variable)

    def first_sum(spot, t):
        return n0[:, ORDER[spot], t, :] + ss[spot, :, t, :]

    arrive(1, 0)
    keep_rows(redge, (0, 1), ends, first_sum)
    rim = rim_of(4, redge, rhalo, FRONT)
    sums((0, 1))
    arrive(1, 1)
    keep_rows(redge, (2, 3), ends, first_sum)
    rim2 = rim_of(6, redge, rhalo, REST)
    for c in rim:
        c.wait()
    put_rows(rhalo, (0, 1), outside)
    gone(0)
    for c in layers + windows:
        c.wait_send()
    first_update((0, 1))
    windows = interface_rows(1)
    send(3, 1)
    sums((2, 3))
    for c in rim2:
        c.wait()
    put_rows(rhalo, (2, 3), outside)
    first_update((2, 3))
    layers = outer_layers(1)

    arrive(2, 0)
    spectral(0, w2, lambda m, v, t0: in_n[m, v, t0 : t0 + 8, :])
    send(3, 0)
    inside(n1, 0, 2 * half)
    around(n1, 1, layers)

    def second_sum(spot, t):
        return n1[:, ORDER[spot], t, :] + ss[spot, :, t, :]

    keep_rows(qedge, (2, 3), ends, second_sum)
    rim2 = rim_of(8, qedge, qhalo, REST)
    interface(n1, 1, windows)
    keep_rows(qedge, (0, 1), ends, second_sum)
    rim = rim_of(12 + 2, qedge, qhalo, FRONT)

    far_rows = (0, 1, 2, 3, T - 4, T - 3, T - 2, T - 1)

    def last_source(spot, t):
        return ww[spot, :, 8 + t, :]

    arrive(3, 1)
    keep_rows(wedge, (2, 3), far_rows, last_source)
    far2 = rim_of(16, wedge, whalo, REST)
    arrive(3, 0)
    keep_rows(wedge, (0, 1), far_rows, last_source)
    far = rim_of(20, wedge, whalo, FRONT)

    def second_update(spots):
        for spot in spots:
            for n in range(2):
                ww[spot, :, 6 + n, :] = whalo[0, 2 + n, spot]
                ww[spot, :, T + 8 + n, :] = whalo[1, n, spot]
            for side in range(2):
                h = [whalo[side, n, spot] for n in range(4)]
                e = [wedge[side, n, spot] for n in range(4)]
                line = h + e[:2] if side == 0 else e[2:] + h
                mask = halo[0, side, NV, 0:1, :]
                for n in range(2):
                    x = line[n : n + 5]
                    z = 0.625 * x[2] + 0.125 * (x[1] + x[3]) + 0.0625 * (x[0] + x[4])
                    t = n - 2 if side == 0 else T + n
                    rr[spot, :, 8 + t, :] = qhalo[side, n, spot] - 0.05 * (z * mask)

        def variable(v):
            for spot in spots:
                a = ORDER[spot]
                rr[spot, v, 8 : T + 8] = (
                    n1[v, a] + ss[spot, v] - 0.05 * (smoothed(ww, spot, v) * active)
                )
                update = smoothed(rr, spot, v) * active
                last_update[v, a] = update
                new_state[v, a] = cur[v, a] - 0.05 * update

        over(NV, variable)

    for c in rim2 + far2:
        c.wait()
    second_update((2, 3))
    for c in rim + far:
        c.wait()
    second_update((0, 1))

    for c in layers + windows:
        c.wait_send()
    for unit in (1, 2, 3):
        gone(unit)


def local(n_dom, flow_state, donor_index, donor_weight, span_count):
    shape = (NV, AX, T, S)
    padded = (NV, AX, T + 16, S)
    pieces = (2, NI, NV, SLAB, S)
    turned = (AX, NV, T + 16, S)
    f32 = jnp.float32
    anywhere = pl.BlockSpec(memory_space=pl.ANY)
    vmem = pl.BlockSpec(memory_space=pltpu.VMEM)
    new_state, last_update = pl.pallas_call(
        functools.partial(kernel, n_dom, n_dom * T),
        out_shape=[jax.ShapeDtypeStruct(shape, f32)] * 2,
        in_specs=[anywhere] * 4,
        out_specs=[vmem, vmem],
        scratch_shapes=[
            pltpu.SMEM((2, T), jnp.int32),
            pltpu.SMEM((1,), jnp.int32),
            pltpu.VMEM((2, T), jnp.int32),
            pltpu.VMEM((2, T), f32),
            pltpu.VMEM(shape, f32),
            pltpu.VMEM(pieces, f32),
            pltpu.VMEM((NI, NV, SLAB, S), f32),
            pltpu.VMEM(pieces, f32),
            pltpu.VMEM(pieces, f32),
            pltpu.VMEM((AX, NV, T, S), f32),
            pltpu.VMEM(turned, f32),
            pltpu.VMEM(shape, f32),
            pltpu.VMEM(shape, f32),
            pltpu.VMEM(turned, f32),
            pltpu.VMEM(padded, f32),
            pltpu.VMEM(padded, f32),
            pltpu.VMEM((2, 3, T, S), f32),
            pltpu.VMEM((ITERS, 2, NV, 2 * T, S), f32),
            pltpu.VMEM((ITERS, 2, NV + 1, AX, S), f32),
            pltpu.VMEM((ITERS, 2, NV + 1, AX, S), f32),
            pltpu.VMEM((2, 2, AX, NV, S), f32),
            pltpu.VMEM((2, 2, AX, NV, S), f32),
            pltpu.VMEM((2, 2, AX, NV, S), f32),
            pltpu.VMEM((2, 2, AX, NV, S), f32),
            pltpu.VMEM((2, 4, AX, NV, S), f32),
            pltpu.VMEM((2, 4, AX, NV, S), f32),
            pltpu.VMEM((NI, NV, SLAB, S), f32),
            pltpu.VMEM((NI, NV, SLAB + 8, S), f32),
            pltpu.VMEM((NI, NV, SLAB + 8, S), f32),
            pltpu.VMEM((2, NV, NI, S), f32),
            pltpu.VMEM((2, NV, NI, S), f32),
            pltpu.SemaphoreType.DMA((5,)),
            pltpu.SemaphoreType.DMA((4,)),
            pltpu.SemaphoreType.DMA((4, 2)),
            pltpu.SemaphoreType.DMA((22,)),
            pltpu.SemaphoreType.DMA((22,)),
        ],
        compiler_params=pltpu.CompilerParams(
            collective_id=0, has_side_effects=True, vmem_limit_bytes=52 * 1024 * 1024
        ),
        cost_estimate=pl.CostEstimate(
            flops=20_000_000, bytes_accessed=3 * PL * T * S * 4, transcendentals=0
        ),
    )(flow_state.reshape(shape), donor_index[0], donor_weight[0], span_count)
    whole = (1, NV, AX, T, S)
    return new_state.reshape(whole), last_update.reshape(whole)


def solution(mesh):
    placed = (
        P("inst", None, None, "dom", None),
        P("inst", None, "dom"),
        P("inst", None, "dom"),
        P("dom"),
    )
    return jax.shard_map(
        functools.partial(local, mesh.shape["dom"]),
        mesh=mesh,
        in_specs=placed,
        out_specs=(P("inst", None, None, "dom", None), P("inst", None, None, "dom", None)),
        check_vma=False,
    )
```

```python
import functools
import math

import jax
import jax.numpy as jnp
import numpy as np
from jax import lax
from jax.experimental import pallas as pl
from jax.experimental.pallas import tpu as pltpu
from jax.sharding import PartitionSpec as P

ITERS = 2
NI = 8
NV = 6
AX = 4
PL = NV * AX
T = 64
S = 128
ZN = 4
SLAB = T // ZN
ORDER = (1, 2, 0, 3)
MESH = pl.DeviceIdType.MESH


def spectral_row():
    k = np.arange(NI)[:, None] - np.arange(NI)[None, :]
    safe = np.where(k == 0, 1.0, np.sin(math.pi * k / NI))
    deriv = np.where(k == 0, 0.0, 0.5 * (-1.0) ** k * np.cos(math.pi * k / NI) / safe)
    return (deriv - 0.1 * deriv @ deriv)[:, 0]


def spectral_apply(x):
    row = spectral_row()
    even = [float(row[j] + row[j + 4]) / 2 for j in range(4)]
    odd = [float(row[j] - row[j + 4]) / 2 for j in range(4)]
    s = [x[z] + x[z + 4] for z in range(4)]
    d = [x[z] - x[z + 4] for z in range(4)]
    q0, q1 = s[0] - s[2], s[1] - s[3]
    s0 = even[0] * q0 + even[3] * q1
    s1 = even[1] * q0 + even[0] * q1
    sym = [s0, s1, -s0, -s1]
    out = [None] * NI
    for z in range(4):
        acc = None
        for y in range(4):
            coef = odd[z - y] if y <= z else -odd[4 + z - y]
            term = coef * d[y]
            acc = term if acc is None else acc + term
        out[z] = sym[z] + acc
        out[z + 4] = sym[z] - acc
    return out


def primitives(u):
    inv = 1.0 / u[0]
    vel = [u[1] * inv, u[2] * inv, u[3] * inv]
    nu = u[5] * inv
    pres = 0.4 * (u[4] - 0.5 * (u[1] * vel[0] + u[2] * vel[1] + u[3] * vel[2]))
    return vel, nu, pres


def centre_terms(u, vel, nu):
    return [
        0.1 * u[0],
        0.1 * u[1] + 0.02 * vel[0],
        0.1 * u[2] + 0.02 * vel[1],
        0.1 * u[3] + 0.02 * vel[2],
        0.1 * u[4],
        0.1 * u[5] + 0.02 * nu,
    ]


def half_flux(u, vel, pres, k):
    h = 0.5 * vel[k]
    f = [0.5 * u[1 + k], u[1] * h, u[2] * h, u[3] * h, (u[4] + pres) * h, u[5] * h]
    f[1 + k] = f[1 + k] + 0.5 * pres
    return f


def next_terms(u, k):
    vel, nu, pres = primitives(u)
    c = centre_terms(u, vel, nu)
    return [f - g for f, g in zip(half_flux(u, vel, pres, k), c)]


def prev_terms(u, k):
    vel, nu, pres = primitives(u)
    c = centre_terms(u, vel, nu)
    return [-(f + g) for f, g in zip(half_flux(u, vel, pres, k), c)]


def kernel(
    n_dom,
    n_cells,
    flow,
    idx,
    wgt,
    count,
    new_state,
    last_update,
    idx_s,
    count_s,
    idx_v,
    wgt_v,
    cur,
    in_u,
    in_n,
    w1,
    w2,
    ss,
    ww,
    n0,
    n1,
    rr,
    a2,
    b2,
    coef,
    win,
    edge,
    halo,
    redge,
    rhalo,
    qedge,
    qhalo,
    wedge,
    whalo,
    slab_n,
    slab_a,
    slab_b,
    slab_out,
    slab_in,
    load_sem,
    p_send,
    p_recv,
    d_send,
    d_recv,
):
    inst = lax.axis_index("inst")
    dom = lax.axis_index("dom")
    left = lax.rem(dom + n_dom - 1, n_dom)
    right = lax.rem(dom + 1, n_dom)

    def flip(d):
        return d + 2 - 4 * lax.rem(d // 2, 2)

    work = flip(dom)
    body, place = inst // ZN, lax.rem(inst, ZN)
    at_start = jnp.where(place == 0, 1, 0)
    at_end = jnp.where(place == ZN - 1, 1, 0)
    before = flip(lax.rem(work + n_dom - at_start, n_dom))
    beyond = flip(lax.rem(work + at_end, n_dom))
    below = (body * ZN + lax.rem(place + ZN - 1, ZN), before)
    above = (body * ZN + lax.rem(place + 1, ZN), beyond)

    loads = [
        pltpu.make_async_copy(source, target, load_sem.at[n])
        for n, (source, target) in enumerate(
            ((flow, cur), (idx, idx_s), (idx, idx_v), (wgt, wgt_v), (count, count_s))
        )
    ]
    for c in loads:
        c.start()
    barrier = pltpu.get_barrier_semaphore()
    for j in range(NI):
        pl.semaphore_signal(barrier, inc=1, device_id=(j, work), device_id_type=MESH)
    for device in ((inst, left), (inst, right), below, above):
        pl.semaphore_signal(barrier, inc=1, device_id=device, device_id_type=MESH)

    def remote(source, target, send, recv, device):
        return pltpu.make_async_remote_copy(
            src_ref=source,
            dst_ref=target,
            send_sem=send,
            recv_sem=recv,
            device_id=device,
            device_id_type=MESH,
        )

    def piece(unit, partner, part, slot):
        side, slab = partner // ZN, lax.rem(partner, ZN)
        row = 1 + side if part == 0 else (AX - 1) * side
        mine = pl.ds(pl.multiple_of(SLAB * slab, SLAB), SLAB)
        spot = 2 * part + slot // ZN
        at = SLAB * lax.rem(slot, ZN)
        if unit == 0:
            source, target = flow.at[:, row, mine], in_u.at[part, slot]
        elif unit == 1:
            source = w1.at[part, partner]
            target = ss.at[spot, :, pl.ds(pl.multiple_of(at, SLAB), SLAB)]
        elif unit == 2:
            source, target = n0.at[:, row, mine], in_n.at[slot]
        else:
            source = w2.at[part, partner]
            target = ww.at[spot, :, pl.ds(pl.multiple_of(at + 8, 8), SLAB)]
        return remote(source, target, p_send.at[unit], p_recv.at[unit, part], (partner, work))

    order = [lax.rem(inst + n, NI) for n in range(NI)]

    def send(unit, part):
        for j in order:
            piece(unit, j, part, inst).start()

    def arrive(unit, part):
        spots = pl.ds(2 * part, 2)
        ref = (in_u.at[part], ss.at[spots], in_n, ww.at[spots, :, pl.ds(8, T)])[unit]
        pltpu.make_async_copy(ref, ref, p_recv.at[unit, part]).wait()

    def gone(unit):
        ref = (flow, w1, n0.at[:, 1:3], w2)[unit]
        pltpu.make_async_copy(ref, ref, p_send.at[unit]).wait()

    def near(slot, source, target, device):
        return remote(source, target, d_send.at[slot], d_recv.at[slot], (inst, device))

    def both(slot, out, back):
        return [near(slot, out(0), back(1), left), near(slot + 1, out(1), back(0), right)]

    def start(copies):
        for c in copies:
            c.start()
        return copies

    def over(n, body):
        def step(i, _):
            body(i)
            return 0

        lax.fori_loop(0, n, step, 0)

    lane = lax.broadcasted_iota(jnp.int32, (8, S), 1)
    first_lane = lane == 0
    last_lane = lane == S - 1

    def spanwise(f, c):
        out = []
        for g, h in zip(f, c):
            up, down = g - h, g + h
            after = jnp.where(last_lane, up, pltpu.roll(up, S - 1, 1))
            prior = jnp.where(first_lane, down, pltpu.roll(down, 1, 1))
            out.append(6.0 * h + (after - prior))
        return out

    def spectral(part, target, plus=None):
        def variable(v):
            for t0 in range(0, SLAB, 8):
                rows = slice(t0, t0 + 8)
                if plus is None:
                    x = [in_u[part, m, v, rows, :] for m in range(NI)]
                else:
                    x = [w1[part, m, v, rows, :] + plus(m, v, t0) for m in range(NI)]
                for m, g in enumerate(spectral_apply(x)):
                    target[part, m, v, rows, :] = g

        over(NV, variable)

    def inside(out, first_tile, last_tile):
        def tile(i, _):
            t0 = pl.multiple_of(8 * i, 8)
            total = []
            first = []
            second = []
            for a in range(AX):
                u = [cur[v, a, pl.ds(t0, 8), :] for v in range(NV)]
                vel, nu, pres = primitives(u)
                c = centre_terms(u, vel, nu)
                f1 = half_flux(u, vel, pres, 0)
                first.append([f - g for f, g in zip(f1, c)])
                second.append([f + g for f, g in zip(f1, c)])
                f2 = half_flux(u, vel, pres, 1)
                for v in range(NV):
                    a2[v, a, pl.ds(t0 + 8, 8), :] = f2[v] - c[v]
                    b2[v, a, pl.ds(t0 + 8, 8), :] = f2[v] + c[v]
                total.append(spanwise(half_flux(u, vel, pres, 2), c))
            for a in range(AX):
                for v in range(NV):
                    r = total[a][v]
                    if a == AX - 1:
                        r = r + first[a][v]
                    elif a != AX // 2 - 1:
                        r = r + first[a + 1][v]
                    if a == 0:
                        r = r - second[a][v]
                    elif a != AX // 2:
                        r = r - second[a - 1][v]
                    out[v, a, pl.ds(t0, 8), :] = r
            return 0

        lax.fori_loop(first_tile, last_tile, tile, 0)

    def around(out, it, layers):
        for c in layers:
            c.wait_recv()
        low = prev_terms([halo[it, 0, v] for v in range(NV)], 1)
        high = next_terms([halo[it, 1, v] for v in range(NV)], 1)
        for v in range(NV):
            for a in range(AX):
                b2[v, a, 7:8, :] = -low[v][a : a + 1]
                a2[v, a, T + 8 : T + 9, :] = high[v][a : a + 1]

        def variable(v):
            for a in range(AX):
                out[v, a] += a2[v, a, 9 : T + 9] - b2[v, a, 7 : T + 7]

        over(NV, variable)

    def interface(out, it, windows):
        for c in windows:
            c.wait_recv()

        def ghosts(i):
            t0 = pl.multiple_of(8 * i, 8)
            for side in range(2):
                taps = [coef[side, n, pl.ds(t0, 8), :] for n in range(3)]
                u = []
                for v in range(NV):
                    g = taps[0] * win[it, side, v, pl.ds(base[side] + t0, 8), :]
                    g = g + taps[1] * win[it, side, v, pl.ds(base[side] + t0 + 1, 8), :]
                    g = g + taps[2] * win[it, side, v, pl.ds(base[side] + t0 + 2, 8), :]
                    u.append(g)
                terms = next_terms(u, 0) if side == 0 else prev_terms(u, 0)
                for v in range(NV):
                    out[v, 1 + side, pl.ds(t0, 8), :] += terms[v]

        over(T // 8, ghosts)

    def outer_layers(it):
        for side, t in enumerate((0, T - 1)):
            for v in range(NV):
                edge[it, side, v] = cur[v, :, t, :]
            edge[it, side, NV] = jnp.broadcast_to(active, (AX, S))
        return start(
            both(10 * it, lambda side: edge.at[it, side], lambda side: halo.at[it, side])
        )

    def interface_rows(it):
        for v in range(NV):
            win[it, 0, v, 0:T] = cur[v, 2]
            win[it, 1, v, T : 2 * T] = cur[v, 1]
        return start(
            [
                near(10 * it + 2, win.at[it, 0, :, 0:T], win.at[it, 0, :, T : 2 * T], left),
                near(10 * it + 3, win.at[it, 1, :, T : 2 * T], win.at[it, 1, :, 0:T], right),
            ]
        )

    def rim_of(slot, out, back, spots):
        return start(both(slot, lambda side: out.at[side, spots], lambda side: back.at[side, spots]))

    FRONT, REST = pl.ds(0, 2), pl.ds(2, 2)

    pl.semaphore_wait(barrier, NI + 4)
    for part in range(2):
        send(0, part)
    for c in loads:
        c.wait()
    active = jnp.where(lax.broadcasted_iota(jnp.int32, (1, S), 1) < count_s[0], 1.0, 0.0)
    layers = outer_layers(0)
    windows = interface_rows(0)

    def least(t, low):
        cell = dom * T + t
        gaps = (idx_s[0, t] - cell, cell - 1 - idx_s[1, t])
        gaps = [jnp.where(g < 0, g + n_cells, g) for g in gaps]
        return jnp.minimum(low[0], gaps[0]), jnp.minimum(low[1], gaps[1])

    most = (jnp.int32(n_cells), jnp.int32(n_cells))
    offset = [jnp.clip(x, 0, T - 2) for x in lax.fori_loop(0, T, least, most)]
    base = [offset[0], T - 2 - offset[1]]
    eye = lax.broadcasted_iota(jnp.int32, (T, T), 0) == lax.broadcasted_iota(
        jnp.int32, (T, T), 1
    )
    for side in range(2):
        cell = dom * T + lax.broadcasted_iota(jnp.int32, (1, T), 1)
        row = idx_v[side : side + 1, :]
        gap = row - cell if side == 0 else cell - 1 - row
        gap = jnp.where(gap < 0, gap + n_cells, gap)
        step = jnp.where(gap > offset[side], 1.0, 0.0)
        w = wgt_v[side : side + 1, :]
        taps = [(1.0 - step) * w, step * w + (1.0 - step) * (1.0 - w), step * (1.0 - w)]
        if side == 1:
            taps = [step * w, (1.0 - step) * w + step * (1.0 - w), (1.0 - step) * (1.0 - w)]
        for i, tap in enumerate(taps):
            column = jnp.sum(jnp.where(eye, tap, 0.0), axis=1, keepdims=True)
            coef[side, i] = jnp.broadcast_to(column, (T, S))

    half = T // 16
    inside(n0, 0, half)
    arrive(0, 0)
    spectral(0, w1)
    send(1, 0)
    arrive(0, 1)
    for v in range(NV):
        slab_out[0, v] = in_u[1, :, v, 0, :]
        slab_out[1, v] = in_u[1, :, v, SLAB - 1, :]
    slabs = start(
        [
            remote(slab_out.at[0], slab_in.at[1], d_send.at[18], d_recv.at[18], below),
            remote(slab_out.at[1], slab_in.at[0], d_send.at[19], d_recv.at[19], above),
        ]
    )
    spectral(1, w1)
    send(1, 1)
    inside(n0, half, 2 * half)
    around(n0, 0, layers)
    interface(n0, 0, windows)
    send(2, 0)

    toward = jnp.where(body == 0, 1.0, -1.0)

    def slab_inside(m):
        for t0 in range(0, SLAB, 8):
            rows = slice(t0, t0 + 8)
            u = [in_u[0, m, v, rows, :] for v in range(NV)]
            vel, nu, pres = primitives(u)
            c1 = centre_terms(u, vel, nu)
            f1 = half_flux(u, vel, pres, 0)
            u = [in_u[1, m, v, rows, :] for v in range(NV)]
            vel, nu, pres = primitives(u)
            c = centre_terms(u, vel, nu)
            f = half_flux(u, vel, pres, 0)
            f2 = half_flux(u, vel, pres, 1)
            r = spanwise(half_flux(u, vel, pres, 2), c)
            for v in range(NV):
                slab_a[m, v, t0 : t0 + 8, :] = f2[v] - c[v]
                slab_b[m, v, t0 + 8 : t0 + 16, :] = f2[v] + c[v]
                slab_n[m, v, rows, :] = r[v] + (toward * (f1[v] - f[v]) - (c1[v] + c[v]))

    over(NI, slab_inside)
    for c in slabs:
        c.wait()
    low = prev_terms([slab_in[0, v] for v in range(NV)], 1)
    high = next_terms([slab_in[1, v] for v in range(NV)], 1)
    for v in range(NV):
        slab_b[:, v, 7, :] = -low[v]
        slab_a[:, v, SLAB, :] = high[v]

    def outer(m, v, t0):
        return slab_n[m, v, t0 : t0 + 8, :] + (
            slab_a[m, v, t0 + 1 : t0 + 9, :] - slab_b[m, v, t0 + 7 : t0 + 15, :]
        )

    spectral(1, w2, outer)

    def keep_rows(out, spots, value):
        n = out.shape[3]
        for spot in spots:
            for v in range(NV):
                out[0, spot, v] = value(spot, v, 0, n)
                out[1, spot, v] = value(spot, v, T - n, T)

    def put_rows(back, spots):
        for spot in spots:
            for v in range(NV):
                rr[spot, v, 6:8, :] = back[0, spot, v]
                rr[spot, v, T + 8 : T + 10, :] = back[1, spot, v]

    def smoothed(ref, spot, v):
        return (
            0.625 * ref[spot, v, 8 : T + 8]
            + 0.125 * (ref[spot, v, 7 : T + 7] + ref[spot, v, 9 : T + 9])
            + 0.0625 * (ref[spot, v, 6 : T + 6] + ref[spot, v, 10 : T + 10])
        )

    def sums(spots):
        def variable(v):
            for spot in spots:
                rr[spot, v, 8 : T + 8] = n0[v, ORDER[spot]] + ss[spot, v]

        over(NV, variable)

    def first_update(spots):
        def variable(v):
            for spot in spots:
                a = ORDER[spot]
                cur[v, a] = cur[v, a] - 0.05 * (smoothed(rr, spot, v) * active)

        over(NV, variable)

    def first_sum(spot, v, t0, t1):
        return n0[v, ORDER[spot], t0:t1, :] + ss[spot, v, t0:t1, :]

    arrive(1, 0)
    keep_rows(redge, (0, 1), first_sum)
    rim = rim_of(4, redge, rhalo, FRONT)
    sums((0, 1))
    arrive(1, 1)
    keep_rows(redge, (2, 3), first_sum)
    rim2 = rim_of(6, redge, rhalo, REST)
    for c in rim:
        c.wait()
    put_rows(rhalo, (0, 1))
    gone(0)
    for c in layers + windows:
        c.wait_send()
    first_update((0, 1))
    windows = interface_rows(1)
    send(3, 1)
    sums((2, 3))
    for c in rim2:
        c.wait()
    put_rows(rhalo, (2, 3))
    first_update((2, 3))
    layers = outer_layers(1)

    arrive(2, 0)
    spectral(0, w2, lambda m, v, t0: in_n[m, v, t0 : t0 + 8, :])
    send(3, 0)
    inside(n1, 0, 2 * half)
    around(n1, 1, layers)

    def second_sum(spot, v, t0, t1):
        return n1[v, ORDER[spot], t0:t1, :] + ss[spot, v, t0:t1, :]

    keep_rows(qedge, (2, 3), second_sum)
    rim2 = rim_of(8, qedge, qhalo, REST)
    interface(n1, 1, windows)
    keep_rows(qedge, (0, 1), second_sum)
    rim = rim_of(12 + 2, qedge, qhalo, FRONT)

    def last_source(spot, v, t0, t1):
        return ww[spot, v, 8 + t0 : 8 + t1, :]

    arrive(3, 1)
    keep_rows(wedge, (2, 3), last_source)
    far2 = rim_of(16, wedge, whalo, REST)
    arrive(3, 0)
    keep_rows(wedge, (0, 1), last_source)
    far = rim_of(20, wedge, whalo, FRONT)

    masks = [halo[0, side, NV, 0:1, :] for side in range(2)]

    def second_update(spots):
        def variable(v):
            for spot in spots:
                a = ORDER[spot]
                ww[spot, v, 4:8, :] = whalo[0, spot, v]
                ww[spot, v, T + 8 : T + 12, :] = whalo[1, spot, v]
                for side, t in enumerate((6, T + 8)):
                    z = (
                        0.625 * ww[spot, v, t : t + 2, :]
                        + 0.125 * (ww[spot, v, t - 1 : t + 1, :] + ww[spot, v, t + 1 : t + 3, :])
                        + 0.0625 * (ww[spot, v, t - 2 : t, :] + ww[spot, v, t + 2 : t + 4, :])
                    )
                    rr[spot, v, t : t + 2, :] = qhalo[side, spot, v] - 0.05 * (z * masks[side])
                rr[spot, v, 8 : T + 8] = (
                    n1[v, a] + ss[spot, v] - 0.05 * (smoothed(ww, spot, v) * active)
                )
                update = smoothed(rr, spot, v) * active
                last_update[v, a] = update
                new_state[v, a] = cur[v, a] - 0.05 * update

        over(NV, variable)

    for c in rim2 + far2:
        c.wait()
    second_update((2, 3))
    for c in rim + far:
        c.wait()
    second_update((0, 1))

    for c in layers + windows:
        c.wait_send()
    for unit in (1, 2, 3):
        gone(unit)


def local(n_dom, flow_state, donor_index, donor_weight, span_count):
    shape = (NV, AX, T, S)
    padded = (NV, AX, T + 16, S)
    pieces = (2, NI, NV, SLAB, S)
    turned = (AX, NV, T + 16, S)
    f32 = jnp.float32
    anywhere = pl.BlockSpec(memory_space=pl.ANY)
    vmem = pl.BlockSpec(memory_space=pltpu.VMEM)
    new_state, last_update = pl.pallas_call(
        functools.partial(kernel, n_dom, n_dom * T),
        out_shape=[jax.ShapeDtypeStruct(shape, f32)] * 2,
        in_specs=[anywhere] * 4,
        out_specs=[vmem, vmem],
        scratch_shapes=[
            pltpu.SMEM((2, T), jnp.int32),
            pltpu.SMEM((1,), jnp.int32),
            pltpu.VMEM((2, T), jnp.int32),
            pltpu.VMEM((2, T), f32),
            pltpu.VMEM(shape, f32),
            pltpu.VMEM(pieces, f32),
            pltpu.VMEM((NI, NV, SLAB, S), f32),
            pltpu.VMEM(pieces, f32),
            pltpu.VMEM(pieces, f32),
            pltpu.VMEM((AX, NV, T, S), f32),
            pltpu.VMEM(turned, f32),
            pltpu.VMEM(shape, f32),
            pltpu.VMEM(shape, f32),
            pltpu.VMEM(turned, f32),
            pltpu.VMEM(padded, f32),
            pltpu.VMEM(padded, f32),
            pltpu.VMEM((2, 3, T, S), f32),
            pltpu.VMEM((ITERS, 2, NV, 2 * T, S), f32),
            pltpu.VMEM((ITERS, 2, NV + 1, AX, S), f32),
            pltpu.VMEM((ITERS, 2, NV + 1, AX, S), f32),
            pltpu.VMEM((2, AX, NV, 2, S), f32),
            pltpu.VMEM((2, AX, NV, 2, S), f32),
            pltpu.VMEM((2, AX, NV, 2, S), f32),
            pltpu.VMEM((2, AX, NV, 2, S), f32),
            pltpu.VMEM((2, AX, NV, 4, S), f32),
            pltpu.VMEM((2, AX, NV, 4, S), f32),
            pltpu.VMEM((NI, NV, SLAB, S), f32),
            pltpu.VMEM((NI, NV, SLAB + 8, S), f32),
            pltpu.VMEM((NI, NV, SLAB + 8, S), f32),
            pltpu.VMEM((2, NV, NI, S), f32),
            pltpu.VMEM((2, NV, NI, S), f32),
            pltpu.SemaphoreType.DMA((5,)),
            pltpu.SemaphoreType.DMA((4,)),
            pltpu.SemaphoreType.DMA((4, 2)),
            pltpu.SemaphoreType.DMA((22,)),
            pltpu.SemaphoreType.DMA((22,)),
        ],
        compiler_params=pltpu.CompilerParams(
            collective_id=0, has_side_effects=True, vmem_limit_bytes=52 * 1024 * 1024
        ),
        cost_estimate=pl.CostEstimate(
            flops=20_000_000, bytes_accessed=3 * PL * T * S * 4, transcendentals=0
        ),
    )(flow_state.reshape(shape), donor_index[0], donor_weight[0], span_count)
    whole = (1, NV, AX, T, S)
    return new_state.reshape(whole), last_update.reshape(whole)


def solution(mesh):
    placed = (
        P("inst", None, None, "dom", None),
        P("inst", None, "dom"),
        P("inst", None, "dom"),
        P("dom"),
    )
    return jax.shard_map(
        functools.partial(local, mesh.shape["dom"]),
        mesh=mesh,
        in_specs=placed,
        out_specs=(P("inst", None, None, "dom", None), P("inst", None, None, "dom", None)),
        check_vma=False,
    )
```

```python
import functools
import math

import jax
import jax.numpy as jnp
import numpy as np
from jax import lax
from jax.experimental import pallas as pl
from jax.experimental.pallas import tpu as pltpu
from jax.sharding import PartitionSpec as P

ITERS = 2
NI = 8
NV = 6
AX = 4
PL = NV * AX
T = 64
S = 128
ZN = 4
SLAB = T // ZN
ORDER = (1, 2, 0, 3)
MESH = pl.DeviceIdType.MESH


def spectral_row():
    k = np.arange(NI)[:, None] - np.arange(NI)[None, :]
    safe = np.where(k == 0, 1.0, np.sin(math.pi * k / NI))
    deriv = np.where(k == 0, 0.0, 0.5 * (-1.0) ** k * np.cos(math.pi * k / NI) / safe)
    return (deriv - 0.1 * deriv @ deriv)[:, 0]


def spectral_apply(x):
    row = spectral_row()
    even = [float(row[j] + row[j + 4]) / 2 for j in range(4)]
    odd = [float(row[j] - row[j + 4]) / 2 for j in range(4)]
    s = [x[z] + x[z + 4] for z in range(4)]
    d = [x[z] - x[z + 4] for z in range(4)]
    q0, q1 = s[0] - s[2], s[1] - s[3]
    s0 = even[0] * q0 + even[3] * q1
    s1 = even[1] * q0 + even[0] * q1
    sym = [s0, s1, -s0, -s1]
    out = [None] * NI
    for z in range(4):
        acc = None
        for y in range(4):
            coef = odd[z - y] if y <= z else -odd[4 + z - y]
            term = coef * d[y]
            acc = term if acc is None else acc + term
        out[z] = sym[z] + acc
        out[z + 4] = sym[z] - acc
    return out


def primitives(u):
    inv = 1.0 / u[0]
    vel = [u[1] * inv, u[2] * inv, u[3] * inv]
    nu = u[5] * inv
    pres = 0.4 * (u[4] - 0.5 * (u[1] * vel[0] + u[2] * vel[1] + u[3] * vel[2]))
    return vel, nu, pres


def centre_terms(u, vel, nu):
    return [
        0.1 * u[0],
        0.1 * u[1] + 0.02 * vel[0],
        0.1 * u[2] + 0.02 * vel[1],
        0.1 * u[3] + 0.02 * vel[2],
        0.1 * u[4],
        0.1 * u[5] + 0.02 * nu,
    ]


def half_flux(u, vel, pres, k):
    h = 0.5 * vel[k]
    f = [0.5 * u[1 + k], u[1] * h, u[2] * h, u[3] * h, (u[4] + pres) * h, u[5] * h]
    f[1 + k] = f[1 + k] + 0.5 * pres
    return f


def next_terms(u, k):
    vel, nu, pres = primitives(u)
    c = centre_terms(u, vel, nu)
    return [f - g for f, g in zip(half_flux(u, vel, pres, k), c)]


def prev_terms(u, k):
    vel, nu, pres = primitives(u)
    c = centre_terms(u, vel, nu)
    return [-(f + g) for f, g in zip(half_flux(u, vel, pres, k), c)]


def kernel(
    n_dom,
    n_cells,
    flow,
    idx,
    wgt,
    count,
    new_state,
    last_update,
    idx_s,
    count_s,
    idx_v,
    wgt_v,
    cur,
    in_u,
    in_n,
    w1,
    w2,
    ss,
    ww,
    n0,
    n1,
    rr,
    a2,
    b2,
    coef,
    win,
    edge,
    halo,
    redge,
    rhalo,
    qedge,
    qhalo,
    wedge,
    whalo,
    slab_n,
    slab_a,
    slab_b,
    slab_out,
    slab_in,
    load_sem,
    p_send,
    p_recv,
    f_send,
    d_send,
    d_recv,
):
    inst = lax.axis_index("inst")
    dom = lax.axis_index("dom")
    left = lax.rem(dom + n_dom - 1, n_dom)
    right = lax.rem(dom + 1, n_dom)

    def flip(d):
        return d + 2 - 4 * lax.rem(d // 2, 2)

    work = flip(dom)
    body, place = inst // ZN, lax.rem(inst, ZN)
    at_start = jnp.where(place == 0, 1, 0)
    at_end = jnp.where(place == ZN - 1, 1, 0)
    before = flip(lax.rem(work + n_dom - at_start, n_dom))
    beyond = flip(lax.rem(work + at_end, n_dom))
    before_block = lax.rem(work + n_dom - 1, n_dom)
    after_block = lax.rem(work + 1, n_dom)
    below = (body * ZN + lax.rem(place + ZN - 1, ZN), before)
    above = (body * ZN + lax.rem(place + 1, ZN), beyond)

    loads = [
        pltpu.make_async_copy(source, target, load_sem.at[n])
        for n, (source, target) in enumerate(
            ((flow, cur), (idx, idx_s), (idx, idx_v), (wgt, wgt_v), (count, count_s))
        )
    ]
    for c in loads:
        c.start()
    barrier = pltpu.get_barrier_semaphore()
    for j in range(NI):
        pl.semaphore_signal(barrier, inc=1, device_id=(j, work), device_id_type=MESH)
    for device in ((inst, left), (inst, right), below, above):
        pl.semaphore_signal(barrier, inc=1, device_id=device, device_id_type=MESH)

    core = lax.rem(dom, 2)
    gets_handed = [body * core, (1 - body) * (1 - core)]
    hands_on = [body * (1 - core), (1 - body) * core]
    for side, block in ((0, right), (1, left)):

        @pl.when(gets_handed[side] == 1)
        def _(side=side, block=block):
            for q in range(ZN):
                device = ((1 - side) * ZN + q, flip(block))
                pl.semaphore_signal(barrier, inc=1, device_id=device, device_id_type=MESH)

    def remote(source, target, send, recv, device):
        return pltpu.make_async_remote_copy(
            src_ref=source,
            dst_ref=target,
            send_sem=send,
            recv_sem=recv,
            device_id=device,
            device_id_type=MESH,
        )

    def piece(unit, partner, part, slot):
        side, slab = partner // ZN, lax.rem(partner, ZN)
        row = 1 + side if part == 0 else (AX - 1) * side
        mine = pl.ds(pl.multiple_of(SLAB * slab, SLAB), SLAB)
        spot = 2 * part + slot // ZN
        at = SLAB * lax.rem(slot, ZN)
        if unit == 0:
            source, target = flow.at[:, row, mine], in_u.at[part, slot]
        elif unit == 1:
            source = w1.at[part, partner]
            target = ss.at[spot, :, pl.ds(pl.multiple_of(at, SLAB), SLAB)]
        elif unit == 2:
            source, target = n0.at[:, row, mine], in_n.at[slot]
        else:
            source = w2.at[part, partner]
            target = ww.at[spot, :, pl.ds(pl.multiple_of(at + 8, 8), SLAB)]
        return remote(source, target, p_send.at[unit], p_recv.at[unit, part], (partner, work))

    order = [lax.rem(inst + n, NI) for n in range(NI)]

    def send(unit, part):
        for j in order:
            piece(unit, j, part, inst).start()

    def arrive(unit, part):
        spots = pl.ds(2 * part, 2)
        ref = (in_u.at[part], ss.at[spots], in_n, ww.at[spots, :, pl.ds(8, T)])[unit]
        pltpu.make_async_copy(ref, ref, p_recv.at[unit, part]).wait()

    def gone(unit):
        ref = (flow, w1, n0.at[:, 1:3], w2)[unit]
        pltpu.make_async_copy(ref, ref, p_send.at[unit]).wait()

    def near(slot, source, target, device):
        return remote(source, target, d_send.at[slot], d_recv.at[slot], (inst, device))

    def both(slot, out, back):
        return [near(slot, out(0), back(1), left), near(slot + 1, out(1), back(0), right)]

    def start(copies):
        for c in copies:
            c.start()
        return copies

    def over(n, body):
        def step(i, _):
            body(i)
            return 0

        lax.fori_loop(0, n, step, 0)

    lane = lax.broadcasted_iota(jnp.int32, (8, S), 1)
    first_lane = lane == 0
    last_lane = lane == S - 1

    def spanwise(f, c):
        out = []
        for g, h in zip(f, c):
            up, down = g - h, g + h
            after = jnp.where(last_lane, up, pltpu.roll(up, S - 1, 1))
            prior = jnp.where(first_lane, down, pltpu.roll(down, 1, 1))
            out.append(6.0 * h + (after - prior))
        return out

    def spectral(part, target, plus=None):
        def variable(v):
            for t0 in range(0, SLAB, 8):
                rows = slice(t0, t0 + 8)
                if plus is None:
                    x = [in_u[part, m, v, rows, :] for m in range(NI)]
                else:
                    x = [w1[part, m, v, rows, :] + plus(m, v, t0) for m in range(NI)]
                for m, g in enumerate(spectral_apply(x)):
                    target[part, m, v, rows, :] = g

        over(NV, variable)

    def inside(out, first_tile, last_tile):
        def tile(i, _):
            t0 = pl.multiple_of(8 * i, 8)
            total = []
            first = []
            second = []
            for a in range(AX):
                u = [cur[v, a, pl.ds(t0, 8), :] for v in range(NV)]
                vel, nu, pres = primitives(u)
                c = centre_terms(u, vel, nu)
                f1 = half_flux(u, vel, pres, 0)
                first.append([f - g for f, g in zip(f1, c)])
                second.append([f + g for f, g in zip(f1, c)])
                f2 = half_flux(u, vel, pres, 1)
                for v in range(NV):
                    a2[v, a, pl.ds(t0 + 8, 8), :] = f2[v] - c[v]
                    b2[v, a, pl.ds(t0 + 8, 8), :] = f2[v] + c[v]
                total.append(spanwise(half_flux(u, vel, pres, 2), c))
            for a in range(AX):
                for v in range(NV):
                    r = total[a][v]
                    if a == AX - 1:
                        r = r + first[a][v]
                    elif a != AX // 2 - 1:
                        r = r + first[a + 1][v]
                    if a == 0:
                        r = r - second[a][v]
                    elif a != AX // 2:
                        r = r - second[a - 1][v]
                    out[v, a, pl.ds(t0, 8), :] = r
            return 0

        lax.fori_loop(first_tile, last_tile, tile, 0)

    def around(out, it, layers):
        for c in layers:
            c.wait_recv()
        low = prev_terms([halo[it, 0, v] for v in range(NV)], 1)
        high = next_terms([halo[it, 1, v] for v in range(NV)], 1)
        for v in range(NV):
            for a in range(AX):
                b2[v, a, 7:8, :] = -low[v][a : a + 1]
                a2[v, a, T + 8 : T + 9, :] = high[v][a : a + 1]

        def variable(v):
            for a in range(AX):
                out[v, a] += a2[v, a, 9 : T + 9] - b2[v, a, 7 : T + 7]

        over(NV, variable)

    def interface(out, it, windows):
        for c in windows:
            c.wait_recv()

        def ghosts(i):
            t0 = pl.multiple_of(8 * i, 8)
            for side in range(2):
                taps = [coef[side, n, pl.ds(t0, 8), :] for n in range(3)]
                u = []
                for v in range(NV):
                    g = taps[0] * win[it, side, v, pl.ds(base[side] + t0, 8), :]
                    g = g + taps[1] * win[it, side, v, pl.ds(base[side] + t0 + 1, 8), :]
                    g = g + taps[2] * win[it, side, v, pl.ds(base[side] + t0 + 2, 8), :]
                    u.append(g)
                terms = next_terms(u, 0) if side == 0 else prev_terms(u, 0)
                for v in range(NV):
                    out[v, 1 + side, pl.ds(t0, 8), :] += terms[v]

        over(T // 8, ghosts)

    def outer_layers(it):
        for side, t in enumerate((0, T - 1)):
            for v in range(NV):
                edge[it, side, v] = cur[v, :, t, :]
            edge[it, side, NV] = jnp.broadcast_to(active, (AX, S))
        return start(
            both(10 * it, lambda side: edge.at[it, side], lambda side: halo.at[it, side])
        )

    def interface_rows(it):
        for v in range(NV):
            win[it, 0, v, 0:T] = cur[v, 2]
            win[it, 1, v, T : 2 * T] = cur[v, 1]
        windows = [
            near(10 * it + 2, win.at[it, 0, :, 0:T], win.at[it, 0, :, T : 2 * T], left),
            near(10 * it + 3, win.at[it, 1, :, T : 2 * T], win.at[it, 1, :, 0:T], right),
        ]
        if it > 0:
            return start(windows)
        for side in range(2):
            pl.when(hands_on[side] == 0)(windows[side].start)
        return windows

    def hand_on():
        for side, block in ((0, before_block), (1, after_block)):
            rows = pl.ds(pl.multiple_of((1 - side) * T + SLAB * place, SLAB), SLAB)

            @pl.when(hands_on[side] == 1)
            def _(side=side, block=block, rows=rows):
                for n in range(ZN):
                    m = (1 - side) * ZN + lax.rem(place + n, ZN)
                    remote(
                        in_u.at[0, m],
                        win.at[0, side, :, rows],
                        f_send,
                        d_recv.at[2 + side],
                        (m, block),
                    ).start()

    def handed_on():
        for side in range(2):

            @pl.when(hands_on[side] == 1)
            def _():
                ref = in_u.at[0, 0:ZN]
                pltpu.make_async_copy(ref, ref, f_send).wait()

            pl.when(hands_on[side] == 0)(windows[side].wait_send)

    def rim_of(slot, out, back, spots):
        return start(both(slot, lambda side: out.at[side, spots], lambda side: back.at[side, spots]))

    FRONT, REST = pl.ds(0, 2), pl.ds(2, 2)

    pl.semaphore_wait(barrier, NI + 4 + ZN * (hands_on[0] + hands_on[1]))
    for part in range(2):
        send(0, part)
    for c in loads:
        c.wait()
    active = jnp.where(lax.broadcasted_iota(jnp.int32, (1, S), 1) < count_s[0], 1.0, 0.0)
    layers = outer_layers(0)
    windows = interface_rows(0)

    def least(t, low):
        cell = dom * T + t
        gaps = (idx_s[0, t] - cell, cell - 1 - idx_s[1, t])
        gaps = [jnp.where(g < 0, g + n_cells, g) for g in gaps]
        return jnp.minimum(low[0], gaps[0]), jnp.minimum(low[1], gaps[1])

    most = (jnp.int32(n_cells), jnp.int32(n_cells))
    offset = [jnp.clip(x, 0, T - 2) for x in lax.fori_loop(0, T, least, most)]
    base = [offset[0], T - 2 - offset[1]]
    eye = lax.broadcasted_iota(jnp.int32, (T, T), 0) == lax.broadcasted_iota(
        jnp.int32, (T, T), 1
    )
    for side in range(2):
        cell = dom * T + lax.broadcasted_iota(jnp.int32, (1, T), 1)
        row = idx_v[side : side + 1, :]
        gap = row - cell if side == 0 else cell - 1 - row
        gap = jnp.where(gap < 0, gap + n_cells, gap)
        step = jnp.where(gap > offset[side], 1.0, 0.0)
        w = wgt_v[side : side + 1, :]
        taps = [(1.0 - step) * w, step * w + (1.0 - step) * (1.0 - w), step * (1.0 - w)]
        if side == 1:
            taps = [step * w, (1.0 - step) * w + step * (1.0 - w), (1.0 - step) * (1.0 - w)]
        for i, tap in enumerate(taps):
            column = jnp.sum(jnp.where(eye, tap, 0.0), axis=1, keepdims=True)
            coef[side, i] = jnp.broadcast_to(column, (T, S))

    half = T // 16
    inside(n0, 0, half)
    arrive(0, 0)
    hand_on()
    spectral(0, w1)
    send(1, 0)
    arrive(0, 1)
    for v in range(NV):
        slab_out[0, v] = in_u[1, :, v, 0, :]
        slab_out[1, v] = in_u[1, :, v, SLAB - 1, :]
    slabs = start(
        [
            remote(slab_out.at[0], slab_in.at[1], d_send.at[18], d_recv.at[18], below),
            remote(slab_out.at[1], slab_in.at[0], d_send.at[19], d_recv.at[19], above),
        ]
    )
    spectral(1, w1)
    send(1, 1)
    inside(n0, half, 2 * half)
    around(n0, 0, layers)
    interface(n0, 0, windows)
    send(2, 0)

    toward = jnp.where(body == 0, 1.0, -1.0)

    def slab_inside(m):
        for t0 in range(0, SLAB, 8):
            rows = slice(t0, t0 + 8)
            u = [in_u[0, m, v, rows, :] for v in range(NV)]
            vel, nu, pres = primitives(u)
            c1 = centre_terms(u, vel, nu)
            f1 = half_flux(u, vel, pres, 0)
            u = [in_u[1, m, v, rows, :] for v in range(NV)]
            vel, nu, pres = primitives(u)
            c = centre_terms(u, vel, nu)
            f = half_flux(u, vel, pres, 0)
            f2 = half_flux(u, vel, pres, 1)
            r = spanwise(half_flux(u, vel, pres, 2), c)
            for v in range(NV):
                slab_a[m, v, t0 : t0 + 8, :] = f2[v] - c[v]
                slab_b[m, v, t0 + 8 : t0 + 16, :] = f2[v] + c[v]
                slab_n[m, v, rows, :] = r[v] + (toward * (f1[v] - f[v]) - (c1[v] + c[v]))

    over(NI, slab_inside)
    for c in slabs:
        c.wait()
    low = prev_terms([slab_in[0, v] for v in range(NV)], 1)
    high = next_terms([slab_in[1, v] for v in range(NV)], 1)
    for v in range(NV):
        slab_b[:, v, 7, :] = -low[v]
        slab_a[:, v, SLAB, :] = high[v]

    def outer(m, v, t0):
        return slab_n[m, v, t0 : t0 + 8, :] + (
            slab_a[m, v, t0 + 1 : t0 + 9, :] - slab_b[m, v, t0 + 7 : t0 + 15, :]
        )

    spectral(1, w2, outer)

    def keep_rows(out, spots, value):
        n = out.shape[3]
        for spot in spots:
            for v in range(NV):
                out[0, spot, v] = value(spot, v, 0, n)
                out[1, spot, v] = value(spot, v, T - n, T)

    def put_rows(back, spots):
        for spot in spots:
            for v in range(NV):
                rr[spot, v, 6:8, :] = back[0, spot, v]
                rr[spot, v, T + 8 : T + 10, :] = back[1, spot, v]

    def smoothed(ref, spot, v):
        return (
            0.625 * ref[spot, v, 8 : T + 8]
            + 0.125 * (ref[spot, v, 7 : T + 7] + ref[spot, v, 9 : T + 9])
            + 0.0625 * (ref[spot, v, 6 : T + 6] + ref[spot, v, 10 : T + 10])
        )

    def sums(spots):
        def variable(v):
            for spot in spots:
                rr[spot, v, 8 : T + 8] = n0[v, ORDER[spot]] + ss[spot, v]

        over(NV, variable)

    def first_update(spots):
        def variable(v):
            for spot in spots:
                a = ORDER[spot]
                cur[v, a] = cur[v, a] - 0.05 * (smoothed(rr, spot, v) * active)

        over(NV, variable)

    def first_sum(spot, v, t0, t1):
        return n0[v, ORDER[spot], t0:t1, :] + ss[spot, v, t0:t1, :]

    arrive(1, 0)
    keep_rows(redge, (0, 1), first_sum)
    rim = rim_of(4, redge, rhalo, FRONT)
    sums((0, 1))
    arrive(1, 1)
    keep_rows(redge, (2, 3), first_sum)
    rim2 = rim_of(6, redge, rhalo, REST)
    for c in rim:
        c.wait()
    put_rows(rhalo, (0, 1))
    gone(0)
    for c in layers:
        c.wait_send()
    handed_on()
    first_update((0, 1))
    windows = interface_rows(1)
    send(3, 1)
    sums((2, 3))
    for c in rim2:
        c.wait()
    put_rows(rhalo, (2, 3))
    first_update((2, 3))
    layers = outer_layers(1)

    arrive(2, 0)
    spectral(0, w2, lambda m, v, t0: in_n[m, v, t0 : t0 + 8, :])
    send(3, 0)
    inside(n1, 0, 2 * half)
    around(n1, 1, layers)

    def second_sum(spot, v, t0, t1):
        return n1[v, ORDER[spot], t0:t1, :] + ss[spot, v, t0:t1, :]

    keep_rows(qedge, (2, 3), second_sum)
    rim2 = rim_of(8, qedge, qhalo, REST)
    interface(n1, 1, windows)
    keep_rows(qedge, (0, 1), second_sum)
    rim = rim_of(12 + 2, qedge, qhalo, FRONT)

    def last_source(spot, v, t0, t1):
        return ww[spot, v, 8 + t0 : 8 + t1, :]

    arrive(3, 1)
    keep_rows(wedge, (2, 3), last_source)
    far2 = rim_of(16, wedge, whalo, REST)
    arrive(3, 0)
    keep_rows(wedge, (0, 1), last_source)
    far = rim_of(20, wedge, whalo, FRONT)

    masks = [halo[0, side, NV, 0:1, :] for side in range(2)]

    def second_update(spots):
        def variable(v):
            for spot in spots:
                a = ORDER[spot]
                ww[spot, v, 4:8, :] = whalo[0, spot, v]
                ww[spot, v, T + 8 : T + 12, :] = whalo[1, spot, v]
                for side, t in enumerate((6, T + 8)):
                    z = (
                        0.625 * ww[spot, v, t : t + 2, :]
                        + 0.125 * (ww[spot, v, t - 1 : t + 1, :] + ww[spot, v, t + 1 : t + 3, :])
                        + 0.0625 * (ww[spot, v, t - 2 : t, :] + ww[spot, v, t + 2 : t + 4, :])
                    )
                    rr[spot, v, t : t + 2, :] = qhalo[side, spot, v] - 0.05 * (z * masks[side])
                rr[spot, v, 8 : T + 8] = (
                    n1[v, a] + ss[spot, v] - 0.05 * (smoothed(ww, spot, v) * active)
                )
                update = smoothed(rr, spot, v) * active
                last_update[v, a] = update
                new_state[v, a] = cur[v, a] - 0.05 * update

        over(NV, variable)

    for c in rim2 + far2:
        c.wait()
    second_update((2, 3))
    for c in rim + far:
        c.wait()
    second_update((0, 1))

    for c in layers + windows:
        c.wait_send()
    for unit in (1, 2, 3):
        gone(unit)


def local(n_dom, flow_state, donor_index, donor_weight, span_count):
    shape = (NV, AX, T, S)
    padded = (NV, AX, T + 16, S)
    pieces = (2, NI, NV, SLAB, S)
    turned = (AX, NV, T + 16, S)
    f32 = jnp.float32
    anywhere = pl.BlockSpec(memory_space=pl.ANY)
    vmem = pl.BlockSpec(memory_space=pltpu.VMEM)
    new_state, last_update = pl.pallas_call(
        functools.partial(kernel, n_dom, n_dom * T),
        out_shape=[jax.ShapeDtypeStruct(shape, f32)] * 2,
        in_specs=[anywhere] * 4,
        out_specs=[vmem, vmem],
        scratch_shapes=[
            pltpu.SMEM((2, T), jnp.int32),
            pltpu.SMEM((1,), jnp.int32),
            pltpu.VMEM((2, T), jnp.int32),
            pltpu.VMEM((2, T), f32),
            pltpu.VMEM(shape, f32),
            pltpu.VMEM(pieces, f32),
            pltpu.VMEM((NI, NV, SLAB, S), f32),
            pltpu.VMEM(pieces, f32),
            pltpu.VMEM(pieces, f32),
            pltpu.VMEM((AX, NV, T, S), f32),
            pltpu.VMEM(turned, f32),
            pltpu.VMEM(shape, f32),
            pltpu.VMEM(shape, f32),
            pltpu.VMEM(turned, f32),
            pltpu.VMEM(padded, f32),
            pltpu.VMEM(padded, f32),
            pltpu.VMEM((2, 3, T, S), f32),
            pltpu.VMEM((ITERS, 2, NV, 2 * T, S), f32),
            pltpu.VMEM((ITERS, 2, NV + 1, AX, S), f32),
            pltpu.VMEM((ITERS, 2, NV + 1, AX, S), f32),
            pltpu.VMEM((2, AX, NV, 2, S), f32),
            pltpu.VMEM((2, AX, NV, 2, S), f32),
            pltpu.VMEM((2, AX, NV, 2, S), f32),
            pltpu.VMEM((2, AX, NV, 2, S), f32),
            pltpu.VMEM((2, AX, NV, 4, S), f32),
            pltpu.VMEM((2, AX, NV, 4, S), f32),
            pltpu.VMEM((NI, NV, SLAB, S), f32),
            pltpu.VMEM((NI, NV, SLAB + 8, S), f32),
            pltpu.VMEM((NI, NV, SLAB + 8, S), f32),
            pltpu.VMEM((2, NV, NI, S), f32),
            pltpu.VMEM((2, NV, NI, S), f32),
            pltpu.SemaphoreType.DMA((5,)),
            pltpu.SemaphoreType.DMA((4,)),
            pltpu.SemaphoreType.DMA((4, 2)),
            pltpu.SemaphoreType.DMA,
            pltpu.SemaphoreType.DMA((22,)),
            pltpu.SemaphoreType.DMA((22,)),
        ],
        compiler_params=pltpu.CompilerParams(
            collective_id=0, has_side_effects=True, vmem_limit_bytes=52 * 1024 * 1024
        ),
        cost_estimate=pl.CostEstimate(
            flops=20_000_000, bytes_accessed=3 * PL * T * S * 4, transcendentals=0
        ),
    )(flow_state.reshape(shape), donor_index[0], donor_weight[0], span_count)
    whole = (1, NV, AX, T, S)
    return new_state.reshape(whole), last_update.reshape(whole)


def solution(mesh):
    placed = (
        P("inst", None, None, "dom", None),
        P("inst", None, "dom"),
        P("inst", None, "dom"),
        P("dom"),
    )
    return jax.shard_map(
        functools.partial(local, mesh.shape["dom"]),
        mesh=mesh,
        in_specs=placed,
        out_specs=(P("inst", None, None, "dom", None), P("inst", None, None, "dom", None)),
        check_vma=False,
    )
```

```python
import functools
import math

import jax
import jax.numpy as jnp
import numpy as np
from jax import lax
from jax.experimental import pallas as pl
from jax.experimental.pallas import tpu as pltpu
from jax.sharding import PartitionSpec as P

ITERS = 2
NI = 8
NV = 6
AX = 4
PL = NV * AX
T = 64
S = 128
ZN = 4
SLAB = T // ZN
ORDER = (1, 2, 0, 3)
MESH = pl.DeviceIdType.MESH


def spectral_row():
    k = np.arange(NI)[:, None] - np.arange(NI)[None, :]
    safe = np.where(k == 0, 1.0, np.sin(math.pi * k / NI))
    deriv = np.where(k == 0, 0.0, 0.5 * (-1.0) ** k * np.cos(math.pi * k / NI) / safe)
    return (deriv - 0.1 * deriv @ deriv)[:, 0]


def spectral_apply(x):
    row = spectral_row()
    even = [float(row[j] + row[j + 4]) / 2 for j in range(4)]
    odd = [float(row[j] - row[j + 4]) / 2 for j in range(4)]
    s = [x[z] + x[z + 4] for z in range(4)]
    d = [x[z] - x[z + 4] for z in range(4)]
    q0, q1 = s[0] - s[2], s[1] - s[3]
    s0 = even[0] * q0 + even[3] * q1
    s1 = even[1] * q0 + even[0] * q1
    sym = [s0, s1, -s0, -s1]
    out = [None] * NI
    for z in range(4):
        acc = None
        for y in range(4):
            coef = odd[z - y] if y <= z else -odd[4 + z - y]
            term = coef * d[y]
            acc = term if acc is None else acc + term
        out[z] = sym[z] + acc
        out[z + 4] = sym[z] - acc
    return out


def primitives(u):
    inv = 1.0 / u[0]
    vel = [u[1] * inv, u[2] * inv, u[3] * inv]
    nu = u[5] * inv
    pres = 0.4 * (u[4] - 0.5 * (u[1] * vel[0] + u[2] * vel[1] + u[3] * vel[2]))
    return vel, nu, pres


def centre_terms(u, vel, nu):
    return [
        0.1 * u[0],
        0.1 * u[1] + 0.02 * vel[0],
        0.1 * u[2] + 0.02 * vel[1],
        0.1 * u[3] + 0.02 * vel[2],
        0.1 * u[4],
        0.1 * u[5] + 0.02 * nu,
    ]


def half_flux(u, vel, pres, k):
    h = 0.5 * vel[k]
    f = [0.5 * u[1 + k], u[1] * h, u[2] * h, u[3] * h, (u[4] + pres) * h, u[5] * h]
    f[1 + k] = f[1 + k] + 0.5 * pres
    return f


def next_terms(u, k):
    vel, nu, pres = primitives(u)
    c = centre_terms(u, vel, nu)
    return [f - g for f, g in zip(half_flux(u, vel, pres, k), c)]


def prev_terms(u, k):
    vel, nu, pres = primitives(u)
    c = centre_terms(u, vel, nu)
    return [-(f + g) for f, g in zip(half_flux(u, vel, pres, k), c)]


def kernel(
    n_dom,
    n_cells,
    flow,
    idx,
    wgt,
    count,
    new_state,
    last_update,
    idx_s,
    count_s,
    idx_v,
    wgt_v,
    cur,
    in_u,
    in_n,
    w1,
    w2,
    ss,
    ww,
    n0,
    n1,
    rr,
    a2,
    b2,
    coef,
    win,
    edge,
    halo,
    redge,
    rhalo,
    qedge,
    qhalo,
    wedge,
    whalo,
    slab_n,
    slab_a,
    slab_b,
    slab_out,
    slab_in,
    relay,
    load_sem,
    p_send,
    p_recv,
    r_send,
    r_recv,
    d_send,
    d_recv,
):
    inst = lax.axis_index("inst")
    dom = lax.axis_index("dom")
    left = lax.rem(dom + n_dom - 1, n_dom)
    right = lax.rem(dom + 1, n_dom)

    def flip(d):
        return d + 2 - 4 * lax.rem(d // 2, 2)

    work = flip(dom)
    body, place = inst // ZN, lax.rem(inst, ZN)
    at_start = jnp.where(place == 0, 1, 0)
    at_end = jnp.where(place == ZN - 1, 1, 0)
    before = flip(lax.rem(work + n_dom - at_start, n_dom))
    beyond = flip(lax.rem(work + at_end, n_dom))
    below = (body * ZN + lax.rem(place + ZN - 1, ZN), before)
    above = (body * ZN + lax.rem(place + 1, ZN), beyond)

    loads = [
        pltpu.make_async_copy(source, target, load_sem.at[n])
        for n, (source, target) in enumerate(
            ((flow, cur), (idx, idx_s), (idx, idx_v), (wgt, wgt_v), (count, count_s))
        )
    ]
    for c in loads:
        c.start()
    barrier = pltpu.get_barrier_semaphore()
    for j in range(NI):
        pl.semaphore_signal(barrier, inc=1, device_id=(j, work), device_id_type=MESH)
    ring = [(body * ZN + lax.rem(place + dz, ZN), dom) for dz in (1, ZN - 1)]
    for device in ((inst, left), (inst, right), below, above, ring[0], ring[1]):
        pl.semaphore_signal(barrier, inc=1, device_id=device, device_id_type=MESH)

    def remote(source, target, send, recv, device):
        return pltpu.make_async_remote_copy(
            src_ref=source,
            dst_ref=target,
            send_sem=send,
            recv_sem=recv,
            device_id=device,
            device_id_type=MESH,
        )

    def source_of(unit, partner, part):
        side, slab = partner // ZN, lax.rem(partner, ZN)
        row = 1 + side if part == 0 else (AX - 1) * side
        mine = pl.ds(pl.multiple_of(SLAB * slab, SLAB), SLAB)
        if unit == 0:
            return flow.at[:, row, mine]
        if unit == 2:
            return n0.at[:, row, mine]
        return (w1 if unit == 1 else w2).at[part, partner]

    def target_of(unit, part, slot):
        spot = 2 * part + slot // ZN
        at = SLAB * lax.rem(slot, ZN)
        if unit == 0:
            return in_u.at[part, slot]
        if unit == 1:
            return ss.at[spot, :, pl.ds(pl.multiple_of(at, SLAB), SLAB)]
        if unit == 2:
            return in_n.at[slot]
        return ww.at[spot, :, pl.ds(pl.multiple_of(at + 8, 8), SLAB)]

    order = [lax.rem(inst + n, NI) for n in range(NI)]
    ahead, behind = lax.rem(place + 1, ZN), lax.rem(place + ZN - 1, ZN)

    def send(unit, part):
        for way, n in enumerate((2, 6)):
            via = order[n] // ZN * ZN + (ahead, behind)[way]
            remote(
                source_of(unit, order[n], part),
                relay.at[unit, part, way],
                p_send.at[unit],
                r_recv.at[unit, part, way],
                (via, work),
            ).start()
        for n in (0, 1, 3, 4, 5, 7):
            remote(
                source_of(unit, order[n], part),
                target_of(unit, part, inst),
                p_send.at[unit],
                p_recv.at[unit, part],
                (order[n], work),
            ).start()

    def hand_on(unit, part):
        for way, (sender, onward) in enumerate(((behind, ahead), (ahead, behind))):
            wraps = jnp.where(sender >= 2, 1, 0)
            origin = lax.rem(body + wraps + way, 2) * ZN + sender
            held = relay.at[unit, part, way]
            pltpu.make_async_copy(held, held, r_recv.at[unit, part, way]).wait()
            remote(
                held,
                target_of(unit, part, origin),
                r_send.at[unit],
                p_recv.at[unit, part],
                (body * ZN + onward, dom),
            ).start()

    def arrive(unit, part):
        spots = pl.ds(2 * part, 2)
        ref = (in_u.at[part], ss.at[spots], in_n, ww.at[spots, :, pl.ds(8, T)])[unit]
        pltpu.make_async_copy(ref, ref, p_recv.at[unit, part]).wait()

    def gone(unit):
        ref = (flow, w1, n0.at[:, 1:3], w2)[unit]
        pltpu.make_async_copy(ref, ref, p_send.at[unit]).wait()
        ref = relay.at[2, 0] if unit == 2 else relay.at[unit]
        pltpu.make_async_copy(ref, ref, r_send.at[unit]).wait()

    def near(slot, source, target, device):
        return remote(source, target, d_send.at[slot], d_recv.at[slot], (inst, device))

    def both(slot, out, back):
        return [near(slot, out(0), back(1), left), near(slot + 1, out(1), back(0), right)]

    def start(copies):
        for c in copies:
            c.start()
        return copies

    def over(n, body):
        def step(i, _):
            body(i)
            return 0

        lax.fori_loop(0, n, step, 0)

    lane = lax.broadcasted_iota(jnp.int32, (8, S), 1)
    first_lane = lane == 0
    last_lane = lane == S - 1

    def spanwise(f, c):
        out = []
        for g, h in zip(f, c):
            up, down = g - h, g + h
            after = jnp.where(last_lane, up, pltpu.roll(up, S - 1, 1))
            prior = jnp.where(first_lane, down, pltpu.roll(down, 1, 1))
            out.append(6.0 * h + (after - prior))
        return out

    def spectral(part, target, plus=None):
        def variable(v):
            for t0 in range(0, SLAB, 8):
                rows = slice(t0, t0 + 8)
                if plus is None:
                    x = [in_u[part, m, v, rows, :] for m in range(NI)]
                else:
                    x = [w1[part, m, v, rows, :] + plus(m, v, t0) for m in range(NI)]
                for m, g in enumerate(spectral_apply(x)):
                    target[part, m, v, rows, :] = g

        over(NV, variable)

    def inside(out, first_tile, last_tile):
        def tile(i, _):
            t0 = pl.multiple_of(8 * i, 8)
            total = []
            first = []
            second = []
            for a in range(AX):
                u = [cur[v, a, pl.ds(t0, 8), :] for v in range(NV)]
                vel, nu, pres = primitives(u)
                c = centre_terms(u, vel, nu)
                f1 = half_flux(u, vel, pres, 0)
                first.append([f - g for f, g in zip(f1, c)])
                second.append([f + g for f, g in zip(f1, c)])
                f2 = half_flux(u, vel, pres, 1)
                for v in range(NV):
                    a2[v, a, pl.ds(t0 + 8, 8), :] = f2[v] - c[v]
                    b2[v, a, pl.ds(t0 + 8, 8), :] = f2[v] + c[v]
                total.append(spanwise(half_flux(u, vel, pres, 2), c))
            for a in range(AX):
                for v in range(NV):
                    r = total[a][v]
                    if a == AX - 1:
                        r = r + first[a][v]
                    elif a != AX // 2 - 1:
                        r = r + first[a + 1][v]
                    if a == 0:
                        r = r - second[a][v]
                    elif a != AX // 2:
                        r = r - second[a - 1][v]
                    out[v, a, pl.ds(t0, 8), :] = r
            return 0

        lax.fori_loop(first_tile, last_tile, tile, 0)

    def around(out, it, layers):
        for c in layers:
            c.wait_recv()
        low = prev_terms([halo[it, 0, v] for v in range(NV)], 1)
        high = next_terms([halo[it, 1, v] for v in range(NV)], 1)
        for v in range(NV):
            for a in range(AX):
                b2[v, a, 7:8, :] = -low[v][a : a + 1]
                a2[v, a, T + 8 : T + 9, :] = high[v][a : a + 1]

        def variable(v):
            for a in range(AX):
                out[v, a] += a2[v, a, 9 : T + 9] - b2[v, a, 7 : T + 7]

        over(NV, variable)

    def interface(out, it, windows):
        for c in windows:
            c.wait_recv()

        def ghosts(i):
            t0 = pl.multiple_of(8 * i, 8)
            for side in range(2):
                taps = [coef[side, n, pl.ds(t0, 8), :] for n in range(3)]
                u = []
                for v in range(NV):
                    g = taps[0] * win[it, side, v, pl.ds(base[side] + t0, 8), :]
                    g = g + taps[1] * win[it, side, v, pl.ds(base[side] + t0 + 1, 8), :]
                    g = g + taps[2] * win[it, side, v, pl.ds(base[side] + t0 + 2, 8), :]
                    u.append(g)
                terms = next_terms(u, 0) if side == 0 else prev_terms(u, 0)
                for v in range(NV):
                    out[v, 1 + side, pl.ds(t0, 8), :] += terms[v]

        over(T // 8, ghosts)

    def outer_layers(it):
        for side, t in enumerate((0, T - 1)):
            for v in range(NV):
                edge[it, side, v] = cur[v, :, t, :]
            edge[it, side, NV] = jnp.broadcast_to(active, (AX, S))
        return start(
            both(10 * it, lambda side: edge.at[it, side], lambda side: halo.at[it, side])
        )

    def interface_rows(it):
        for v in range(NV):
            win[it, 0, v, 0:T] = cur[v, 2]
            win[it, 1, v, T : 2 * T] = cur[v, 1]
        return start(
            [
                near(10 * it + 2, win.at[it, 0, :, 0:T], win.at[it, 0, :, T : 2 * T], left),
                near(10 * it + 3, win.at[it, 1, :, T : 2 * T], win.at[it, 1, :, 0:T], right),
            ]
        )

    def rim_of(slot, out, back, spots):
        return start(both(slot, lambda side: out.at[side, spots], lambda side: back.at[side, spots]))

    FRONT, REST = pl.ds(0, 2), pl.ds(2, 2)

    pl.semaphore_wait(barrier, NI + 6)
    for part in range(2):
        send(0, part)
    for c in loads:
        c.wait()
    active = jnp.where(lax.broadcasted_iota(jnp.int32, (1, S), 1) < count_s[0], 1.0, 0.0)
    layers = outer_layers(0)
    windows = interface_rows(0)

    def least(t, low):
        cell = dom * T + t
        gaps = (idx_s[0, t] - cell, cell - 1 - idx_s[1, t])
        gaps = [jnp.where(g < 0, g + n_cells, g) for g in gaps]
        return jnp.minimum(low[0], gaps[0]), jnp.minimum(low[1], gaps[1])

    most = (jnp.int32(n_cells), jnp.int32(n_cells))
    offset = [jnp.clip(x, 0, T - 2) for x in lax.fori_loop(0, T, least, most)]
    base = [offset[0], T - 2 - offset[1]]
    eye = lax.broadcasted_iota(jnp.int32, (T, T), 0) == lax.broadcasted_iota(
        jnp.int32, (T, T), 1
    )
    for side in range(2):
        cell = dom * T + lax.broadcasted_iota(jnp.int32, (1, T), 1)
        row = idx_v[side : side + 1, :]
        gap = row - cell if side == 0 else cell - 1 - row
        gap = jnp.where(gap < 0, gap + n_cells, gap)
        step = jnp.where(gap > offset[side], 1.0, 0.0)
        w = wgt_v[side : side + 1, :]
        taps = [(1.0 - step) * w, step * w + (1.0 - step) * (1.0 - w), step * (1.0 - w)]
        if side == 1:
            taps = [step * w, (1.0 - step) * w + step * (1.0 - w), (1.0 - step) * (1.0 - w)]
        for i, tap in enumerate(taps):
            column = jnp.sum(jnp.where(eye, tap, 0.0), axis=1, keepdims=True)
            coef[side, i] = jnp.broadcast_to(column, (T, S))

    half = T // 16
    hand_on(0, 0)
    inside(n0, 0, half)
    hand_on(0, 1)
    arrive(0, 0)
    spectral(0, w1)
    send(1, 0)
    arrive(0, 1)
    for v in range(NV):
        slab_out[0, v] = in_u[1, :, v, 0, :]
        slab_out[1, v] = in_u[1, :, v, SLAB - 1, :]
    slabs = start(
        [
            remote(slab_out.at[0], slab_in.at[1], d_send.at[18], d_recv.at[18], below),
            remote(slab_out.at[1], slab_in.at[0], d_send.at[19], d_recv.at[19], above),
        ]
    )
    spectral(1, w1)
    send(1, 1)
    hand_on(1, 0)
    inside(n0, half, 2 * half)
    around(n0, 0, layers)
    hand_on(1, 1)
    interface(n0, 0, windows)
    send(2, 0)

    toward = jnp.where(body == 0, 1.0, -1.0)

    def slab_inside(m):
        for t0 in range(0, SLAB, 8):
            rows = slice(t0, t0 + 8)
            u = [in_u[0, m, v, rows, :] for v in range(NV)]
            vel, nu, pres = primitives(u)
            c1 = centre_terms(u, vel, nu)
            f1 = half_flux(u, vel, pres, 0)
            u = [in_u[1, m, v, rows, :] for v in range(NV)]
            vel, nu, pres = primitives(u)
            c = centre_terms(u, vel, nu)
            f = half_flux(u, vel, pres, 0)
            f2 = half_flux(u, vel, pres, 1)
            r = spanwise(half_flux(u, vel, pres, 2), c)
            for v in range(NV):
                slab_a[m, v, t0 : t0 + 8, :] = f2[v] - c[v]
                slab_b[m, v, t0 + 8 : t0 + 16, :] = f2[v] + c[v]
                slab_n[m, v, rows, :] = r[v] + (toward * (f1[v] - f[v]) - (c1[v] + c[v]))

    over(NI, slab_inside)
    hand_on(2, 0)
    for c in slabs:
        c.wait()
    low = prev_terms([slab_in[0, v] for v in range(NV)], 1)
    high = next_terms([slab_in[1, v] for v in range(NV)], 1)
    for v in range(NV):
        slab_b[:, v, 7, :] = -low[v]
        slab_a[:, v, SLAB, :] = high[v]

    def outer(m, v, t0):
        return slab_n[m, v, t0 : t0 + 8, :] + (
            slab_a[m, v, t0 + 1 : t0 + 9, :] - slab_b[m, v, t0 + 7 : t0 + 15, :]
        )

    spectral(1, w2, outer)

    def keep_rows(out, spots, value):
        n = out.shape[3]
        for spot in spots:
            for v in range(NV):
                out[0, spot, v] = value(spot, v, 0, n)
                out[1, spot, v] = value(spot, v, T - n, T)

    def put_rows(back, spots):
        for spot in spots:
            for v in range(NV):
                rr[spot, v, 6:8, :] = back[0, spot, v]
                rr[spot, v, T + 8 : T + 10, :] = back[1, spot, v]

    def smoothed(ref, spot, v):
        return (
            0.625 * ref[spot, v, 8 : T + 8]
            + 0.125 * (ref[spot, v, 7 : T + 7] + ref[spot, v, 9 : T + 9])
            + 0.0625 * (ref[spot, v, 6 : T + 6] + ref[spot, v, 10 : T + 10])
        )

    def sums(spots):
        def variable(v):
            for spot in spots:
                rr[spot, v, 8 : T + 8] = n0[v, ORDER[spot]] + ss[spot, v]

        over(NV, variable)

    def first_update(spots):
        def variable(v):
            for spot in spots:
                a = ORDER[spot]
                cur[v, a] = cur[v, a] - 0.05 * (smoothed(rr, spot, v) * active)

        over(NV, variable)

    def first_sum(spot, v, t0, t1):
        return n0[v, ORDER[spot], t0:t1, :] + ss[spot, v, t0:t1, :]

    arrive(1, 0)
    keep_rows(redge, (0, 1), first_sum)
    rim = rim_of(4, redge, rhalo, FRONT)
    sums((0, 1))
    arrive(1, 1)
    keep_rows(redge, (2, 3), first_sum)
    rim2 = rim_of(6, redge, rhalo, REST)
    for c in rim:
        c.wait()
    put_rows(rhalo, (0, 1))
    gone(0)
    for c in layers + windows:
        c.wait_send()
    first_update((0, 1))
    windows = interface_rows(1)
    send(3, 1)
    sums((2, 3))
    for c in rim2:
        c.wait()
    put_rows(rhalo, (2, 3))
    first_update((2, 3))
    layers = outer_layers(1)
    hand_on(3, 1)

    arrive(2, 0)
    spectral(0, w2, lambda m, v, t0: in_n[m, v, t0 : t0 + 8, :])
    send(3, 0)
    inside(n1, 0, half)
    hand_on(3, 0)
    inside(n1, half, 2 * half)
    around(n1, 1, layers)

    def second_sum(spot, v, t0, t1):
        return n1[v, ORDER[spot], t0:t1, :] + ss[spot, v, t0:t1, :]

    keep_rows(qedge, (2, 3), second_sum)
    rim2 = rim_of(8, qedge, qhalo, REST)
    interface(n1, 1, windows)
    keep_rows(qedge, (0, 1), second_sum)
    rim = rim_of(12 + 2, qedge, qhalo, FRONT)

    def last_source(spot, v, t0, t1):
        return ww[spot, v, 8 + t0 : 8 + t1, :]

    arrive(3, 1)
    keep_rows(wedge, (2, 3), last_source)
    far2 = rim_of(16, wedge, whalo, REST)
    arrive(3, 0)
    keep_rows(wedge, (0, 1), last_source)
    far = rim_of(20, wedge, whalo, FRONT)

    masks = [halo[0, side, NV, 0:1, :] for side in range(2)]

    def second_update(spots):
        def variable(v):
            for spot in spots:
                a = ORDER[spot]
                ww[spot, v, 4:8, :] = whalo[0, spot, v]
                ww[spot, v, T + 8 : T + 12, :] = whalo[1, spot, v]
                for side, t in enumerate((6, T + 8)):
                    z = (
                        0.625 * ww[spot, v, t : t + 2, :]
                        + 0.125 * (ww[spot, v, t - 1 : t + 1, :] + ww[spot, v, t + 1 : t + 3, :])
                        + 0.0625 * (ww[spot, v, t - 2 : t, :] + ww[spot, v, t + 2 : t + 4, :])
                    )
                    rr[spot, v, t : t + 2, :] = qhalo[side, spot, v] - 0.05 * (z * masks[side])
                rr[spot, v, 8 : T + 8] = (
                    n1[v, a] + ss[spot, v] - 0.05 * (smoothed(ww, spot, v) * active)
                )
                update = smoothed(rr, spot, v) * active
                last_update[v, a] = update
                new_state[v, a] = cur[v, a] - 0.05 * update

        over(NV, variable)

    for c in rim2 + far2:
        c.wait()
    second_update((2, 3))
    for c in rim + far:
        c.wait()
    second_update((0, 1))

    for c in layers + windows:
        c.wait_send()
    for unit in (1, 2, 3):
        gone(unit)


def local(n_dom, flow_state, donor_index, donor_weight, span_count):
    shape = (NV, AX, T, S)
    padded = (NV, AX, T + 16, S)
    pieces = (2, NI, NV, SLAB, S)
    turned = (AX, NV, T + 16, S)
    f32 = jnp.float32
    anywhere = pl.BlockSpec(memory_space=pl.ANY)
    vmem = pl.BlockSpec(memory_space=pltpu.VMEM)
    new_state, last_update = pl.pallas_call(
        functools.partial(kernel, n_dom, n_dom * T),
        out_shape=[jax.ShapeDtypeStruct(shape, f32)] * 2,
        in_specs=[anywhere] * 4,
        out_specs=[vmem, vmem],
        scratch_shapes=[
            pltpu.SMEM((2, T), jnp.int32),
            pltpu.SMEM((1,), jnp.int32),
            pltpu.VMEM((2, T), jnp.int32),
            pltpu.VMEM((2, T), f32),
            pltpu.VMEM(shape, f32),
            pltpu.VMEM(pieces, f32),
            pltpu.VMEM((NI, NV, SLAB, S), f32),
            pltpu.VMEM(pieces, f32),
            pltpu.VMEM(pieces, f32),
            pltpu.VMEM((AX, NV, T, S), f32),
            pltpu.VMEM(turned, f32),
            pltpu.VMEM(shape, f32),
            pltpu.VMEM(shape, f32),
            pltpu.VMEM(turned, f32),
            pltpu.VMEM(padded, f32),
            pltpu.VMEM(padded, f32),
            pltpu.VMEM((2, 3, T, S), f32),
            pltpu.VMEM((ITERS, 2, NV, 2 * T, S), f32),
            pltpu.VMEM((ITERS, 2, NV + 1, AX, S), f32),
            pltpu.VMEM((ITERS, 2, NV + 1, AX, S), f32),
            pltpu.VMEM((2, AX, NV, 2, S), f32),
            pltpu.VMEM((2, AX, NV, 2, S), f32),
            pltpu.VMEM((2, AX, NV, 2, S), f32),
            pltpu.VMEM((2, AX, NV, 2, S), f32),
            pltpu.VMEM((2, AX, NV, 4, S), f32),
            pltpu.VMEM((2, AX, NV, 4, S), f32),
            pltpu.VMEM((NI, NV, SLAB, S), f32),
            pltpu.VMEM((NI, NV, SLAB + 8, S), f32),
            pltpu.VMEM((NI, NV, SLAB + 8, S), f32),
            pltpu.VMEM((2, NV, NI, S), f32),
            pltpu.VMEM((2, NV, NI, S), f32),
            pltpu.VMEM((4, 2, 2, NV, SLAB, S), f32),
            pltpu.SemaphoreType.DMA((5,)),
            pltpu.SemaphoreType.DMA((4,)),
            pltpu.SemaphoreType.DMA((4, 2)),
            pltpu.SemaphoreType.DMA((4,)),
            pltpu.SemaphoreType.DMA((4, 2, 2)),
            pltpu.SemaphoreType.DMA((22,)),
            pltpu.SemaphoreType.DMA((22,)),
        ],
        compiler_params=pltpu.CompilerParams(
            collective_id=0, has_side_effects=True, vmem_limit_bytes=52 * 1024 * 1024
        ),
        cost_estimate=pl.CostEstimate(
            flops=20_000_000, bytes_accessed=3 * PL * T * S * 4, transcendentals=0
        ),
    )(flow_state.reshape(shape), donor_index[0], donor_weight[0], span_count)
    whole = (1, NV, AX, T, S)
    return new_state.reshape(whole), last_update.reshape(whole)


def solution(mesh):
    placed = (
        P("inst", None, None, "dom", None),
        P("inst", None, "dom"),
        P("inst", None, "dom"),
        P("dom"),
    )
    return jax.shard_map(
        functools.partial(local, mesh.shape["dom"]),
        mesh=mesh,
        in_specs=placed,
        out_specs=(P("inst", None, None, "dom", None), P("inst", None, None, "dom", None)),
        check_vma=False,
    )
```

```python
import functools
import math

import jax
import jax.numpy as jnp
import numpy as np
from jax import lax
from jax.experimental import pallas as pl
from jax.experimental.pallas import tpu as pltpu
from jax.sharding import PartitionSpec as P

ITERS = 2
NI = 8
NV = 6
AX = 4
PL = NV * AX
T = 64
S = 128
ZN = 4
SLAB = T // ZN
ORDER = (1, 2, 0, 3)
MESH = pl.DeviceIdType.MESH


def spectral_row():
    k = np.arange(NI)[:, None] - np.arange(NI)[None, :]
    safe = np.where(k == 0, 1.0, np.sin(math.pi * k / NI))
    deriv = np.where(k == 0, 0.0, 0.5 * (-1.0) ** k * np.cos(math.pi * k / NI) / safe)
    return (deriv - 0.1 * deriv @ deriv)[:, 0]


def spectral_apply(x):
    row = spectral_row()
    even = [float(row[j] + row[j + 4]) / 2 for j in range(4)]
    odd = [float(row[j] - row[j + 4]) / 2 for j in range(4)]
    s = [x[z] + x[z + 4] for z in range(4)]
    d = [x[z] - x[z + 4] for z in range(4)]
    q0, q1 = s[0] - s[2], s[1] - s[3]
    s0 = even[0] * q0 + even[3] * q1
    s1 = even[1] * q0 + even[0] * q1
    sym = [s0, s1, -s0, -s1]
    out = [None] * NI
    for z in range(4):
        acc = None
        for y in range(4):
            coef = odd[z - y] if y <= z else -odd[4 + z - y]
            term = coef * d[y]
            acc = term if acc is None else acc + term
        out[z] = sym[z] + acc
        out[z + 4] = sym[z] - acc
    return out


def primitives(u):
    inv = 1.0 / u[0]
    vel = [u[1] * inv, u[2] * inv, u[3] * inv]
    nu = u[5] * inv
    pres = 0.4 * (u[4] - 0.5 * (u[1] * vel[0] + u[2] * vel[1] + u[3] * vel[2]))
    return vel, nu, pres


def centre_terms(u, vel, nu):
    return [
        0.1 * u[0],
        0.1 * u[1] + 0.02 * vel[0],
        0.1 * u[2] + 0.02 * vel[1],
        0.1 * u[3] + 0.02 * vel[2],
        0.1 * u[4],
        0.1 * u[5] + 0.02 * nu,
    ]


def half_flux(u, vel, pres, k):
    h = 0.5 * vel[k]
    f = [0.5 * u[1 + k], u[1] * h, u[2] * h, u[3] * h, (u[4] + pres) * h, u[5] * h]
    f[1 + k] = f[1 + k] + 0.5 * pres
    return f


def next_terms(u, k):
    vel, nu, pres = primitives(u)
    c = centre_terms(u, vel, nu)
    return [f - g for f, g in zip(half_flux(u, vel, pres, k), c)]


def prev_terms(u, k):
    vel, nu, pres = primitives(u)
    c = centre_terms(u, vel, nu)
    return [-(f + g) for f, g in zip(half_flux(u, vel, pres, k), c)]


def kernel(
    n_dom,
    n_cells,
    flow,
    idx,
    wgt,
    count,
    new_state,
    last_update,
    idx_s,
    count_s,
    idx_v,
    wgt_v,
    cur,
    in_u,
    in_n,
    w1,
    w2,
    ss,
    ww,
    n0,
    n1,
    rr,
    a2,
    b2,
    coef,
    win,
    edge,
    halo,
    redge,
    rhalo,
    qedge,
    qhalo,
    wedge,
    whalo,
    slab_n,
    slab_a,
    slab_b,
    slab_out,
    slab_in,
    load_sem,
    p_send,
    p_recv,
    d_send,
    d_recv,
):
    inst = lax.axis_index("inst")
    dom = lax.axis_index("dom")
    left = lax.rem(dom + n_dom - 1, n_dom)
    right = lax.rem(dom + 1, n_dom)

    def flip(d):
        return d + 2 - 4 * lax.rem(d // 2, 2)

    work = flip(dom)
    body, place = inst // ZN, lax.rem(inst, ZN)
    at_start = jnp.where(place == 0, 1, 0)
    at_end = jnp.where(place == ZN - 1, 1, 0)
    before = flip(lax.rem(work + n_dom - at_start, n_dom))
    beyond = flip(lax.rem(work + at_end, n_dom))
    below = (body * ZN + lax.rem(place + ZN - 1, ZN), before)
    above = (body * ZN + lax.rem(place + 1, ZN), beyond)

    loads = [
        pltpu.make_async_copy(source, target, load_sem.at[n])
        for n, (source, target) in enumerate(
            ((flow, cur), (idx, idx_s), (idx, idx_v), (wgt, wgt_v), (count, count_s))
        )
    ]
    for c in loads:
        c.start()
    barrier = pltpu.get_barrier_semaphore()
    for j in range(NI):
        pl.semaphore_signal(barrier, inc=1, device_id=(j, work), device_id_type=MESH)
    for device in ((inst, left), (inst, right), below, above):
        pl.semaphore_signal(barrier, inc=1, device_id=device, device_id_type=MESH)

    def remote(source, target, send, recv, device):
        return pltpu.make_async_remote_copy(
            src_ref=source,
            dst_ref=target,
            send_sem=send,
            recv_sem=recv,
            device_id=device,
            device_id_type=MESH,
        )

    def piece(unit, partner, part, slot):
        side, slab = partner // ZN, lax.rem(partner, ZN)
        row = 1 + side if part == 0 else (AX - 1) * side
        mine = pl.ds(pl.multiple_of(SLAB * slab, SLAB), SLAB)
        spot = 2 * part + slot // ZN
        at = SLAB * lax.rem(slot, ZN)
        if unit == 0:
            source, target = flow.at[:, row, mine], in_u.at[part, slot]
        elif unit == 1:
            source = w1.at[part, partner]
            target = ss.at[spot, :, pl.ds(pl.multiple_of(at, SLAB), SLAB)]
        elif unit == 2:
            source, target = n0.at[:, row, mine], in_n.at[slot]
        else:
            source = w2.at[part, partner]
            target = ww.at[spot, :, pl.ds(pl.multiple_of(at + 8, 8), SLAB)]
        return remote(source, target, p_send.at[unit], p_recv.at[unit, part], (partner, work))

    order = [lax.rem(inst + n, NI) for n in range(NI)]

    def send(unit, part):
        for j in order:
            piece(unit, j, part, inst).start()

    def arrive(unit, part):
        spots = pl.ds(2 * part, 2)
        ref = (in_u.at[part], ss.at[spots], in_n, ww.at[spots, :, pl.ds(8, T)])[unit]
        pltpu.make_async_copy(ref, ref, p_recv.at[unit, part]).wait()

    def gone(unit):
        ref = (flow, w1, n0.at[:, 1:3], w2)[unit]
        pltpu.make_async_copy(ref, ref, p_send.at[unit]).wait()

    def near(slot, source, target, device):
        return remote(source, target, d_send.at[slot], d_recv.at[slot], (inst, device))

    def both(slot, out, back):
        return [near(slot, out(0), back(1), left), near(slot + 1, out(1), back(0), right)]

    def start(copies):
        for c in copies:
            c.start()
        return copies

    def over(n, body):
        def step(i, _):
            body(i)
            return 0

        lax.fori_loop(0, n, step, 0)

    lane = lax.broadcasted_iota(jnp.int32, (8, S), 1)
    first_lane = lane == 0
    last_lane = lane == S - 1

    def spanwise(f, c):
        out = []
        for g, h in zip(f, c):
            up, down = g - h, g + h
            after = jnp.where(last_lane, up, pltpu.roll(up, S - 1, 1))
            prior = jnp.where(first_lane, down, pltpu.roll(down, 1, 1))
            out.append(6.0 * h + (after - prior))
        return out

    def spectral(part, target, plus=None):
        def variable(v):
            for t0 in range(0, SLAB, 8):
                rows = slice(t0, t0 + 8)
                if plus is None:
                    x = [in_u[part, m, v, rows, :] for m in range(NI)]
                else:
                    x = [w1[part, m, v, rows, :] + plus(m, v, t0) for m in range(NI)]
                for m, g in enumerate(spectral_apply(x)):
                    target[part, m, v, rows, :] = g

        over(NV, variable)

    def inside(out, first_tile, last_tile):
        def tile(i, _):
            t0 = pl.multiple_of(8 * i, 8)
            total = []
            first = []
            second = []
            for a in range(AX):
                u = [cur[v, a, pl.ds(t0, 8), :] for v in range(NV)]
                vel, nu, pres = primitives(u)
                c = centre_terms(u, vel, nu)
                f1 = half_flux(u, vel, pres, 0)
                first.append([f - g for f, g in zip(f1, c)])
                second.append([f + g for f, g in zip(f1, c)])
                f2 = half_flux(u, vel, pres, 1)
                for v in range(NV):
                    a2[v, a, pl.ds(t0 + 8, 8), :] = f2[v] - c[v]
                    b2[v, a, pl.ds(t0 + 8, 8), :] = f2[v] + c[v]
                total.append(spanwise(half_flux(u, vel, pres, 2), c))
            for a in range(AX):
                for v in range(NV):
                    r = total[a][v]
                    if a == AX - 1:
                        r = r + first[a][v]
                    elif a != AX // 2 - 1:
                        r = r + first[a + 1][v]
                    if a == 0:
                        r = r - second[a][v]
                    elif a != AX // 2:
                        r = r - second[a - 1][v]
                    out[v, a, pl.ds(t0, 8), :] = r
            return 0

        lax.fori_loop(first_tile, last_tile, tile, 0)

    def around(out, it, layers):
        for c in layers:
            c.wait_recv()
        low = prev_terms([halo[it, 0, v] for v in range(NV)], 1)
        high = next_terms([halo[it, 1, v] for v in range(NV)], 1)
        for v in range(NV):
            for a in range(AX):
                b2[v, a, 7:8, :] = -low[v][a : a + 1]
                a2[v, a, T + 8 : T + 9, :] = high[v][a : a + 1]

        def variable(v):
            for a in range(AX):
                out[v, a] += a2[v, a, 9 : T + 9] - b2[v, a, 7 : T + 7]

        over(NV, variable)

    def interface(out, it, tiles):
        def ghosts(n):
            i = tiles[0] + n * tiles[2]
            t0 = pl.multiple_of(8 * i, 8)
            for side in range(2):
                taps = [coef[side, n, pl.ds(t0, 8), :] for n in range(3)]
                u = []
                for v in range(NV):
                    g = taps[0] * win[it, side, v, pl.ds(base[side] + t0, 8), :]
                    g = g + taps[1] * win[it, side, v, pl.ds(base[side] + t0 + 1, 8), :]
                    g = g + taps[2] * win[it, side, v, pl.ds(base[side] + t0 + 2, 8), :]
                    u.append(g)
                terms = next_terms(u, 0) if side == 0 else prev_terms(u, 0)
                for v in range(NV):
                    out[v, 1 + side, pl.ds(t0, 8), :] += terms[v]

        over(tiles[1], ghosts)

    def outer_layers(it):
        for side, t in enumerate((0, T - 1)):
            for v in range(NV):
                edge[it, side, v] = cur[v, :, t, :]
            edge[it, side, NV] = jnp.broadcast_to(active, (AX, S))
        return start(
            both(10 * it, lambda side: edge.at[it, side], lambda side: halo.at[it, side])
        )

    def interface_rows(it):
        for v in range(NV):
            win[it, 0, v, 0:T] = cur[v, 2]
            win[it, 1, v, T : 2 * T] = cur[v, 1]
        return start(
            [
                near(10 * it + 2, win.at[it, 0, :, 0:T], win.at[it, 0, :, T : 2 * T], left),
                near(10 * it + 3, win.at[it, 1, :, T : 2 * T], win.at[it, 1, :, 0:T], right),
            ]
        )

    def rim_of(slot, out, back, spots):
        return start(
            both(slot, lambda side: out.at[side, :, spots], lambda side: back.at[side, :, spots])
        )

    FRONT, REST = pl.ds(0, 2), pl.ds(2, 2)

    pl.semaphore_wait(barrier, NI + 4)
    for part in range(2):
        send(0, part)
    for c in loads:
        c.wait()
    active = jnp.where(lax.broadcasted_iota(jnp.int32, (1, S), 1) < count_s[0], 1.0, 0.0)
    layers = outer_layers(0)
    windows = interface_rows(0)

    def least(t, low):
        cell = dom * T + t
        gaps = (idx_s[0, t] - cell, cell - 1 - idx_s[1, t])
        gaps = [jnp.where(g < 0, g + n_cells, g) for g in gaps]
        return jnp.minimum(low[0], gaps[0]), jnp.minimum(low[1], gaps[1])

    most = (jnp.int32(n_cells), jnp.int32(n_cells))
    offset = [jnp.clip(x, 0, T - 2) for x in lax.fori_loop(0, T, least, most)]
    base = [offset[0], T - 2 - offset[1]]
    eye = lax.broadcasted_iota(jnp.int32, (T, T), 0) == lax.broadcasted_iota(
        jnp.int32, (T, T), 1
    )
    for side in range(2):
        cell = dom * T + lax.broadcasted_iota(jnp.int32, (1, T), 1)
        row = idx_v[side : side + 1, :]
        gap = row - cell if side == 0 else cell - 1 - row
        gap = jnp.where(gap < 0, gap + n_cells, gap)
        step = jnp.where(gap > offset[side], 1.0, 0.0)
        w = wgt_v[side : side + 1, :]
        taps = [(1.0 - step) * w, step * w + (1.0 - step) * (1.0 - w), step * (1.0 - w)]
        if side == 1:
            taps = [step * w, (1.0 - step) * w + step * (1.0 - w), (1.0 - step) * (1.0 - w)]
        for i, tap in enumerate(taps):
            column = jnp.sum(jnp.where(eye, tap, 0.0), axis=1, keepdims=True)
            coef[side, i] = jnp.broadcast_to(column, (T, S))

    half = T // 16
    arrive(0, 0)
    spectral(0, w1)
    send(1, 0)
    inside(n0, 0, half)
    arrive(0, 1)
    spectral(1, w1)
    send(1, 1)
    for v in range(NV):
        slab_out[0, v] = in_u[1, :, v, 0, :]
        slab_out[1, v] = in_u[1, :, v, SLAB - 1, :]
    slabs = start(
        [
            remote(slab_out.at[0], slab_in.at[1], d_send.at[18], d_recv.at[18], below),
            remote(slab_out.at[1], slab_in.at[0], d_send.at[19], d_recv.at[19], above),
        ]
    )
    inside(n0, half, 2 * half)
    around(n0, 0, layers)
    for c in windows:
        c.wait_recv()
    interface(n0, 0, (0, T // 8, 1))
    send(2, 0)

    toward = jnp.where(body == 0, 1.0, -1.0)

    def slab_inside(m):
        for t0 in range(0, SLAB, 8):
            rows = slice(t0, t0 + 8)
            u = [in_u[0, m, v, rows, :] for v in range(NV)]
            vel, nu, pres = primitives(u)
            c1 = centre_terms(u, vel, nu)
            f1 = half_flux(u, vel, pres, 0)
            u = [in_u[1, m, v, rows, :] for v in range(NV)]
            vel, nu, pres = primitives(u)
            c = centre_terms(u, vel, nu)
            f = half_flux(u, vel, pres, 0)
            f2 = half_flux(u, vel, pres, 1)
            r = spanwise(half_flux(u, vel, pres, 2), c)
            for v in range(NV):
                slab_a[m, v, t0 : t0 + 8, :] = f2[v] - c[v]
                slab_b[m, v, t0 + 8 : t0 + 16, :] = f2[v] + c[v]
                slab_n[m, v, rows, :] = r[v] + (toward * (f1[v] - f[v]) - (c1[v] + c[v]))

    over(NI, slab_inside)
    for c in slabs:
        c.wait()
    low = prev_terms([slab_in[0, v] for v in range(NV)], 1)
    high = next_terms([slab_in[1, v] for v in range(NV)], 1)
    for v in range(NV):
        slab_b[:, v, 7, :] = -low[v]
        slab_a[:, v, SLAB, :] = high[v]

    def outer(m, v, t0):
        return slab_n[m, v, t0 : t0 + 8, :] + (
            slab_a[m, v, t0 + 1 : t0 + 9, :] - slab_b[m, v, t0 + 7 : t0 + 15, :]
        )

    spectral(1, w2, outer)

    def keep_rows(out, spots, times, value):
        for spot in spots:
            for n, t in enumerate(times):
                out[n // (len(times) // 2), n % (len(times) // 2), spot] = value(spot, t)

    def put_rows(back, spots, times):
        for spot in spots:
            for n, t in enumerate(times):
                rr[spot, :, 8 + t, :] = back[n // 2, n % 2, spot]

    ends = (0, 1, T - 2, T - 1)
    outside = (-2, -1, T, T + 1)

    def smoothed(ref, spot, v):
        return (
            0.625 * ref[spot, v, 8 : T + 8]
            + 0.125 * (ref[spot, v, 7 : T + 7] + ref[spot, v, 9 : T + 9])
            + 0.0625 * (ref[spot, v, 6 : T + 6] + ref[spot, v, 10 : T + 10])
        )

    def sums(spots):
        def variable(v):
            for spot in spots:
                rr[spot, v, 8 : T + 8] = n0[v, ORDER[spot]] + ss[spot, v]

        over(NV, variable)

    def first_update(spots):
        def variable(v):
            for spot in spots:
                a = ORDER[spot]
                cur[v, a] = cur[v, a] - 0.05 * (smoothed(rr, spot, v) * active)

        over(NV, variable)

    def first_sum(spot, t):
        return n0[:, ORDER[spot], t, :] + ss[spot, :, t, :]

    arrive(1, 0)
    keep_rows(redge, (0, 1), ends, first_sum)
    rim = rim_of(4, redge, rhalo, FRONT)
    sums((0, 1))
    arrive(1, 1)
    keep_rows(redge, (2, 3), ends, first_sum)
    rim2 = rim_of(6, redge, rhalo, REST)
    for c in rim:
        c.wait()
    put_rows(rhalo, (0, 1), outside)
    gone(0)
    for c in layers + windows:
        c.wait_send()
    first_update((0, 1))
    windows = interface_rows(1)
    send(3, 1)
    sums((2, 3))
    for c in rim2:
        c.wait()
    put_rows(rhalo, (2, 3), outside)
    first_update((2, 3))
    layers = outer_layers(1)

    arrive(2, 0)
    spectral(0, w2, lambda m, v, t0: in_n[m, v, t0 : t0 + 8, :])
    send(3, 0)
    inside(n1, 0, 2 * half)
    around(n1, 1, layers)

    def second_sum(spot, t):
        return n1[:, ORDER[spot], t, :] + ss[spot, :, t, :]

    keep_rows(qedge, (2, 3), ends, second_sum)
    rim2 = rim_of(8, qedge, qhalo, REST)
    for c in windows:
        c.wait_recv()
    interface(n1, 1, (0, 2, T // 8 - 1))
    keep_rows(qedge, (0, 1), ends, second_sum)
    rim = rim_of(12 + 2, qedge, qhalo, FRONT)
    interface(n1, 1, (1, T // 8 - 2, 1))

    far_rows = (0, 1, 2, 3, T - 4, T - 3, T - 2, T - 1)

    def last_source(spot, t):
        return ww[spot, :, 8 + t, :]

    arrive(3, 1)
    keep_rows(wedge, (2, 3), far_rows, last_source)
    far2 = rim_of(16, wedge, whalo, REST)
    arrive(3, 0)
    keep_rows(wedge, (0, 1), far_rows, last_source)
    far = rim_of(20, wedge, whalo, FRONT)

    def second_update(spots):
        for spot in spots:
            for n in range(2):
                ww[spot, :, 6 + n, :] = whalo[0, 2 + n, spot]
                ww[spot, :, T + 8 + n, :] = whalo[1, n, spot]
            for side in range(2):
                h = [whalo[side, n, spot] for n in range(4)]
                e = [wedge[side, n, spot] for n in range(4)]
                line = h + e[:2] if side == 0 else e[2:] + h
                mask = halo[0, side, NV, 0:1, :]
                for n in range(2):
                    x = line[n : n + 5]
                    z = 0.625 * x[2] + 0.125 * (x[1] + x[3]) + 0.0625 * (x[0] + x[4])
                    t = n - 2 if side == 0 else T + n
                    rr[spot, :, 8 + t, :] = qhalo[side, n, spot] - 0.05 * (z * mask)

        def variable(v):
            for spot in spots:
                a = ORDER[spot]
                rr[spot, v, 8 : T + 8] = (
                    n1[v, a] + ss[spot, v] - 0.05 * (smoothed(ww, spot, v) * active)
                )
                update = smoothed(rr, spot, v) * active
                last_update[v, a] = update
                new_state[v, a] = cur[v, a] - 0.05 * update

        over(NV, variable)

    for c in rim2 + far2:
        c.wait()
    second_update((2, 3))
    for c in rim + far:
        c.wait()
    second_update((0, 1))

    for c in layers + windows:
        c.wait_send()
    for unit in (1, 2, 3):
        gone(unit)


def local(n_dom, flow_state, donor_index, donor_weight, span_count):
    shape = (NV, AX, T, S)
    padded = (NV, AX, T + 16, S)
    pieces = (2, NI, NV, SLAB, S)
    turned = (AX, NV, T + 16, S)
    f32 = jnp.float32
    anywhere = pl.BlockSpec(memory_space=pl.ANY)
    vmem = pl.BlockSpec(memory_space=pltpu.VMEM)
    new_state, last_update = pl.pallas_call(
        functools.partial(kernel, n_dom, n_dom * T),
        out_shape=[jax.ShapeDtypeStruct(shape, f32)] * 2,
        in_specs=[anywhere] * 4,
        out_specs=[vmem, vmem],
        scratch_shapes=[
            pltpu.SMEM((2, T), jnp.int32),
            pltpu.SMEM((1,), jnp.int32),
            pltpu.VMEM((2, T), jnp.int32),
            pltpu.VMEM((2, T), f32),
            pltpu.VMEM(shape, f32),
            pltpu.VMEM(pieces, f32),
            pltpu.VMEM((NI, NV, SLAB, S), f32),
            pltpu.VMEM(pieces, f32),
            pltpu.VMEM(pieces, f32),
            pltpu.VMEM((AX, NV, T, S), f32),
            pltpu.VMEM(turned, f32),
            pltpu.VMEM(shape, f32),
            pltpu.VMEM(shape, f32),
            pltpu.VMEM(turned, f32),
            pltpu.VMEM(padded, f32),
            pltpu.VMEM(padded, f32),
            pltpu.VMEM((2, 3, T, S), f32),
            pltpu.VMEM((ITERS, 2, NV, 2 * T, S), f32),
            pltpu.VMEM((ITERS, 2, NV + 1, AX, S), f32),
            pltpu.VMEM((ITERS, 2, NV + 1, AX, S), f32),
            pltpu.VMEM((2, 2, AX, NV, S), f32),
            pltpu.VMEM((2, 2, AX, NV, S), f32),
            pltpu.VMEM((2, 2, AX, NV, S), f32),
            pltpu.VMEM((2, 2, AX, NV, S), f32),
            pltpu.VMEM((2, 4, AX, NV, S), f32),
            pltpu.VMEM((2, 4, AX, NV, S), f32),
            pltpu.VMEM((NI, NV, SLAB, S), f32),
            pltpu.VMEM((NI, NV, SLAB + 8, S), f32),
            pltpu.VMEM((NI, NV, SLAB + 8, S), f32),
            pltpu.VMEM((2, NV, NI, S), f32),
            pltpu.VMEM((2, NV, NI, S), f32),
            pltpu.SemaphoreType.DMA((5,)),
            pltpu.SemaphoreType.DMA((4,)),
            pltpu.SemaphoreType.DMA((4, 2)),
            pltpu.SemaphoreType.DMA((22,)),
            pltpu.SemaphoreType.DMA((22,)),
        ],
        compiler_params=pltpu.CompilerParams(
            collective_id=0, has_side_effects=True, vmem_limit_bytes=52 * 1024 * 1024
        ),
        cost_estimate=pl.CostEstimate(
            flops=20_000_000, bytes_accessed=3 * PL * T * S * 4, transcendentals=0
        ),
    )(flow_state.reshape(shape), donor_index[0], donor_weight[0], span_count)
    whole = (1, NV, AX, T, S)
    return new_state.reshape(whole), last_update.reshape(whole)


def solution(mesh):
    placed = (
        P("inst", None, None, "dom", None),
        P("inst", None, "dom"),
        P("inst", None, "dom"),
        P("dom"),
    )
    return jax.shard_map(
        functools.partial(local, mesh.shape["dom"]),
        mesh=mesh,
        in_specs=placed,
        out_specs=(P("inst", None, None, "dom", None), P("inst", None, None, "dom", None)),
        check_vma=False,
    )
```

```python
import functools
import math

import jax
import jax.numpy as jnp
import numpy as np
from jax import lax
from jax.experimental import pallas as pl
from jax.experimental.pallas import tpu as pltpu
from jax.sharding import PartitionSpec as P

ITERS = 2
NI = 8
NV = 6
AX = 4
PL = NV * AX
T = 64
S = 128
ZN = 4
SLAB = T // ZN
ORDER = (1, 2, 0, 3)
MESH = pl.DeviceIdType.MESH


def spectral_row():
    k = np.arange(NI)[:, None] - np.arange(NI)[None, :]
    safe = np.where(k == 0, 1.0, np.sin(math.pi * k / NI))
    deriv = np.where(k == 0, 0.0, 0.5 * (-1.0) ** k * np.cos(math.pi * k / NI) / safe)
    return (deriv - 0.1 * deriv @ deriv)[:, 0]


def spectral_apply(x):
    row = spectral_row()
    even = [float(row[j] + row[j + 4]) / 2 for j in range(4)]
    odd = [float(row[j] - row[j + 4]) / 2 for j in range(4)]
    s = [x[z] + x[z + 4] for z in range(4)]
    d = [x[z] - x[z + 4] for z in range(4)]
    q0, q1 = s[0] - s[2], s[1] - s[3]
    s0 = even[0] * q0 + even[3] * q1
    s1 = even[1] * q0 + even[0] * q1
    sym = [s0, s1, -s0, -s1]
    out = [None] * NI
    for z in range(4):
        acc = None
        for y in range(4):
            coef = odd[z - y] if y <= z else -odd[4 + z - y]
            term = coef * d[y]
            acc = term if acc is None else acc + term
        out[z] = sym[z] + acc
        out[z + 4] = sym[z] - acc
    return out


def primitives(u):
    inv = 1.0 / u[0]
    vel = [u[1] * inv, u[2] * inv, u[3] * inv]
    nu = u[5] * inv
    pres = 0.4 * (u[4] - 0.5 * (u[1] * vel[0] + u[2] * vel[1] + u[3] * vel[2]))
    return vel, nu, pres


def centre_terms(u, vel, nu):
    return [
        0.1 * u[0],
        0.1 * u[1] + 0.02 * vel[0],
        0.1 * u[2] + 0.02 * vel[1],
        0.1 * u[3] + 0.02 * vel[2],
        0.1 * u[4],
        0.1 * u[5] + 0.02 * nu,
    ]


def half_flux(u, vel, pres, k):
    h = 0.5 * vel[k]
    f = [0.5 * u[1 + k], u[1] * h, u[2] * h, u[3] * h, (u[4] + pres) * h, u[5] * h]
    f[1 + k] = f[1 + k] + 0.5 * pres
    return f


def next_terms(u, k):
    vel, nu, pres = primitives(u)
    c = centre_terms(u, vel, nu)
    return [f - g for f, g in zip(half_flux(u, vel, pres, k), c)]


def prev_terms(u, k):
    vel, nu, pres = primitives(u)
    c = centre_terms(u, vel, nu)
    return [-(f + g) for f, g in zip(half_flux(u, vel, pres, k), c)]


def kernel(
    n_dom,
    n_cells,
    flow,
    idx,
    wgt,
    count,
    new_state,
    last_update,
    idx_s,
    count_s,
    idx_v,
    wgt_v,
    cur,
    in_u,
    in_n,
    w1,
    w2,
    ss,
    ww,
    n0,
    n1,
    rr,
    a2,
    b2,
    coef,
    win,
    edge,
    halo,
    redge,
    rhalo,
    qedge,
    qhalo,
    wedge,
    whalo,
    slab_n,
    slab_a,
    slab_b,
    slab_out,
    slab_in,
    load_sem,
    p_send,
    p_recv,
    d_send,
    d_recv,
):
    inst = lax.axis_index("inst")
    dom = lax.axis_index("dom")
    left = lax.rem(dom + n_dom - 1, n_dom)
    right = lax.rem(dom + 1, n_dom)

    others = [lax.rem(inst + n, NI) for n in range(1, NI)]
    body, place = inst // ZN, lax.rem(inst, ZN)
    at_start = jnp.where(place == 0, 1, 0)
    at_end = jnp.where(place == ZN - 1, 1, 0)
    before = lax.rem(dom + n_dom - at_start, n_dom)
    beyond = lax.rem(dom + at_end, n_dom)
    below = (body * ZN + lax.rem(place + ZN - 1, ZN), before)
    above = (body * ZN + lax.rem(place + 1, ZN), beyond)

    loads = [
        pltpu.make_async_copy(source, target, load_sem.at[n])
        for n, (source, target) in enumerate(
            ((flow, cur), (idx, idx_s), (idx, idx_v), (wgt, wgt_v), (count, count_s))
        )
    ]
    for c in loads:
        c.start()
    barrier = pltpu.get_barrier_semaphore()
    for j in others:
        pl.semaphore_signal(barrier, inc=1, device_id=(j, dom), device_id_type=MESH)
    for device in ((inst, left), (inst, right), below, above):
        pl.semaphore_signal(barrier, inc=1, device_id=device, device_id_type=MESH)

    def remote(source, target, send, recv, device):
        return pltpu.make_async_remote_copy(
            src_ref=source,
            dst_ref=target,
            send_sem=send,
            recv_sem=recv,
            device_id=device,
            device_id_type=MESH,
        )

    def source_of(unit, partner, part):
        side, slab = partner // ZN, lax.rem(partner, ZN)
        row = 1 + side if part == 0 else (AX - 1) * side
        mine = pl.ds(pl.multiple_of(SLAB * slab, SLAB), SLAB)
        if unit == 0:
            return flow.at[:, row, mine]
        if unit == 2:
            return n0.at[:, row, mine]
        return (w1 if unit == 1 else w2).at[part, partner]

    def target_of(unit, part, slot):
        spot = 2 * part + slot // ZN
        at = SLAB * lax.rem(slot, ZN)
        if unit == 0:
            return in_u.at[part, slot]
        if unit == 1:
            return ss.at[spot, :, pl.ds(pl.multiple_of(at, SLAB), SLAB)]
        if unit == 2:
            return in_n.at[slot]
        return ww.at[spot, :, pl.ds(pl.multiple_of(at + 8, 8), SLAB)]

    def send(unit, part):
        target = target_of(unit, part, inst)
        for j in others:
            remote(
                source_of(unit, j, part), target, p_send.at[unit], p_recv.at[unit, part], (j, dom)
            ).start()
        pltpu.make_async_copy(source_of(unit, inst, part), target, p_recv.at[unit, part]).start()

    def arrive(unit, part):
        spots = pl.ds(2 * part, 2)
        ref = (in_u.at[part], ss.at[spots], in_n, ww.at[spots, :, pl.ds(8, T)])[unit]
        pltpu.make_async_copy(ref, ref, p_recv.at[unit, part]).wait()

    def gone(unit):
        ref = in_n.at[0 : NI - 1] if unit == 2 else w1.at[:, 0 : NI - 1]
        pltpu.make_async_copy(ref, ref, p_send.at[unit]).wait()

    def near(slot, source, target, device):
        return remote(source, target, d_send.at[slot], d_recv.at[slot], (inst, device))

    def both(slot, out, back):
        return [near(slot, out(0), back(1), left), near(slot + 1, out(1), back(0), right)]

    def start(copies):
        for c in copies:
            c.start()
        return copies

    def over(n, body):
        def step(i, _):
            body(i)
            return 0

        lax.fori_loop(0, n, step, 0)

    lane = lax.broadcasted_iota(jnp.int32, (8, S), 1)
    first_lane = lane == 0
    last_lane = lane == S - 1

    def spanwise(f, c):
        out = []
        for g, h in zip(f, c):
            up, down = g - h, g + h
            after = jnp.where(last_lane, up, pltpu.roll(up, S - 1, 1))
            prior = jnp.where(first_lane, down, pltpu.roll(down, 1, 1))
            out.append(6.0 * h + (after - prior))
        return out

    def spectral(part, target, plus=None):
        def variable(v):
            for t0 in range(0, SLAB, 8):
                rows = slice(t0, t0 + 8)
                if plus is None:
                    x = [in_u[part, m, v, rows, :] for m in range(NI)]
                else:
                    x = [w1[part, m, v, rows, :] + plus(m, v, t0) for m in range(NI)]
                for m, g in enumerate(spectral_apply(x)):
                    target[part, m, v, rows, :] = g

        over(NV, variable)

    def inside(out, first_tile, last_tile):
        def tile(i, _):
            t0 = pl.multiple_of(8 * i, 8)
            total = []
            first = []
            second = []
            for a in range(AX):
                u = [cur[v, a, pl.ds(t0, 8), :] for v in range(NV)]
                vel, nu, pres = primitives(u)
                c = centre_terms(u, vel, nu)
                f1 = half_flux(u, vel, pres, 0)
                first.append([f - g for f, g in zip(f1, c)])
                second.append([f + g for f, g in zip(f1, c)])
                f2 = half_flux(u, vel, pres, 1)
                for v in range(NV):
                    a2[v, a, pl.ds(t0 + 8, 8), :] = f2[v] - c[v]
                    b2[v, a, pl.ds(t0 + 8, 8), :] = f2[v] + c[v]
                total.append(spanwise(half_flux(u, vel, pres, 2), c))
            for a in range(AX):
                for v in range(NV):
                    r = total[a][v]
                    if a == AX - 1:
                        r = r + first[a][v]
                    elif a != AX // 2 - 1:
                        r = r + first[a + 1][v]
                    if a == 0:
                        r = r - second[a][v]
                    elif a != AX // 2:
                        r = r - second[a - 1][v]
                    out[v, a, pl.ds(t0, 8), :] = r
            return 0

        lax.fori_loop(first_tile, last_tile, tile, 0)

    def around(out, it, layers):
        for c in layers:
            c.wait_recv()
        low = prev_terms([halo[it, 0, v] for v in range(NV)], 1)
        high = next_terms([halo[it, 1, v] for v in range(NV)], 1)
        for v in range(NV):
            for a in range(AX):
                b2[v, a, 7:8, :] = -low[v][a : a + 1]
                a2[v, a, T + 8 : T + 9, :] = high[v][a : a + 1]

        def variable(v):
            for a in range(AX):
                out[v, a] += a2[v, a, 9 : T + 9] - b2[v, a, 7 : T + 7]

        over(NV, variable)

    def interface(out, it, tiles):
        def ghosts(n):
            i = tiles[0] + n * tiles[2]
            t0 = pl.multiple_of(8 * i, 8)
            for side in range(2):
                taps = [coef[side, n, pl.ds(t0, 8), :] for n in range(3)]
                u = []
                for v in range(NV):
                    g = taps[0] * win[it, side, v, pl.ds(base[side] + t0, 8), :]
                    g = g + taps[1] * win[it, side, v, pl.ds(base[side] + t0 + 1, 8), :]
                    g = g + taps[2] * win[it, side, v, pl.ds(base[side] + t0 + 2, 8), :]
                    u.append(g)
                terms = next_terms(u, 0) if side == 0 else prev_terms(u, 0)
                for v in range(NV):
                    out[v, 1 + side, pl.ds(t0, 8), :] += terms[v]

        over(tiles[1], ghosts)

    def outer_layers(it):
        for side, t in enumerate((0, T - 1)):
            for v in range(NV):
                edge[it, side, v] = cur[v, :, t, :]
            edge[it, side, NV] = jnp.broadcast_to(active, (AX, S))
        return start(
            both(10 * it, lambda side: edge.at[it, side], lambda side: halo.at[it, side])
        )

    def interface_rows(it):
        for v in range(NV):
            win[it, 0, v, 0:T] = cur[v, 2]
            win[it, 1, v, T : 2 * T] = cur[v, 1]
        return start(
            [
                near(10 * it + 2, win.at[it, 0, :, 0:T], win.at[it, 0, :, T : 2 * T], left),
                near(10 * it + 3, win.at[it, 1, :, T : 2 * T], win.at[it, 1, :, 0:T], right),
            ]
        )

    def rim_of(slot, out, back, spots):
        return start(
            both(slot, lambda side: out.at[side, :, spots], lambda side: back.at[side, :, spots])
        )

    FRONT, REST = pl.ds(0, 2), pl.ds(2, 2)

    pl.semaphore_wait(barrier, NI + 3)
    for part in range(2):
        send(0, part)
    for c in loads:
        c.wait()
    active = jnp.where(lax.broadcasted_iota(jnp.int32, (1, S), 1) < count_s[0], 1.0, 0.0)
    layers = outer_layers(0)
    windows = interface_rows(0)

    def least(t, low):
        cell = dom * T + t
        gaps = (idx_s[0, t] - cell, cell - 1 - idx_s[1, t])
        gaps = [jnp.where(g < 0, g + n_cells, g) for g in gaps]
        return jnp.minimum(low[0], gaps[0]), jnp.minimum(low[1], gaps[1])

    most = (jnp.int32(n_cells), jnp.int32(n_cells))
    offset = [jnp.clip(x, 0, T - 2) for x in lax.fori_loop(0, T, least, most)]
    base = [offset[0], T - 2 - offset[1]]
    eye = lax.broadcasted_iota(jnp.int32, (T, T), 0) == lax.broadcasted_iota(
        jnp.int32, (T, T), 1
    )
    for side in range(2):
        cell = dom * T + lax.broadcasted_iota(jnp.int32, (1, T), 1)
        row = idx_v[side : side + 1, :]
        gap = row - cell if side == 0 else cell - 1 - row
        gap = jnp.where(gap < 0, gap + n_cells, gap)
        step = jnp.where(gap > offset[side], 1.0, 0.0)
        w = wgt_v[side : side + 1, :]
        taps = [(1.0 - step) * w, step * w + (1.0 - step) * (1.0 - w), step * (1.0 - w)]
        if side == 1:
            taps = [step * w, (1.0 - step) * w + step * (1.0 - w), (1.0 - step) * (1.0 - w)]
        for i, tap in enumerate(taps):
            column = jnp.sum(jnp.where(eye, tap, 0.0), axis=1, keepdims=True)
            coef[side, i] = jnp.broadcast_to(column, (T, S))

    half = T // 16
    arrive(0, 0)
    spectral(0, w1)
    send(1, 0)
    inside(n0, 0, half)
    arrive(0, 1)
    spectral(1, w1)
    send(1, 1)
    for v in range(NV):
        slab_out[0, v] = in_u[1, :, v, 0, :]
        slab_out[1, v] = in_u[1, :, v, SLAB - 1, :]
    slabs = start(
        [
            remote(slab_out.at[0], slab_in.at[1], d_send.at[18], d_recv.at[18], below),
            remote(slab_out.at[1], slab_in.at[0], d_send.at[19], d_recv.at[19], above),
        ]
    )
    inside(n0, half, 2 * half)
    around(n0, 0, layers)
    for c in windows:
        c.wait_recv()
    interface(n0, 0, (0, T // 8, 1))
    send(2, 0)

    toward = jnp.where(body == 0, 1.0, -1.0)

    def slab_inside(m):
        for t0 in range(0, SLAB, 8):
            rows = slice(t0, t0 + 8)
            u = [in_u[0, m, v, rows, :] for v in range(NV)]
            vel, nu, pres = primitives(u)
            c1 = centre_terms(u, vel, nu)
            f1 = half_flux(u, vel, pres, 0)
            u = [in_u[1, m, v, rows, :] for v in range(NV)]
            vel, nu, pres = primitives(u)
            c = centre_terms(u, vel, nu)
            f = half_flux(u, vel, pres, 0)
            f2 = half_flux(u, vel, pres, 1)
            r = spanwise(half_flux(u, vel, pres, 2), c)
            for v in range(NV):
                slab_a[m, v, t0 : t0 + 8, :] = f2[v] - c[v]
                slab_b[m, v, t0 + 8 : t0 + 16, :] = f2[v] + c[v]
                slab_n[m, v, rows, :] = r[v] + (toward * (f1[v] - f[v]) - (c1[v] + c[v]))

    over(NI, slab_inside)
    for c in slabs:
        c.wait()
    low = prev_terms([slab_in[0, v] for v in range(NV)], 1)
    high = next_terms([slab_in[1, v] for v in range(NV)], 1)
    for v in range(NV):
        slab_b[:, v, 7, :] = -low[v]
        slab_a[:, v, SLAB, :] = high[v]

    def outer(m, v, t0):
        return slab_n[m, v, t0 : t0 + 8, :] + (
            slab_a[m, v, t0 + 1 : t0 + 9, :] - slab_b[m, v, t0 + 7 : t0 + 15, :]
        )

    spectral(1, w2, outer)

    def keep_rows(out, spots, times, value):
        for spot in spots:
            for n, t in enumerate(times):
                out[n // (len(times) // 2), n % (len(times) // 2), spot] = value(spot, t)

    def put_rows(back, spots, times):
        for spot in spots:
            for n, t in enumerate(times):
                rr[spot, :, 8 + t, :] = back[n // 2, n % 2, spot]

    ends = (0, 1, T - 2, T - 1)
    outside = (-2, -1, T, T + 1)

    def smoothed(ref, spot, v):
        return (
            0.625 * ref[spot, v, 8 : T + 8]
            + 0.125 * (ref[spot, v, 7 : T + 7] + ref[spot, v, 9 : T + 9])
            + 0.0625 * (ref[spot, v, 6 : T + 6] + ref[spot, v, 10 : T + 10])
        )

    def sums(spots):
        def variable(v):
            for spot in spots:
                rr[spot, v, 8 : T + 8] = n0[v, ORDER[spot]] + ss[spot, v]

        over(NV, variable)

    def first_update(spots):
        def variable(v):
            for spot in spots:
                a = ORDER[spot]
                cur[v, a] = cur[v, a] - 0.05 * (smoothed(rr, spot, v) * active)

        over(NV, variable)

    def first_sum(spot, t):
        return n0[:, ORDER[spot], t, :] + ss[spot, :, t, :]

    arrive(1, 0)
    keep_rows(redge, (0, 1), ends, first_sum)
    rim = rim_of(4, redge, rhalo, FRONT)
    sums((0, 1))
    arrive(1, 1)
    keep_rows(redge, (2, 3), ends, first_sum)
    rim2 = rim_of(6, redge, rhalo, REST)
    for c in rim:
        c.wait()
    put_rows(rhalo, (0, 1), outside)
    gone(0)
    for c in layers + windows:
        c.wait_send()
    first_update((0, 1))
    windows = interface_rows(1)
    send(3, 1)
    sums((2, 3))
    for c in rim2:
        c.wait()
    put_rows(rhalo, (2, 3), outside)
    first_update((2, 3))
    layers = outer_layers(1)

    arrive(2, 0)
    spectral(0, w2, lambda m, v, t0: in_n[m, v, t0 : t0 + 8, :])
    send(3, 0)
    inside(n1, 0, 2 * half)
    around(n1, 1, layers)

    def second_sum(spot, t):
        return n1[:, ORDER[spot], t, :] + ss[spot, :, t, :]

    keep_rows(qedge, (2, 3), ends, second_sum)
    rim2 = rim_of(8, qedge, qhalo, REST)
    for c in windows:
        c.wait_recv()
    interface(n1, 1, (0, 2, T // 8 - 1))
    keep_rows(qedge, (0, 1), ends, second_sum)
    rim = rim_of(12 + 2, qedge, qhalo, FRONT)
    interface(n1, 1, (1, T // 8 - 2, 1))

    far_rows = (0, 1, 2, 3, T - 4, T - 3, T - 2, T - 1)

    def last_source(spot, t):
        return ww[spot, :, 8 + t, :]

    arrive(3, 1)
    keep_rows(wedge, (2, 3), far_rows, last_source)
    far2 = rim_of(16, wedge, whalo, REST)
    arrive(3, 0)
    keep_rows(wedge, (0, 1), far_rows, last_source)
    far = rim_of(20, wedge, whalo, FRONT)

    def second_update(spots):
        for spot in spots:
            for n in range(2):
                ww[spot, :, 6 + n, :] = whalo[0, 2 + n, spot]
                ww[spot, :, T + 8 + n, :] = whalo[1, n, spot]
            for side in range(2):
                h = [whalo[side, n, spot] for n in range(4)]
                e = [wedge[side, n, spot] for n in range(4)]
                line = h + e[:2] if side == 0 else e[2:] + h
                mask = halo[0, side, NV, 0:1, :]
                for n in range(2):
                    x = line[n : n + 5]
                    z = 0.625 * x[2] + 0.125 * (x[1] + x[3]) + 0.0625 * (x[0] + x[4])
                    t = n - 2 if side == 0 else T + n
                    rr[spot, :, 8 + t, :] = qhalo[side, n, spot] - 0.05 * (z * mask)

        def variable(v):
            for spot in spots:
                a = ORDER[spot]
                rr[spot, v, 8 : T + 8] = (
                    n1[v, a] + ss[spot, v] - 0.05 * (smoothed(ww, spot, v) * active)
                )
                update = smoothed(rr, spot, v) * active
                last_update[v, a] = update
                new_state[v, a] = cur[v, a] - 0.05 * update

        over(NV, variable)

    for c in rim2 + far2:
        c.wait()
    second_update((2, 3))
    for c in rim + far:
        c.wait()
    second_update((0, 1))

    for c in layers + windows:
        c.wait_send()
    for unit in (1, 2, 3):
        gone(unit)


def local(n_dom, flow_state, donor_index, donor_weight, span_count):
    shape = (NV, AX, T, S)
    padded = (NV, AX, T + 16, S)
    pieces = (2, NI, NV, SLAB, S)
    turned = (AX, NV, T + 16, S)
    f32 = jnp.float32
    anywhere = pl.BlockSpec(memory_space=pl.ANY)
    vmem = pl.BlockSpec(memory_space=pltpu.VMEM)
    new_state, last_update = pl.pallas_call(
        functools.partial(kernel, n_dom, n_dom * T),
        out_shape=[jax.ShapeDtypeStruct(shape, f32)] * 2,
        in_specs=[anywhere] * 4,
        out_specs=[vmem, vmem],
        scratch_shapes=[
            pltpu.SMEM((2, T), jnp.int32),
            pltpu.SMEM((1,), jnp.int32),
            pltpu.VMEM((2, T), jnp.int32),
            pltpu.VMEM((2, T), f32),
            pltpu.VMEM(shape, f32),
            pltpu.VMEM(pieces, f32),
            pltpu.VMEM((NI, NV, SLAB, S), f32),
            pltpu.VMEM(pieces, f32),
            pltpu.VMEM(pieces, f32),
            pltpu.VMEM((AX, NV, T, S), f32),
            pltpu.VMEM(turned, f32),
            pltpu.VMEM(shape, f32),
            pltpu.VMEM(shape, f32),
            pltpu.VMEM(turned, f32),
            pltpu.VMEM(padded, f32),
            pltpu.VMEM(padded, f32),
            pltpu.VMEM((2, 3, T, S), f32),
            pltpu.VMEM((ITERS, 2, NV, 2 * T, S), f32),
            pltpu.VMEM((ITERS, 2, NV + 1, AX, S), f32),
            pltpu.VMEM((ITERS, 2, NV + 1, AX, S), f32),
            pltpu.VMEM((2, 2, AX, NV, S), f32),
            pltpu.VMEM((2, 2, AX, NV, S), f32),
            pltpu.VMEM((2, 2, AX, NV, S), f32),
            pltpu.VMEM((2, 2, AX, NV, S), f32),
            pltpu.VMEM((2, 4, AX, NV, S), f32),
            pltpu.VMEM((2, 4, AX, NV, S), f32),
            pltpu.VMEM((NI, NV, SLAB, S), f32),
            pltpu.VMEM((NI, NV, SLAB + 8, S), f32),
            pltpu.VMEM((NI, NV, SLAB + 8, S), f32),
            pltpu.VMEM((2, NV, NI, S), f32),
            pltpu.VMEM((2, NV, NI, S), f32),
            pltpu.SemaphoreType.DMA((5,)),
            pltpu.SemaphoreType.DMA((4,)),
            pltpu.SemaphoreType.DMA((4, 2)),
            pltpu.SemaphoreType.DMA((22,)),
            pltpu.SemaphoreType.DMA((22,)),
        ],
        compiler_params=pltpu.CompilerParams(
            collective_id=0, has_side_effects=True, vmem_limit_bytes=52 * 1024 * 1024
        ),
        cost_estimate=pl.CostEstimate(
            flops=20_000_000, bytes_accessed=3 * PL * T * S * 4, transcendentals=0
        ),
    )(flow_state.reshape(shape), donor_index[0], donor_weight[0], span_count)
    whole = (1, NV, AX, T, S)
    return new_state.reshape(whole), last_update.reshape(whole)


def solution(mesh):
    placed = (
        P("inst", None, None, "dom", None),
        P("inst", None, "dom"),
        P("inst", None, "dom"),
        P("dom"),
    )
    return jax.shard_map(
        functools.partial(local, mesh.shape["dom"]),
        mesh=mesh,
        in_specs=placed,
        out_specs=(P("inst", None, None, "dom", None), P("inst", None, None, "dom", None)),
        check_vma=False,
    )
```

```python
import functools
import math

import jax
import jax.numpy as jnp
import numpy as np
from jax import lax
from jax.experimental import pallas as pl
from jax.experimental.pallas import tpu as pltpu
from jax.sharding import PartitionSpec as P

ITERS = 2
NI = 8
NV = 6
AX = 4
PL = NV * AX
T = 64
S = 128
ZN = 4
SLAB = T // ZN
ORDER = (1, 2, 0, 3)
MESH = pl.DeviceIdType.MESH


def spectral_row():
    k = np.arange(NI)[:, None] - np.arange(NI)[None, :]
    safe = np.where(k == 0, 1.0, np.sin(math.pi * k / NI))
    deriv = np.where(k == 0, 0.0, 0.5 * (-1.0) ** k * np.cos(math.pi * k / NI) / safe)
    return (deriv - 0.1 * deriv @ deriv)[:, 0]


def spectral_apply(x):
    row = spectral_row()
    even = [float(row[j] + row[j + 4]) / 2 for j in range(4)]
    odd = [float(row[j] - row[j + 4]) / 2 for j in range(4)]
    s = [x[z] + x[z + 4] for z in range(4)]
    d = [x[z] - x[z + 4] for z in range(4)]
    q0, q1 = s[0] - s[2], s[1] - s[3]
    s0 = even[0] * q0 + even[3] * q1
    s1 = even[1] * q0 + even[0] * q1
    sym = [s0, s1, -s0, -s1]
    out = [None] * NI
    for z in range(4):
        acc = None
        for y in range(4):
            coef = odd[z - y] if y <= z else -odd[4 + z - y]
            term = coef * d[y]
            acc = term if acc is None else acc + term
        out[z] = sym[z] + acc
        out[z + 4] = sym[z] - acc
    return out


def primitives(u):
    inv = 1.0 / u[0]
    vel = [u[1] * inv, u[2] * inv, u[3] * inv]
    nu = u[5] * inv
    pres = 0.4 * (u[4] - 0.5 * (u[1] * vel[0] + u[2] * vel[1] + u[3] * vel[2]))
    return vel, nu, pres


def centre_terms(u, vel, nu):
    return [
        0.1 * u[0],
        0.1 * u[1] + 0.02 * vel[0],
        0.1 * u[2] + 0.02 * vel[1],
        0.1 * u[3] + 0.02 * vel[2],
        0.1 * u[4],
        0.1 * u[5] + 0.02 * nu,
    ]


def half_flux(u, vel, pres, k):
    h = 0.5 * vel[k]
    f = [0.5 * u[1 + k], u[1] * h, u[2] * h, u[3] * h, (u[4] + pres) * h, u[5] * h]
    f[1 + k] = f[1 + k] + 0.5 * pres
    return f


def next_terms(u, k):
    vel, nu, pres = primitives(u)
    c = centre_terms(u, vel, nu)
    return [f - g for f, g in zip(half_flux(u, vel, pres, k), c)]


def prev_terms(u, k):
    vel, nu, pres = primitives(u)
    c = centre_terms(u, vel, nu)
    return [-(f + g) for f, g in zip(half_flux(u, vel, pres, k), c)]


def kernel(
    n_dom,
    n_cells,
    flow,
    idx,
    wgt,
    count,
    new_state,
    last_update,
    idx_s,
    count_s,
    idx_v,
    wgt_v,
    cur,
    in_u,
    in_n,
    w1,
    w2,
    ss,
    ww,
    n0,
    n1,
    rr,
    a2,
    b2,
    coef,
    win,
    edge,
    halo,
    redge,
    rhalo,
    qedge,
    qhalo,
    wedge,
    whalo,
    slab_n,
    slab_a,
    slab_b,
    slab_out,
    slab_in,
    load_sem,
    p_send,
    p_recv,
    d_send,
    d_recv,
):
    inst = lax.axis_index("inst")
    dom = lax.axis_index("dom")
    left = lax.rem(dom + n_dom - 1, n_dom)
    right = lax.rem(dom + 1, n_dom)

    body, place = inst // ZN, lax.rem(inst, ZN)
    others = [
        lax.rem(body + other, 2) * ZN + lax.rem(place + dz, ZN)
        for other in (1, 0)
        for dz in (2, 1, 3, 0)
        if other or dz
    ]
    at_start = jnp.where(place == 0, 1, 0)
    at_end = jnp.where(place == ZN - 1, 1, 0)
    before = lax.rem(dom + n_dom - at_start, n_dom)
    beyond = lax.rem(dom + at_end, n_dom)
    below = (body * ZN + lax.rem(place + ZN - 1, ZN), before)
    above = (body * ZN + lax.rem(place + 1, ZN), beyond)

    loads = [
        pltpu.make_async_copy(source, target, load_sem.at[n])
        for n, (source, target) in enumerate(
            ((flow, cur), (idx, idx_s), (idx, idx_v), (wgt, wgt_v), (count, count_s))
        )
    ]
    for c in loads:
        c.start()
    barrier = pltpu.get_barrier_semaphore()
    for j in others:
        pl.semaphore_signal(barrier, inc=1, device_id=(j, dom), device_id_type=MESH)
    for device in ((inst, left), (inst, right), below, above):
        pl.semaphore_signal(barrier, inc=1, device_id=device, device_id_type=MESH)

    def remote(source, target, send, recv, device):
        return pltpu.make_async_remote_copy(
            src_ref=source,
            dst_ref=target,
            send_sem=send,
            recv_sem=recv,
            device_id=device,
            device_id_type=MESH,
        )

    def source_of(unit, partner, part):
        side, slab = partner // ZN, lax.rem(partner, ZN)
        row = 1 + side if part == 0 else (AX - 1) * side
        mine = pl.ds(pl.multiple_of(SLAB * slab, SLAB), SLAB)
        if unit == 0:
            return flow.at[:, row, mine]
        if unit == 2:
            return n0.at[:, row, mine]
        return (w1 if unit == 1 else w2).at[part, partner]

    def target_of(unit, part, slot):
        spot = 2 * part + slot // ZN
        at = SLAB * lax.rem(slot, ZN)
        if unit == 0:
            return in_u.at[part, slot]
        if unit == 1:
            return ss.at[spot, :, pl.ds(pl.multiple_of(at, SLAB), SLAB)]
        if unit == 2:
            return in_n.at[slot]
        return ww.at[spot, :, pl.ds(pl.multiple_of(at + 8, 8), SLAB)]

    def send(unit, part):
        target = target_of(unit, part, inst)
        for j in others:
            remote(
                source_of(unit, j, part), target, p_send.at[unit], p_recv.at[unit, part], (j, dom)
            ).start()
        pltpu.make_async_copy(source_of(unit, inst, part), target, p_recv.at[unit, part]).start()

    def arrive(unit, part):
        spots = pl.ds(2 * part, 2)
        ref = (in_u.at[part], ss.at[spots], in_n, ww.at[spots, :, pl.ds(8, T)])[unit]
        pltpu.make_async_copy(ref, ref, p_recv.at[unit, part]).wait()

    def gone(unit):
        ref = in_n.at[0 : NI - 1] if unit == 2 else w1.at[:, 0 : NI - 1]
        pltpu.make_async_copy(ref, ref, p_send.at[unit]).wait()

    def near(slot, source, target, device):
        return remote(source, target, d_send.at[slot], d_recv.at[slot], (inst, device))

    def both(slot, out, back):
        return [near(slot, out(0), back(1), left), near(slot + 1, out(1), back(0), right)]

    def start(copies):
        for c in copies:
            c.start()
        return copies

    def over(n, body):
        def step(i, _):
            body(i)
            return 0

        lax.fori_loop(0, n, step, 0)

    lane = lax.broadcasted_iota(jnp.int32, (8, S), 1)
    first_lane = lane == 0
    last_lane = lane == S - 1

    def spanwise(f, c):
        out = []
        for g, h in zip(f, c):
            up, down = g - h, g + h
            after = jnp.where(last_lane, up, pltpu.roll(up, S - 1, 1))
            prior = jnp.where(first_lane, down, pltpu.roll(down, 1, 1))
            out.append(6.0 * h + (after - prior))
        return out

    def spectral(part, target, plus=None):
        def variable(v):
            for t0 in range(0, SLAB, 8):
                rows = slice(t0, t0 + 8)
                if plus is None:
                    x = [in_u[part, m, v, rows, :] for m in range(NI)]
                else:
                    x = [w1[part, m, v, rows, :] + plus(m, v, t0) for m in range(NI)]
                for m, g in enumerate(spectral_apply(x)):
                    target[part, m, v, rows, :] = g

        over(NV, variable)

    def inside(out, first_tile, last_tile):
        def tile(i, _):
            t0 = pl.multiple_of(8 * i, 8)
            total = []
            first = []
            second = []
            for a in range(AX):
                u = [cur[v, a, pl.ds(t0, 8), :] for v in range(NV)]
                vel, nu, pres = primitives(u)
                c = centre_terms(u, vel, nu)
                f1 = half_flux(u, vel, pres, 0)
                first.append([f - g for f, g in zip(f1, c)])
                second.append([f + g for f, g in zip(f1, c)])
                f2 = half_flux(u, vel, pres, 1)
                for v in range(NV):
                    a2[v, a, pl.ds(t0 + 8, 8), :] = f2[v] - c[v]
                    b2[v, a, pl.ds(t0 + 8, 8), :] = f2[v] + c[v]
                total.append(spanwise(half_flux(u, vel, pres, 2), c))
            for a in range(AX):
                for v in range(NV):
                    r = total[a][v]
                    if a == AX - 1:
                        r = r + first[a][v]
                    elif a != AX // 2 - 1:
                        r = r + first[a + 1][v]
                    if a == 0:
                        r = r - second[a][v]
                    elif a != AX // 2:
                        r = r - second[a - 1][v]
                    out[v, a, pl.ds(t0, 8), :] = r
            return 0

        lax.fori_loop(first_tile, last_tile, tile, 0)

    def around(out, it, layers):
        for c in layers:
            c.wait_recv()
        low = prev_terms([halo[it, 0, v] for v in range(NV)], 1)
        high = next_terms([halo[it, 1, v] for v in range(NV)], 1)
        for v in range(NV):
            for a in range(AX):
                b2[v, a, 7:8, :] = -low[v][a : a + 1]
                a2[v, a, T + 8 : T + 9, :] = high[v][a : a + 1]

        def variable(v):
            for a in range(AX):
                out[v, a] += a2[v, a, 9 : T + 9] - b2[v, a, 7 : T + 7]

        over(NV, variable)

    def interface(out, it, tiles):
        def ghosts(n):
            i = tiles[0] + n * tiles[2]
            t0 = pl.multiple_of(8 * i, 8)
            for side in range(2):
                taps = [coef[side, n, pl.ds(t0, 8), :] for n in range(3)]
                u = []
                for v in range(NV):
                    g = taps[0] * win[it, side, v, pl.ds(base[side] + t0, 8), :]
                    g = g + taps[1] * win[it, side, v, pl.ds(base[side] + t0 + 1, 8), :]
                    g = g + taps[2] * win[it, side, v, pl.ds(base[side] + t0 + 2, 8), :]
                    u.append(g)
                terms = next_terms(u, 0) if side == 0 else prev_terms(u, 0)
                for v in range(NV):
                    out[v, 1 + side, pl.ds(t0, 8), :] += terms[v]

        over(tiles[1], ghosts)

    def outer_layers(it):
        for side, t in enumerate((0, T - 1)):
            for v in range(NV):
                edge[it, side, v] = cur[v, :, t, :]
            edge[it, side, NV] = jnp.broadcast_to(active, (AX, S))
        return start(
            both(10 * it, lambda side: edge.at[it, side], lambda side: halo.at[it, side])
        )

    def interface_rows(it):
        for v in range(NV):
            win[it, 0, v, 0:T] = cur[v, 2]
            win[it, 1, v, T : 2 * T] = cur[v, 1]
        return start(
            [
                near(10 * it + 2, win.at[it, 0, :, 0:T], win.at[it, 0, :, T : 2 * T], left),
                near(10 * it + 3, win.at[it, 1, :, T : 2 * T], win.at[it, 1, :, 0:T], right),
            ]
        )

    def rim_of(slot, out, back, spots):
        return start(both(slot, lambda side: out.at[side, spots], lambda side: back.at[side, spots]))

    FRONT, REST = pl.ds(0, 2), pl.ds(2, 2)

    pl.semaphore_wait(barrier, NI + 3)
    for part in range(2):
        send(0, part)
    for c in loads:
        c.wait()
    active = jnp.where(lax.broadcasted_iota(jnp.int32, (1, S), 1) < count_s[0], 1.0, 0.0)
    layers = outer_layers(0)
    windows = interface_rows(0)

    def least(t, low):
        cell = dom * T + t
        gaps = (idx_s[0, t] - cell, cell - 1 - idx_s[1, t])
        gaps = [jnp.where(g < 0, g + n_cells, g) for g in gaps]
        return jnp.minimum(low[0], gaps[0]), jnp.minimum(low[1], gaps[1])

    most = (jnp.int32(n_cells), jnp.int32(n_cells))
    offset = [jnp.clip(x, 0, T - 2) for x in lax.fori_loop(0, T, least, most)]
    base = [offset[0], T - 2 - offset[1]]
    eye = lax.broadcasted_iota(jnp.int32, (T, T), 0) == lax.broadcasted_iota(
        jnp.int32, (T, T), 1
    )
    for side in range(2):
        cell = dom * T + lax.broadcasted_iota(jnp.int32, (1, T), 1)
        row = idx_v[side : side + 1, :]
        gap = row - cell if side == 0 else cell - 1 - row
        gap = jnp.where(gap < 0, gap + n_cells, gap)
        step = jnp.where(gap > offset[side], 1.0, 0.0)
        w = wgt_v[side : side + 1, :]
        taps = [(1.0 - step) * w, step * w + (1.0 - step) * (1.0 - w), step * (1.0 - w)]
        if side == 1:
            taps = [step * w, (1.0 - step) * w + step * (1.0 - w), (1.0 - step) * (1.0 - w)]
        for i, tap in enumerate(taps):
            column = jnp.sum(jnp.where(eye, tap, 0.0), axis=1, keepdims=True)
            coef[side, i] = jnp.broadcast_to(column, (T, S))

    half = T // 16
    arrive(0, 0)
    spectral(0, w1)
    send(1, 0)
    inside(n0, 0, half)
    arrive(0, 1)
    spectral(1, w1)
    send(1, 1)
    for v in range(NV):
        slab_out[0, v] = in_u[1, :, v, 0, :]
        slab_out[1, v] = in_u[1, :, v, SLAB - 1, :]
    slabs = start(
        [
            remote(slab_out.at[0], slab_in.at[1], d_send.at[18], d_recv.at[18], below),
            remote(slab_out.at[1], slab_in.at[0], d_send.at[19], d_recv.at[19], above),
        ]
    )
    inside(n0, half, 2 * half)
    around(n0, 0, layers)
    for c in windows:
        c.wait_recv()
    interface(n0, 0, (0, T // 8, 1))
    send(2, 0)

    toward = jnp.where(body == 0, 1.0, -1.0)

    def slab_inside(m):
        for t0 in range(0, SLAB, 8):
            rows = slice(t0, t0 + 8)
            u = [in_u[0, m, v, rows, :] for v in range(NV)]
            vel, nu, pres = primitives(u)
            c1 = centre_terms(u, vel, nu)
            f1 = half_flux(u, vel, pres, 0)
            u = [in_u[1, m, v, rows, :] for v in range(NV)]
            vel, nu, pres = primitives(u)
            c = centre_terms(u, vel, nu)
            f = half_flux(u, vel, pres, 0)
            f2 = half_flux(u, vel, pres, 1)
            r = spanwise(half_flux(u, vel, pres, 2), c)
            for v in range(NV):
                slab_a[m, v, t0 : t0 + 8, :] = f2[v] - c[v]
                slab_b[m, v, t0 + 8 : t0 + 16, :] = f2[v] + c[v]
                slab_n[m, v, rows, :] = r[v] + (toward * (f1[v] - f[v]) - (c1[v] + c[v]))

    over(NI, slab_inside)
    for c in slabs:
        c.wait()
    low = prev_terms([slab_in[0, v] for v in range(NV)], 1)
    high = next_terms([slab_in[1, v] for v in range(NV)], 1)
    for v in range(NV):
        slab_b[:, v, 7, :] = -low[v]
        slab_a[:, v, SLAB, :] = high[v]

    def outer(m, v, t0):
        return slab_n[m, v, t0 : t0 + 8, :] + (
            slab_a[m, v, t0 + 1 : t0 + 9, :] - slab_b[m, v, t0 + 7 : t0 + 15, :]
        )

    spectral(1, w2, outer)

    def keep_rows(out, spots, value):
        n = out.shape[3]
        for spot in spots:
            for v in range(NV):
                out[0, spot, v] = value(spot, v, 0, n)
                out[1, spot, v] = value(spot, v, T - n, T)

    def put_rows(back, spots):
        for spot in spots:
            for v in range(NV):
                rr[spot, v, 6:8, :] = back[0, spot, v]
                rr[spot, v, T + 8 : T + 10, :] = back[1, spot, v]

    def smoothed(ref, spot, v):
        return (
            0.625 * ref[spot, v, 8 : T + 8]
            + 0.125 * (ref[spot, v, 7 : T + 7] + ref[spot, v, 9 : T + 9])
            + 0.0625 * (ref[spot, v, 6 : T + 6] + ref[spot, v, 10 : T + 10])
        )

    def sums(spots):
        def variable(v):
            for spot in spots:
                rr[spot, v, 8 : T + 8] = n0[v, ORDER[spot]] + ss[spot, v]

        over(NV, variable)

    def first_update(spots):
        def variable(v):
            for spot in spots:
                a = ORDER[spot]
                cur[v, a] = cur[v, a] - 0.05 * (smoothed(rr, spot, v) * active)

        over(NV, variable)

    def first_sum(spot, v, t0, t1):
        return n0[v, ORDER[spot], t0:t1, :] + ss[spot, v, t0:t1, :]

    arrive(1, 0)
    keep_rows(redge, (0, 1), first_sum)
    rim = rim_of(4, redge, rhalo, FRONT)
    sums((0, 1))
    arrive(1, 1)
    keep_rows(redge, (2, 3), first_sum)
    rim2 = rim_of(6, redge, rhalo, REST)
    for c in rim:
        c.wait()
    put_rows(rhalo, (0, 1))
    gone(0)
    for c in layers + windows:
        c.wait_send()
    first_update((0, 1))
    windows = interface_rows(1)
    send(3, 1)
    sums((2, 3))
    for c in rim2:
        c.wait()
    put_rows(rhalo, (2, 3))
    first_update((2, 3))
    layers = outer_layers(1)

    arrive(2, 0)
    spectral(0, w2, lambda m, v, t0: in_n[m, v, t0 : t0 + 8, :])
    send(3, 0)
    inside(n1, 0, 2 * half)
    around(n1, 1, layers)

    def second_sum(spot, v, t0, t1):
        return n1[v, ORDER[spot], t0:t1, :] + ss[spot, v, t0:t1, :]

    keep_rows(qedge, (2, 3), second_sum)
    rim2 = rim_of(8, qedge, qhalo, REST)
    for c in windows:
        c.wait_recv()
    interface(n1, 1, (0, 2, T // 8 - 1))
    keep_rows(qedge, (0, 1), second_sum)
    rim = rim_of(12 + 2, qedge, qhalo, FRONT)
    interface(n1, 1, (1, T // 8 - 2, 1))

    def last_source(spot, v, t0, t1):
        return ww[spot, v, 8 + t0 : 8 + t1, :]

    arrive(3, 1)
    keep_rows(wedge, (2, 3), last_source)
    far2 = rim_of(16, wedge, whalo, REST)
    arrive(3, 0)
    keep_rows(wedge, (0, 1), last_source)
    far = rim_of(20, wedge, whalo, FRONT)

    masks = [halo[0, side, NV, 0:1, :] for side in range(2)]

    def second_update(spots):
        def variable(v):
            for spot in spots:
                a = ORDER[spot]
                ww[spot, v, 4:8, :] = whalo[0, spot, v]
                ww[spot, v, T + 8 : T + 12, :] = whalo[1, spot, v]
                for side, t in enumerate((6, T + 8)):
                    z = (
                        0.625 * ww[spot, v, t : t + 2, :]
                        + 0.125 * (ww[spot, v, t - 1 : t + 1, :] + ww[spot, v, t + 1 : t + 3, :])
                        + 0.0625 * (ww[spot, v, t - 2 : t, :] + ww[spot, v, t + 2 : t + 4, :])
                    )
                    rr[spot, v, t : t + 2, :] = qhalo[side, spot, v] - 0.05 * (z * masks[side])
                rr[spot, v, 8 : T + 8] = (
                    n1[v, a] + ss[spot, v] - 0.05 * (smoothed(ww, spot, v) * active)
                )
                update = smoothed(rr, spot, v) * active
                last_update[v, a] = update
                new_state[v, a] = cur[v, a] - 0.05 * update

        over(NV, variable)

    for c in rim2 + far2:
        c.wait()
    second_update((2, 3))
    for c in rim + far:
        c.wait()
    second_update((0, 1))

    for c in layers + windows:
        c.wait_send()
    for unit in (1, 2, 3):
        gone(unit)


def local(n_dom, flow_state, donor_index, donor_weight, span_count):
    shape = (NV, AX, T, S)
    padded = (NV, AX, T + 16, S)
    pieces = (2, NI, NV, SLAB, S)
    turned = (AX, NV, T + 16, S)
    f32 = jnp.float32
    anywhere = pl.BlockSpec(memory_space=pl.ANY)
    vmem = pl.BlockSpec(memory_space=pltpu.VMEM)
    new_state, last_update = pl.pallas_call(
        functools.partial(kernel, n_dom, n_dom * T),
        out_shape=[jax.ShapeDtypeStruct(shape, f32)] * 2,
        in_specs=[anywhere] * 4,
        out_specs=[vmem, vmem],
        scratch_shapes=[
            pltpu.SMEM((2, T), jnp.int32),
            pltpu.SMEM((1,), jnp.int32),
            pltpu.VMEM((2, T), jnp.int32),
            pltpu.VMEM((2, T), f32),
            pltpu.VMEM(shape, f32),
            pltpu.VMEM(pieces, f32),
            pltpu.VMEM((NI, NV, SLAB, S), f32),
            pltpu.VMEM(pieces, f32),
            pltpu.VMEM(pieces, f32),
            pltpu.VMEM((AX, NV, T, S), f32),
            pltpu.VMEM(turned, f32),
            pltpu.VMEM(shape, f32),
            pltpu.VMEM(shape, f32),
            pltpu.VMEM(turned, f32),
            pltpu.VMEM(padded, f32),
            pltpu.VMEM(padded, f32),
            pltpu.VMEM((2, 3, T, S), f32),
            pltpu.VMEM((ITERS, 2, NV, 2 * T, S), f32),
            pltpu.VMEM((ITERS, 2, NV + 1, AX, S), f32),
            pltpu.VMEM((ITERS, 2, NV + 1, AX, S), f32),
            pltpu.VMEM((2, AX, NV, 2, S), f32),
            pltpu.VMEM((2, AX, NV, 2, S), f32),
            pltpu.VMEM((2, AX, NV, 2, S), f32),
            pltpu.VMEM((2, AX, NV, 2, S), f32),
            pltpu.VMEM((2, AX, NV, 4, S), f32),
            pltpu.VMEM((2, AX, NV, 4, S), f32),
            pltpu.VMEM((NI, NV, SLAB, S), f32),
            pltpu.VMEM((NI, NV, SLAB + 8, S), f32),
            pltpu.VMEM((NI, NV, SLAB + 8, S), f32),
            pltpu.VMEM((2, NV, NI, S), f32),
            pltpu.VMEM((2, NV, NI, S), f32),
            pltpu.SemaphoreType.DMA((5,)),
            pltpu.SemaphoreType.DMA((4,)),
            pltpu.SemaphoreType.DMA((4, 2)),
            pltpu.SemaphoreType.DMA((22,)),
            pltpu.SemaphoreType.DMA((22,)),
        ],
        compiler_params=pltpu.CompilerParams(
            collective_id=0, has_side_effects=True, vmem_limit_bytes=52 * 1024 * 1024
        ),
        cost_estimate=pl.CostEstimate(
            flops=20_000_000, bytes_accessed=3 * PL * T * S * 4, transcendentals=0
        ),
    )(flow_state.reshape(shape), donor_index[0], donor_weight[0], span_count)
    whole = (1, NV, AX, T, S)
    return new_state.reshape(whole), last_update.reshape(whole)


def solution(mesh):
    placed = (
        P("inst", None, None, "dom", None),
        P("inst", None, "dom"),
        P("inst", None, "dom"),
        P("dom"),
    )
    return jax.shard_map(
        functools.partial(local, mesh.shape["dom"]),
        mesh=mesh,
        in_specs=placed,
        out_specs=(P("inst", None, None, "dom", None), P("inst", None, None, "dom", None)),
        check_vma=False,
    )
```

```python
import functools
import math

import jax
import jax.numpy as jnp
import numpy as np
from jax import lax
from jax.experimental import pallas as pl
from jax.experimental.pallas import tpu as pltpu
from jax.sharding import PartitionSpec as P

ITERS = 2
NI = 8
NV = 6
AX = 4
PL = NV * AX
T = 64
S = 128
ZN = 4
SLAB = T // ZN
ORDER = (1, 2, 0, 3)
MESH = pl.DeviceIdType.MESH


def spectral_row():
    k = np.arange(NI)[:, None] - np.arange(NI)[None, :]
    safe = np.where(k == 0, 1.0, np.sin(math.pi * k / NI))
    deriv = np.where(k == 0, 0.0, 0.5 * (-1.0) ** k * np.cos(math.pi * k / NI) / safe)
    return (deriv - 0.1 * deriv @ deriv)[:, 0]


def spectral_apply(x):
    row = spectral_row()
    even = [float(row[j] + row[j + 4]) / 2 for j in range(4)]
    odd = [float(row[j] - row[j + 4]) / 2 for j in range(4)]
    s = [x[z] + x[z + 4] for z in range(4)]
    d = [x[z] - x[z + 4] for z in range(4)]
    q0, q1 = s[0] - s[2], s[1] - s[3]
    s0 = even[0] * q0 + even[3] * q1
    s1 = even[1] * q0 + even[0] * q1
    sym = [s0, s1, -s0, -s1]
    out = [None] * NI
    for z in range(4):
        acc = None
        for y in range(4):
            coef = odd[z - y] if y <= z else -odd[4 + z - y]
            term = coef * d[y]
            acc = term if acc is None else acc + term
        out[z] = sym[z] + acc
        out[z + 4] = sym[z] - acc
    return out


def primitives(u):
    inv = 1.0 / u[0]
    vel = [u[1] * inv, u[2] * inv, u[3] * inv]
    nu = u[5] * inv
    pres = 0.4 * (u[4] - 0.5 * (u[1] * vel[0] + u[2] * vel[1] + u[3] * vel[2]))
    return vel, nu, pres


def centre_terms(u, vel, nu):
    return [
        0.1 * u[0],
        0.1 * u[1] + 0.02 * vel[0],
        0.1 * u[2] + 0.02 * vel[1],
        0.1 * u[3] + 0.02 * vel[2],
        0.1 * u[4],
        0.1 * u[5] + 0.02 * nu,
    ]


def half_flux(u, vel, pres, k):
    h = 0.5 * vel[k]
    f = [0.5 * u[1 + k], u[1] * h, u[2] * h, u[3] * h, (u[4] + pres) * h, u[5] * h]
    f[1 + k] = f[1 + k] + 0.5 * pres
    return f


def next_terms(u, k):
    vel, nu, pres = primitives(u)
    c = centre_terms(u, vel, nu)
    return [f - g for f, g in zip(half_flux(u, vel, pres, k), c)]


def prev_terms(u, k):
    vel, nu, pres = primitives(u)
    c = centre_terms(u, vel, nu)
    return [-(f + g) for f, g in zip(half_flux(u, vel, pres, k), c)]


def kernel(
    n_dom,
    n_cells,
    flow,
    idx,
    wgt,
    count,
    new_state,
    last_update,
    idx_s,
    count_s,
    idx_v,
    wgt_v,
    cur,
    in_u,
    in_n,
    w1,
    w2,
    ss,
    ww,
    n0,
    n1,
    rr,
    a2,
    b2,
    coef,
    win,
    edge,
    halo,
    redge,
    rhalo,
    qedge,
    qhalo,
    wedge,
    whalo,
    slab_n,
    slab_a,
    slab_b,
    slab_out,
    slab_in,
    load_sem,
    p_send,
    p_recv,
    d_send,
    d_recv,
):
    inst = lax.axis_index("inst")
    dom = lax.axis_index("dom")
    left = lax.rem(dom + n_dom - 1, n_dom)
    right = lax.rem(dom + 1, n_dom)

    others = [lax.rem(inst + n, NI) for n in range(1, NI)]
    body, place = inst // ZN, lax.rem(inst, ZN)
    at_start = jnp.where(place == 0, 1, 0)
    at_end = jnp.where(place == ZN - 1, 1, 0)
    before = lax.rem(dom + n_dom - at_start, n_dom)
    beyond = lax.rem(dom + at_end, n_dom)
    below = (body * ZN + lax.rem(place + ZN - 1, ZN), before)
    above = (body * ZN + lax.rem(place + 1, ZN), beyond)

    loads = [
        pltpu.make_async_copy(source, target, load_sem.at[n])
        for n, (source, target) in enumerate(
            ((flow, cur), (idx, idx_s), (idx, idx_v), (wgt, wgt_v), (count, count_s))
        )
    ]
    for c in loads:
        c.start()
    barrier = pltpu.get_barrier_semaphore()
    for j in others:
        pl.semaphore_signal(barrier, inc=1, device_id=(j, dom), device_id_type=MESH)
    for device in ((inst, left), (inst, right), below, above):
        pl.semaphore_signal(barrier, inc=1, device_id=device, device_id_type=MESH)

    def remote(source, target, send, recv, device):
        return pltpu.make_async_remote_copy(
            src_ref=source,
            dst_ref=target,
            send_sem=send,
            recv_sem=recv,
            device_id=device,
            device_id_type=MESH,
        )

    def source_of(unit, partner, part):
        side, slab = partner // ZN, lax.rem(partner, ZN)
        row = 1 + side if part == 0 else (AX - 1) * side
        mine = pl.ds(pl.multiple_of(SLAB * slab, SLAB), SLAB)
        if unit == 0:
            return flow.at[:, row, mine]
        if unit == 2:
            return n0.at[:, row, mine]
        return (w1 if unit == 1 else w2).at[part, partner]

    def target_of(unit, part, slot):
        spot = 2 * part + slot // ZN
        at = SLAB * lax.rem(slot, ZN)
        if unit == 0:
            return in_u.at[part, slot]
        if unit == 1:
            return ss.at[spot, :, pl.ds(pl.multiple_of(at, SLAB), SLAB)]
        if unit == 2:
            return in_n.at[slot]
        return ww.at[spot, :, pl.ds(pl.multiple_of(at + 8, 8), SLAB)]

    def send(unit, part, part_v):
        some = pl.ds(NV // 2 * part_v, NV // 2)
        target = target_of(unit, part, inst).at[some]
        came = p_recv.at[unit, part, part_v]
        for j in others:
            source = source_of(unit, j, part).at[some]
            remote(source, target, p_send.at[unit], came, (j, dom)).start()
        pltpu.make_async_copy(source_of(unit, inst, part).at[some], target, came).start()

    def arrive(unit, part, part_v):
        spots = pl.ds(2 * part, 2)
        some = pl.ds(NV // 2 * part_v, NV // 2)
        ref = (
            in_u.at[part, :, some],
            ss.at[spots, some],
            in_n.at[:, some],
            ww.at[spots, some, pl.ds(8, T)],
        )[unit]
        pltpu.make_async_copy(ref, ref, p_recv.at[unit, part, part_v]).wait()

    def gone(unit):
        ref = in_n.at[0 : NI - 1] if unit == 2 else w1.at[:, 0 : NI - 1]
        pltpu.make_async_copy(ref, ref, p_send.at[unit]).wait()

    def near(slot, source, target, device):
        return remote(source, target, d_send.at[slot], d_recv.at[slot], (inst, device))

    def both(slot, out, back):
        return [near(slot, out(0), back(1), left), near(slot + 1, out(1), back(0), right)]

    def start(copies):
        for c in copies:
            c.start()
        return copies

    def over(n, body):
        def step(i, _):
            body(i)
            return 0

        lax.fori_loop(0, n, step, 0)

    lane = lax.broadcasted_iota(jnp.int32, (8, S), 1)
    first_lane = lane == 0
    last_lane = lane == S - 1

    def spanwise(f, c):
        out = []
        for g, h in zip(f, c):
            up, down = g - h, g + h
            after = jnp.where(last_lane, up, pltpu.roll(up, S - 1, 1))
            prior = jnp.where(first_lane, down, pltpu.roll(down, 1, 1))
            out.append(6.0 * h + (after - prior))
        return out

    def spectral(part, part_v, target, plus=None):
        def variable(n):
            v = NV // 2 * part_v + n
            for t0 in range(0, SLAB, 8):
                rows = slice(t0, t0 + 8)
                if plus is None:
                    x = [in_u[part, m, v, rows, :] for m in range(NI)]
                else:
                    x = [w1[part, m, v, rows, :] + plus(m, v, t0) for m in range(NI)]
                for m, g in enumerate(spectral_apply(x)):
                    target[part, m, v, rows, :] = g

        over(NV // 2, variable)

    def inside(out, first_tile, last_tile):
        def tile(i, _):
            t0 = pl.multiple_of(8 * i, 8)
            total = []
            first = []
            second = []
            for a in range(AX):
                u = [cur[v, a, pl.ds(t0, 8), :] for v in range(NV)]
                vel, nu, pres = primitives(u)
                c = centre_terms(u, vel, nu)
                f1 = half_flux(u, vel, pres, 0)
                first.append([f - g for f, g in zip(f1, c)])
                second.append([f + g for f, g in zip(f1, c)])
                f2 = half_flux(u, vel, pres, 1)
                for v in range(NV):
                    a2[v, a, pl.ds(t0 + 8, 8), :] = f2[v] - c[v]
                    b2[v, a, pl.ds(t0 + 8, 8), :] = f2[v] + c[v]
                total.append(spanwise(half_flux(u, vel, pres, 2), c))
            for a in range(AX):
                for v in range(NV):
                    r = total[a][v]
                    if a == AX - 1:
                        r = r + first[a][v]
                    elif a != AX // 2 - 1:
                        r = r + first[a + 1][v]
                    if a == 0:
                        r = r - second[a][v]
                    elif a != AX // 2:
                        r = r - second[a - 1][v]
                    out[v, a, pl.ds(t0, 8), :] = r
            return 0

        lax.fori_loop(first_tile, last_tile, tile, 0)

    def around(out, it, layers):
        for c in layers:
            c.wait_recv()
        low = prev_terms([halo[it, 0, v] for v in range(NV)], 1)
        high = next_terms([halo[it, 1, v] for v in range(NV)], 1)
        for v in range(NV):
            for a in range(AX):
                b2[v, a, 7:8, :] = -low[v][a : a + 1]
                a2[v, a, T + 8 : T + 9, :] = high[v][a : a + 1]

        def variable(v):
            for a in range(AX):
                out[v, a] += a2[v, a, 9 : T + 9] - b2[v, a, 7 : T + 7]

        over(NV, variable)

    def interface(out, it, tiles):
        def ghosts(n):
            i = tiles[0] + n * tiles[2]
            t0 = pl.multiple_of(8 * i, 8)
            for side in range(2):
                taps = [coef[side, n, pl.ds(t0, 8), :] for n in range(3)]
                u = []
                for v in range(NV):
                    g = taps[0] * win[it, side, v, pl.ds(base[side] + t0, 8), :]
                    g = g + taps[1] * win[it, side, v, pl.ds(base[side] + t0 + 1, 8), :]
                    g = g + taps[2] * win[it, side, v, pl.ds(base[side] + t0 + 2, 8), :]
                    u.append(g)
                terms = next_terms(u, 0) if side == 0 else prev_terms(u, 0)
                for v in range(NV):
                    out[v, 1 + side, pl.ds(t0, 8), :] += terms[v]

        over(tiles[1], ghosts)

    def outer_layers(it):
        for side, t in enumerate((0, T - 1)):
            for v in range(NV):
                edge[it, side, v] = cur[v, :, t, :]
            edge[it, side, NV] = jnp.broadcast_to(active, (AX, S))
        return start(
            both(10 * it, lambda side: edge.at[it, side], lambda side: halo.at[it, side])
        )

    def interface_rows(it):
        for v in range(NV):
            win[it, 0, v, 0:T] = cur[v, 2]
            win[it, 1, v, T : 2 * T] = cur[v, 1]
        return start(
            [
                near(10 * it + 2, win.at[it, 0, :, 0:T], win.at[it, 0, :, T : 2 * T], left),
                near(10 * it + 3, win.at[it, 1, :, T : 2 * T], win.at[it, 1, :, 0:T], right),
            ]
        )

    def rim_of(slot, out, back, spots):
        return start(
            both(slot, lambda side: out.at[side, :, spots], lambda side: back.at[side, :, spots])
        )

    FRONT, REST = pl.ds(0, 2), pl.ds(2, 2)

    pl.semaphore_wait(barrier, NI + 3)
    for part in range(2):
        for k in range(2):
            send(0, part, k)
    for c in loads:
        c.wait()
    active = jnp.where(lax.broadcasted_iota(jnp.int32, (1, S), 1) < count_s[0], 1.0, 0.0)
    layers = outer_layers(0)
    windows = interface_rows(0)

    def least(t, low):
        cell = dom * T + t
        gaps = (idx_s[0, t] - cell, cell - 1 - idx_s[1, t])
        gaps = [jnp.where(g < 0, g + n_cells, g) for g in gaps]
        return jnp.minimum(low[0], gaps[0]), jnp.minimum(low[1], gaps[1])

    most = (jnp.int32(n_cells), jnp.int32(n_cells))
    offset = [jnp.clip(x, 0, T - 2) for x in lax.fori_loop(0, T, least, most)]
    base = [offset[0], T - 2 - offset[1]]
    eye = lax.broadcasted_iota(jnp.int32, (T, T), 0) == lax.broadcasted_iota(
        jnp.int32, (T, T), 1
    )
    for side in range(2):
        cell = dom * T + lax.broadcasted_iota(jnp.int32, (1, T), 1)
        row = idx_v[side : side + 1, :]
        gap = row - cell if side == 0 else cell - 1 - row
        gap = jnp.where(gap < 0, gap + n_cells, gap)
        step = jnp.where(gap > offset[side], 1.0, 0.0)
        w = wgt_v[side : side + 1, :]
        taps = [(1.0 - step) * w, step * w + (1.0 - step) * (1.0 - w), step * (1.0 - w)]
        if side == 1:
            taps = [step * w, (1.0 - step) * w + step * (1.0 - w), (1.0 - step) * (1.0 - w)]
        for i, tap in enumerate(taps):
            column = jnp.sum(jnp.where(eye, tap, 0.0), axis=1, keepdims=True)
            coef[side, i] = jnp.broadcast_to(column, (T, S))

    half = T // 16
    for k in range(2):
        arrive(0, 0, k)
        spectral(0, k, w1)
        send(1, 0, k)
    inside(n0, 0, half)
    for k in range(2):
        arrive(0, 1, k)
        spectral(1, k, w1)
        send(1, 1, k)
    for v in range(NV):
        slab_out[0, v] = in_u[1, :, v, 0, :]
        slab_out[1, v] = in_u[1, :, v, SLAB - 1, :]
    slabs = start(
        [
            remote(slab_out.at[0], slab_in.at[1], d_send.at[18], d_recv.at[18], below),
            remote(slab_out.at[1], slab_in.at[0], d_send.at[19], d_recv.at[19], above),
        ]
    )
    inside(n0, half, 2 * half)
    around(n0, 0, layers)
    for c in windows:
        c.wait_recv()
    interface(n0, 0, (0, T // 8, 1))
    for k in range(2):
        send(2, 0, k)

    toward = jnp.where(body == 0, 1.0, -1.0)

    def slab_inside(m):
        for t0 in range(0, SLAB, 8):
            rows = slice(t0, t0 + 8)
            u = [in_u[0, m, v, rows, :] for v in range(NV)]
            vel, nu, pres = primitives(u)
            c1 = centre_terms(u, vel, nu)
            f1 = half_flux(u, vel, pres, 0)
            u = [in_u[1, m, v, rows, :] for v in range(NV)]
            vel, nu, pres = primitives(u)
            c = centre_terms(u, vel, nu)
            f = half_flux(u, vel, pres, 0)
            f2 = half_flux(u, vel, pres, 1)
            r = spanwise(half_flux(u, vel, pres, 2), c)
            for v in range(NV):
                slab_a[m, v, t0 : t0 + 8, :] = f2[v] - c[v]
                slab_b[m, v, t0 + 8 : t0 + 16, :] = f2[v] + c[v]
                slab_n[m, v, rows, :] = r[v] + (toward * (f1[v] - f[v]) - (c1[v] + c[v]))

    over(NI, slab_inside)
    for c in slabs:
        c.wait()
    low = prev_terms([slab_in[0, v] for v in range(NV)], 1)
    high = next_terms([slab_in[1, v] for v in range(NV)], 1)
    for v in range(NV):
        slab_b[:, v, 7, :] = -low[v]
        slab_a[:, v, SLAB, :] = high[v]

    def outer(m, v, t0):
        return slab_n[m, v, t0 : t0 + 8, :] + (
            slab_a[m, v, t0 + 1 : t0 + 9, :] - slab_b[m, v, t0 + 7 : t0 + 15, :]
        )

    for k in range(2):
        spectral(1, k, w2, outer)

    def keep_rows(out, spots, times, value):
        for spot in spots:
            for n, t in enumerate(times):
                out[n // (len(times) // 2), n % (len(times) // 2), spot] = value(spot, t)

    def put_rows(back, spots, times):
        for spot in spots:
            for n, t in enumerate(times):
                rr[spot, :, 8 + t, :] = back[n // 2, n % 2, spot]

    ends = (0, 1, T - 2, T - 1)
    outside = (-2, -1, T, T + 1)

    def smoothed(ref, spot, v):
        return (
            0.625 * ref[spot, v, 8 : T + 8]
            + 0.125 * (ref[spot, v, 7 : T + 7] + ref[spot, v, 9 : T + 9])
            + 0.0625 * (ref[spot, v, 6 : T + 6] + ref[spot, v, 10 : T + 10])
        )

    def sums(spots):
        def variable(v):
            for spot in spots:
                rr[spot, v, 8 : T + 8] = n0[v, ORDER[spot]] + ss[spot, v]

        over(NV, variable)

    def first_update(spots):
        def variable(v):
            for spot in spots:
                a = ORDER[spot]
                cur[v, a] = cur[v, a] - 0.05 * (smoothed(rr, spot, v) * active)

        over(NV, variable)

    def first_sum(spot, t):
        return n0[:, ORDER[spot], t, :] + ss[spot, :, t, :]

    arrive(1, 0, 0)
    arrive(1, 0, 1)
    keep_rows(redge, (0, 1), ends, first_sum)
    rim = rim_of(4, redge, rhalo, FRONT)
    sums((0, 1))
    arrive(1, 1, 0)
    arrive(1, 1, 1)
    keep_rows(redge, (2, 3), ends, first_sum)
    rim2 = rim_of(6, redge, rhalo, REST)
    for c in rim:
        c.wait()
    put_rows(rhalo, (0, 1), outside)
    gone(0)
    for c in layers + windows:
        c.wait_send()
    first_update((0, 1))
    windows = interface_rows(1)
    for k in range(2):
        send(3, 1, k)
    sums((2, 3))
    for c in rim2:
        c.wait()
    put_rows(rhalo, (2, 3), outside)
    first_update((2, 3))
    layers = outer_layers(1)

    for k in range(2):
        arrive(2, 0, k)
        spectral(0, k, w2, lambda m, v, t0: in_n[m, v, t0 : t0 + 8, :])
        send(3, 0, k)
    inside(n1, 0, 2 * half)
    around(n1, 1, layers)

    def second_sum(spot, t):
        return n1[:, ORDER[spot], t, :] + ss[spot, :, t, :]

    keep_rows(qedge, (2, 3), ends, second_sum)
    rim2 = rim_of(8, qedge, qhalo, REST)
    for c in windows:
        c.wait_recv()
    interface(n1, 1, (0, 2, T // 8 - 1))
    keep_rows(qedge, (0, 1), ends, second_sum)
    rim = rim_of(12 + 2, qedge, qhalo, FRONT)
    interface(n1, 1, (1, T // 8 - 2, 1))

    far_rows = (0, 1, 2, 3, T - 4, T - 3, T - 2, T - 1)

    def last_source(spot, t):
        return ww[spot, :, 8 + t, :]

    arrive(3, 1, 0)
    arrive(3, 1, 1)
    keep_rows(wedge, (2, 3), far_rows, last_source)
    far2 = rim_of(16, wedge, whalo, REST)
    arrive(3, 0, 0)
    arrive(3, 0, 1)
    keep_rows(wedge, (0, 1), far_rows, last_source)
    far = rim_of(20, wedge, whalo, FRONT)

    def second_update(spots):
        for spot in spots:
            for n in range(2):
                ww[spot, :, 6 + n, :] = whalo[0, 2 + n, spot]
                ww[spot, :, T + 8 + n, :] = whalo[1, n, spot]
            for side in range(2):
                h = [whalo[side, n, spot] for n in range(4)]
                e = [wedge[side, n, spot] for n in range(4)]
                line = h + e[:2] if side == 0 else e[2:] + h
                mask = halo[0, side, NV, 0:1, :]
                for n in range(2):
                    x = line[n : n + 5]
                    z = 0.625 * x[2] + 0.125 * (x[1] + x[3]) + 0.0625 * (x[0] + x[4])
                    t = n - 2 if side == 0 else T + n
                    rr[spot, :, 8 + t, :] = qhalo[side, n, spot] - 0.05 * (z * mask)

        def variable(v):
            for spot in spots:
                a = ORDER[spot]
                rr[spot, v, 8 : T + 8] = (
                    n1[v, a] + ss[spot, v] - 0.05 * (smoothed(ww, spot, v) * active)
                )
                update = smoothed(rr, spot, v) * active
                last_update[v, a] = update
                new_state[v, a] = cur[v, a] - 0.05 * update

        over(NV, variable)

    for c in rim2 + far2:
        c.wait()
    second_update((2, 3))
    for c in rim + far:
        c.wait()
    second_update((0, 1))

    for c in layers + windows:
        c.wait_send()
    for unit in (1, 2, 3):
        gone(unit)


def local(n_dom, flow_state, donor_index, donor_weight, span_count):
    shape = (NV, AX, T, S)
    padded = (NV, AX, T + 16, S)
    pieces = (2, NI, NV, SLAB, S)
    turned = (AX, NV, T + 16, S)
    f32 = jnp.float32
    anywhere = pl.BlockSpec(memory_space=pl.ANY)
    vmem = pl.BlockSpec(memory_space=pltpu.VMEM)
    new_state, last_update = pl.pallas_call(
        functools.partial(kernel, n_dom, n_dom * T),
        out_shape=[jax.ShapeDtypeStruct(shape, f32)] * 2,
        in_specs=[anywhere] * 4,
        out_specs=[vmem, vmem],
        scratch_shapes=[
            pltpu.SMEM((2, T), jnp.int32),
            pltpu.SMEM((1,), jnp.int32),
            pltpu.VMEM((2, T), jnp.int32),
            pltpu.VMEM((2, T), f32),
            pltpu.VMEM(shape, f32),
            pltpu.VMEM(pieces, f32),
            pltpu.VMEM((NI, NV, SLAB, S), f32),
            pltpu.VMEM(pieces, f32),
            pltpu.VMEM(pieces, f32),
            pltpu.VMEM((AX, NV, T, S), f32),
            pltpu.VMEM(turned, f32),
            pltpu.VMEM(shape, f32),
            pltpu.VMEM(shape, f32),
            pltpu.VMEM(turned, f32),
            pltpu.VMEM(padded, f32),
            pltpu.VMEM(padded, f32),
            pltpu.VMEM((2, 3, T, S), f32),
            pltpu.VMEM((ITERS, 2, NV, 2 * T, S), f32),
            pltpu.VMEM((ITERS, 2, NV + 1, AX, S), f32),
            pltpu.VMEM((ITERS, 2, NV + 1, AX, S), f32),
            pltpu.VMEM((2, 2, AX, NV, S), f32),
            pltpu.VMEM((2, 2, AX, NV, S), f32),
            pltpu.VMEM((2, 2, AX, NV, S), f32),
            pltpu.VMEM((2, 2, AX, NV, S), f32),
            pltpu.VMEM((2, 4, AX, NV, S), f32),
            pltpu.VMEM((2, 4, AX, NV, S), f32),
            pltpu.VMEM((NI, NV, SLAB, S), f32),
            pltpu.VMEM((NI, NV, SLAB + 8, S), f32),
            pltpu.VMEM((NI, NV, SLAB + 8, S), f32),
            pltpu.VMEM((2, NV, NI, S), f32),
            pltpu.VMEM((2, NV, NI, S), f32),
            pltpu.SemaphoreType.DMA((5,)),
            pltpu.SemaphoreType.DMA((4,)),
            pltpu.SemaphoreType.DMA((4, 2, 2)),
            pltpu.SemaphoreType.DMA((22,)),
            pltpu.SemaphoreType.DMA((22,)),
        ],
        compiler_params=pltpu.CompilerParams(
            collective_id=0, has_side_effects=True, vmem_limit_bytes=52 * 1024 * 1024
        ),
        cost_estimate=pl.CostEstimate(
            flops=20_000_000, bytes_accessed=3 * PL * T * S * 4, transcendentals=0
        ),
    )(flow_state.reshape(shape), donor_index[0], donor_weight[0], span_count)
    whole = (1, NV, AX, T, S)
    return new_state.reshape(whole), last_update.reshape(whole)


def solution(mesh):
    placed = (
        P("inst", None, None, "dom", None),
        P("inst", None, "dom"),
        P("inst", None, "dom"),
        P("dom"),
    )
    return jax.shard_map(
        functools.partial(local, mesh.shape["dom"]),
        mesh=mesh,
        in_specs=placed,
        out_specs=(P("inst", None, None, "dom", None), P("inst", None, None, "dom", None)),
        check_vma=False,
    )
```

```python
import functools
import math

import jax
import jax.numpy as jnp
import numpy as np
from jax import lax
from jax.experimental import pallas as pl
from jax.experimental.pallas import tpu as pltpu
from jax.sharding import PartitionSpec as P

ITERS = 2
NI = 8
NV = 6
AX = 4
PL = NV * AX
T = 64
S = 128
ZN = 4
SLAB = T // ZN
ORDER = (1, 2, 0, 3)
MESH = pl.DeviceIdType.MESH


def spectral_row():
    k = np.arange(NI)[:, None] - np.arange(NI)[None, :]
    safe = np.where(k == 0, 1.0, np.sin(math.pi * k / NI))
    deriv = np.where(k == 0, 0.0, 0.5 * (-1.0) ** k * np.cos(math.pi * k / NI) / safe)
    return (deriv - 0.1 * deriv @ deriv)[:, 0]


def spectral_apply(x):
    row = spectral_row()
    even = [float(row[j] + row[j + 4]) / 2 for j in range(4)]
    odd = [float(row[j] - row[j + 4]) / 2 for j in range(4)]
    s = [x[z] + x[z + 4] for z in range(4)]
    d = [x[z] - x[z + 4] for z in range(4)]
    q0, q1 = s[0] - s[2], s[1] - s[3]
    s0 = even[0] * q0 + even[3] * q1
    s1 = even[1] * q0 + even[0] * q1
    sym = [s0, s1, -s0, -s1]
    out = [None] * NI
    for z in range(4):
        acc = None
        for y in range(4):
            coef = odd[z - y] if y <= z else -odd[4 + z - y]
            term = coef * d[y]
            acc = term if acc is None else acc + term
        out[z] = sym[z] + acc
        out[z + 4] = sym[z] - acc
    return out


def primitives(u):
    inv = 1.0 / u[0]
    vel = [u[1] * inv, u[2] * inv, u[3] * inv]
    nu = u[5] * inv
    pres = 0.4 * (u[4] - 0.5 * (u[1] * vel[0] + u[2] * vel[1] + u[3] * vel[2]))
    return vel, nu, pres


def centre_terms(u, vel, nu):
    return [
        0.1 * u[0],
        0.1 * u[1] + 0.02 * vel[0],
        0.1 * u[2] + 0.02 * vel[1],
        0.1 * u[3] + 0.02 * vel[2],
        0.1 * u[4],
        0.1 * u[5] + 0.02 * nu,
    ]


def half_flux(u, vel, pres, k):
    h = 0.5 * vel[k]
    f = [0.5 * u[1 + k], u[1] * h, u[2] * h, u[3] * h, (u[4] + pres) * h, u[5] * h]
    f[1 + k] = f[1 + k] + 0.5 * pres
    return f


def next_terms(u, k):
    vel, nu, pres = primitives(u)
    c = centre_terms(u, vel, nu)
    return [f - g for f, g in zip(half_flux(u, vel, pres, k), c)]


def prev_terms(u, k):
    vel, nu, pres = primitives(u)
    c = centre_terms(u, vel, nu)
    return [-(f + g) for f, g in zip(half_flux(u, vel, pres, k), c)]


def kernel(
    n_dom,
    n_cells,
    flow,
    idx,
    wgt,
    count,
    new_state,
    last_update,
    idx_s,
    count_s,
    idx_v,
    wgt_v,
    cur,
    in_u,
    in_n,
    w1,
    w2,
    ss,
    ww,
    n0,
    n1,
    rr,
    a2,
    b2,
    coef,
    win,
    edge,
    halo,
    redge,
    rhalo,
    qedge,
    qhalo,
    wedge,
    whalo,
    slab_n,
    slab_a,
    slab_b,
    slab_out,
    slab_in,
    load_sem,
    p_send,
    p_recv,
    d_send,
    d_recv,
):
    inst = lax.axis_index("inst")
    dom = lax.axis_index("dom")
    left = lax.rem(dom + n_dom - 1, n_dom)
    right = lax.rem(dom + 1, n_dom)

    others = [lax.rem(inst + n, NI) for n in range(1, NI)]
    body, place = inst // ZN, lax.rem(inst, ZN)
    at_start = jnp.where(place == 0, 1, 0)
    at_end = jnp.where(place == ZN - 1, 1, 0)
    before = lax.rem(dom + n_dom - at_start, n_dom)
    beyond = lax.rem(dom + at_end, n_dom)
    below = (body * ZN + lax.rem(place + ZN - 1, ZN), before)
    above = (body * ZN + lax.rem(place + 1, ZN), beyond)

    loads = [
        pltpu.make_async_copy(source, target, load_sem.at[n])
        for n, (source, target) in enumerate(
            ((flow, cur), (idx, idx_s), (idx, idx_v), (wgt, wgt_v), (count, count_s))
        )
    ]
    for c in loads:
        c.start()
    barrier = pltpu.get_barrier_semaphore()
    for j in others:
        pl.semaphore_signal(barrier, inc=1, device_id=(j, dom), device_id_type=MESH)
    for device in ((inst, left), (inst, right), below, above):
        pl.semaphore_signal(barrier, inc=1, device_id=device, device_id_type=MESH)

    def remote(source, target, send, recv, device):
        return pltpu.make_async_remote_copy(
            src_ref=source,
            dst_ref=target,
            send_sem=send,
            recv_sem=recv,
            device_id=device,
            device_id_type=MESH,
        )

    def source_of(unit, partner, part):
        side, slab = partner // ZN, lax.rem(partner, ZN)
        row = 1 + side if part == 0 else (AX - 1) * side
        mine = pl.ds(pl.multiple_of(SLAB * slab, SLAB), SLAB)
        if unit == 0:
            return flow.at[:, row, mine]
        if unit == 2:
            return n0.at[:, row, mine]
        return (w1 if unit == 1 else w2).at[part, partner]

    def target_of(unit, part, slot):
        spot = 2 * part + slot // ZN
        at = SLAB * lax.rem(slot, ZN)
        if unit == 0:
            return in_u.at[part, slot]
        if unit == 1:
            return ss.at[spot, :, pl.ds(pl.multiple_of(at, SLAB), SLAB)]
        if unit == 2:
            return in_n.at[slot]
        return ww.at[spot, :, pl.ds(pl.multiple_of(at + 8, 8), SLAB)]

    def send(unit, part):
        target = target_of(unit, part, inst)
        for j in others:
            remote(
                source_of(unit, j, part), target, p_send.at[unit], p_recv.at[unit, part], (j, dom)
            ).start()
        pltpu.make_async_copy(source_of(unit, inst, part), target, p_recv.at[unit, part]).start()

    def arrive(unit, part):
        spots = pl.ds(2 * part, 2)
        ref = (in_u.at[part], ss.at[spots], in_n, ww.at[spots, :, pl.ds(8, T)])[unit]
        pltpu.make_async_copy(ref, ref, p_recv.at[unit, part]).wait()

    def gone(unit):
        ref = in_n.at[0 : NI - 1] if unit == 2 else w1.at[:, 0 : NI - 1]
        pltpu.make_async_copy(ref, ref, p_send.at[unit]).wait()

    def near(slot, source, target, device):
        return remote(source, target, d_send.at[slot], d_recv.at[slot], (inst, device))

    def both(slot, out, back):
        return [near(slot, out(0), back(1), left), near(slot + 1, out(1), back(0), right)]

    def start(copies):
        for c in copies:
            c.start()
        return copies

    def over(n, body):
        def step(i, _):
            body(i)
            return 0

        lax.fori_loop(0, n, step, 0)

    lane = lax.broadcasted_iota(jnp.int32, (8, S), 1)
    first_lane = lane == 0
    last_lane = lane == S - 1

    def spanwise(f, c):
        out = []
        for g, h in zip(f, c):
            up, down = g - h, g + h
            after = jnp.where(last_lane, up, pltpu.roll(up, S - 1, 1))
            prior = jnp.where(first_lane, down, pltpu.roll(down, 1, 1))
            out.append(6.0 * h + (after - prior))
        return out

    def spectral(part, target, plus=None):
        def variable(v):
            for t0 in range(0, SLAB, 8):
                rows = slice(t0, t0 + 8)
                if plus is None:
                    x = [in_u[part, m, v, rows, :] for m in range(NI)]
                else:
                    x = [w1[part, m, v, rows, :] + plus(m, v, t0) for m in range(NI)]
                for m, g in enumerate(spectral_apply(x)):
                    target[part, m, v, rows, :] = g

        over(NV, variable)

    def inside(out, first_tile, last_tile):
        def tile(i, _):
            t0 = pl.multiple_of(8 * i, 8)
            total = []
            first = []
            second = []
            for a in range(AX):
                u = [cur[v, a, pl.ds(t0, 8), :] for v in range(NV)]
                vel, nu, pres = primitives(u)
                c = centre_terms(u, vel, nu)
                f1 = half_flux(u, vel, pres, 0)
                first.append([f - g for f, g in zip(f1, c)])
                second.append([f + g for f, g in zip(f1, c)])
                f2 = half_flux(u, vel, pres, 1)
                for v in range(NV):
                    a2[v, a, pl.ds(t0 + 8, 8), :] = f2[v] - c[v]
                    b2[v, a, pl.ds(t0 + 8, 8), :] = f2[v] + c[v]
                total.append(spanwise(half_flux(u, vel, pres, 2), c))
            for a in range(AX):
                for v in range(NV):
                    r = total[a][v]
                    if a == AX - 1:
                        r = r + first[a][v]
                    elif a != AX // 2 - 1:
                        r = r + first[a + 1][v]
                    if a == 0:
                        r = r - second[a][v]
                    elif a != AX // 2:
                        r = r - second[a - 1][v]
                    out[v, a, pl.ds(t0, 8), :] = r
            return 0

        lax.fori_loop(first_tile, last_tile, tile, 0)

    def around(out, it, layers):
        for c in layers:
            c.wait_recv()
        low = prev_terms([halo[it, 0, v] for v in range(NV)], 1)
        high = next_terms([halo[it, 1, v] for v in range(NV)], 1)
        for v in range(NV):
            for a in range(AX):
                b2[v, a, 7:8, :] = -low[v][a : a + 1]
                a2[v, a, T + 8 : T + 9, :] = high[v][a : a + 1]

        def variable(v):
            for a in range(AX):
                out[v, a] += a2[v, a, 9 : T + 9] - b2[v, a, 7 : T + 7]

        over(NV, variable)

    def interface(out, it, tiles):
        def ghosts(n):
            i = tiles[0] + n * tiles[2]
            t0 = pl.multiple_of(8 * i, 8)
            for side in range(2):
                taps = [coef[side, n, pl.ds(t0, 8), :] for n in range(3)]
                u = []
                for v in range(NV):
                    g = taps[0] * win[it, side, v, pl.ds(base[side] + t0, 8), :]
                    g = g + taps[1] * win[it, side, v, pl.ds(base[side] + t0 + 1, 8), :]
                    g = g + taps[2] * win[it, side, v, pl.ds(base[side] + t0 + 2, 8), :]
                    u.append(g)
                terms = next_terms(u, 0) if side == 0 else prev_terms(u, 0)
                for v in range(NV):
                    out[v, 1 + side, pl.ds(t0, 8), :] += terms[v]

        over(tiles[1], ghosts)

    def outer_layers(it):
        for side, t in enumerate((0, T - 1)):
            for v in range(NV):
                edge[it, side, v] = cur[v, :, t, :]
            edge[it, side, NV] = jnp.broadcast_to(active, (AX, S))
        return start(
            both(10 * it, lambda side: edge.at[it, side], lambda side: halo.at[it, side])
        )

    def interface_rows(it):
        for v in range(NV):
            win[it, 0, v, 0:T] = cur[v, 2]
            win[it, 1, v, T : 2 * T] = cur[v, 1]
        return start(
            [
                near(10 * it + 2, win.at[it, 0, :, 0:T], win.at[it, 0, :, T : 2 * T], left),
                near(10 * it + 3, win.at[it, 1, :, T : 2 * T], win.at[it, 1, :, 0:T], right),
            ]
        )

    def rim_of(slot, out, back, spots):
        return start(
            both(slot, lambda side: out.at[side, :, spots], lambda side: back.at[side, :, spots])
        )

    FRONT, REST = pl.ds(0, 2), pl.ds(2, 2)

    pl.semaphore_wait(barrier, NI + 3)
    for part in range(2):
        send(0, part)
    for c in loads:
        c.wait()
    active = jnp.where(lax.broadcasted_iota(jnp.int32, (1, S), 1) < count_s[0], 1.0, 0.0)
    layers = outer_layers(0)
    windows = interface_rows(0)

    def least(t, low):
        cell = dom * T + t
        gaps = (idx_s[0, t] - cell, cell - 1 - idx_s[1, t])
        gaps = [jnp.where(g < 0, g + n_cells, g) for g in gaps]
        return jnp.minimum(low[0], gaps[0]), jnp.minimum(low[1], gaps[1])

    most = (jnp.int32(n_cells), jnp.int32(n_cells))
    offset = [jnp.clip(x, 0, T - 2) for x in lax.fori_loop(0, T, least, most)]
    base = [offset[0], T - 2 - offset[1]]
    eye = lax.broadcasted_iota(jnp.int32, (T, T), 0) == lax.broadcasted_iota(
        jnp.int32, (T, T), 1
    )
    for side in range(2):
        cell = dom * T + lax.broadcasted_iota(jnp.int32, (1, T), 1)
        row = idx_v[side : side + 1, :]
        gap = row - cell if side == 0 else cell - 1 - row
        gap = jnp.where(gap < 0, gap + n_cells, gap)
        step = jnp.where(gap > offset[side], 1.0, 0.0)
        w = wgt_v[side : side + 1, :]
        taps = [(1.0 - step) * w, step * w + (1.0 - step) * (1.0 - w), step * (1.0 - w)]
        if side == 1:
            taps = [step * w, (1.0 - step) * w + step * (1.0 - w), (1.0 - step) * (1.0 - w)]
        for i, tap in enumerate(taps):
            column = jnp.sum(jnp.where(eye, tap, 0.0), axis=1, keepdims=True)
            coef[side, i] = jnp.broadcast_to(column, (T, S))

    half = T // 16
    arrive(0, 0)
    spectral(0, w1)
    send(1, 0)
    inside(n0, 0, half)
    arrive(0, 1)
    spectral(1, w1)
    send(1, 1)
    for v in range(NV):
        slab_out[0, v] = in_u[1, :, v, 0, :]
        slab_out[1, v] = in_u[1, :, v, SLAB - 1, :]
    slabs = start(
        [
            remote(slab_out.at[0], slab_in.at[1], d_send.at[18], d_recv.at[18], below),
            remote(slab_out.at[1], slab_in.at[0], d_send.at[19], d_recv.at[19], above),
        ]
    )
    inside(n0, half, 2 * half)
    around(n0, 0, layers)
    for c in windows:
        c.wait_recv()
    interface(n0, 0, (0, T // 8, 1))
    send(2, 0)

    toward = jnp.where(body == 0, 1.0, -1.0)

    def slab_inside(m):
        for t0 in range(0, SLAB, 8):
            rows = slice(t0, t0 + 8)
            u = [in_u[0, m, v, rows, :] for v in range(NV)]
            vel, nu, pres = primitives(u)
            c1 = centre_terms(u, vel, nu)
            f1 = half_flux(u, vel, pres, 0)
            u = [in_u[1, m, v, rows, :] for v in range(NV)]
            vel, nu, pres = primitives(u)
            c = centre_terms(u, vel, nu)
            f = half_flux(u, vel, pres, 0)
            f2 = half_flux(u, vel, pres, 1)
            r = spanwise(half_flux(u, vel, pres, 2), c)
            for v in range(NV):
                slab_a[m, v, t0 : t0 + 8, :] = f2[v] - c[v]
                slab_b[m, v, t0 + 8 : t0 + 16, :] = f2[v] + c[v]
                slab_n[m, v, rows, :] = r[v] + (toward * (f1[v] - f[v]) - (c1[v] + c[v]))

    over(NI, slab_inside)
    for c in slabs:
        c.wait()
    low = prev_terms([slab_in[0, v] for v in range(NV)], 1)
    high = next_terms([slab_in[1, v] for v in range(NV)], 1)
    for v in range(NV):
        slab_b[:, v, 7, :] = -low[v]
        slab_a[:, v, SLAB, :] = high[v]

    def outer(m, v, t0):
        return slab_n[m, v, t0 : t0 + 8, :] + (
            slab_a[m, v, t0 + 1 : t0 + 9, :] - slab_b[m, v, t0 + 7 : t0 + 15, :]
        )

    spectral(1, w2, outer)

    def keep_rows(out, spots, times, value):
        for spot in spots:
            for n, t in enumerate(times):
                out[n // (len(times) // 2), n % (len(times) // 2), spot] = value(spot, t)

    def put_rows(back, spots, times):
        for spot in spots:
            for n, t in enumerate(times):
                rr[spot, :, 8 + t, :] = back[n // 2, n % 2, spot]

    ends = (0, 1, T - 2, T - 1)
    outside = (-2, -1, T, T + 1)

    def smoothed(ref, spot, v):
        return (
            0.625 * ref[spot, v, 8 : T + 8]
            + 0.125 * (ref[spot, v, 7 : T + 7] + ref[spot, v, 9 : T + 9])
            + 0.0625 * (ref[spot, v, 6 : T + 6] + ref[spot, v, 10 : T + 10])
        )

    def sums(spots):
        def variable(v):
            for spot in spots:
                rr[spot, v, 8 : T + 8] = n0[v, ORDER[spot]] + ss[spot, v]

        over(NV, variable)

    def first_update(spots):
        def variable(v):
            for spot in spots:
                a = ORDER[spot]
                cur[v, a] = cur[v, a] - 0.05 * (smoothed(rr, spot, v) * active)

        over(NV, variable)

    def first_sum(spot, t):
        return n0[:, ORDER[spot], t, :] + ss[spot, :, t, :]

    arrive(1, 0)
    keep_rows(redge, (0, 1), ends, first_sum)
    rim = rim_of(4, redge, rhalo, FRONT)
    sums((0, 1))
    arrive(1, 1)
    keep_rows(redge, (2, 3), ends, first_sum)
    rim2 = rim_of(6, redge, rhalo, REST)
    for c in rim:
        c.wait()
    put_rows(rhalo, (0, 1), outside)
    gone(0)
    for c in layers + windows:
        c.wait_send()
    first_update((0, 1))
    windows = interface_rows(1)
    send(3, 1)
    sums((2, 3))
    for c in rim2:
        c.wait()
    put_rows(rhalo, (2, 3), outside)
    first_update((2, 3))
    layers = outer_layers(1)

    inside(n1, 0, half)
    arrive(2, 0)
    spectral(0, w2, lambda m, v, t0: in_n[m, v, t0 : t0 + 8, :])
    send(3, 0)
    inside(n1, half, 2 * half)
    around(n1, 1, layers)

    def second_sum(spot, t):
        return n1[:, ORDER[spot], t, :] + ss[spot, :, t, :]

    keep_rows(qedge, (2, 3), ends, second_sum)
    rim2 = rim_of(8, qedge, qhalo, REST)
    for c in windows:
        c.wait_recv()
    interface(n1, 1, (0, 2, T // 8 - 1))
    keep_rows(qedge, (0, 1), ends, second_sum)
    rim = rim_of(12 + 2, qedge, qhalo, FRONT)
    interface(n1, 1, (1, T // 8 - 2, 1))

    far_rows = (0, 1, 2, 3, T - 4, T - 3, T - 2, T - 1)

    def last_source(spot, t):
        return ww[spot, :, 8 + t, :]

    arrive(3, 1)
    keep_rows(wedge, (2, 3), far_rows, last_source)
    far2 = rim_of(16, wedge, whalo, REST)
    arrive(3, 0)
    keep_rows(wedge, (0, 1), far_rows, last_source)
    far = rim_of(20, wedge, whalo, FRONT)

    def second_update(spots):
        for spot in spots:
            for n in range(2):
                ww[spot, :, 6 + n, :] = whalo[0, 2 + n, spot]
                ww[spot, :, T + 8 + n, :] = whalo[1, n, spot]
            for side in range(2):
                h = [whalo[side, n, spot] for n in range(4)]
                e = [wedge[side, n, spot] for n in range(4)]
                line = h + e[:2] if side == 0 else e[2:] + h
                mask = halo[0, side, NV, 0:1, :]
                for n in range(2):
                    x = line[n : n + 5]
                    z = 0.625 * x[2] + 0.125 * (x[1] + x[3]) + 0.0625 * (x[0] + x[4])
                    t = n - 2 if side == 0 else T + n
                    rr[spot, :, 8 + t, :] = qhalo[side, n, spot] - 0.05 * (z * mask)

        def variable(v):
            for spot in spots:
                a = ORDER[spot]
                rr[spot, v, 8 : T + 8] = (
                    n1[v, a] + ss[spot, v] - 0.05 * (smoothed(ww, spot, v) * active)
                )
                update = smoothed(rr, spot, v) * active
                last_update[v, a] = update
                new_state[v, a] = cur[v, a] - 0.05 * update

        over(NV, variable)

    for c in rim2 + far2:
        c.wait()
    second_update((2, 3))
    for c in rim + far:
        c.wait()
    second_update((0, 1))

    for c in layers + windows:
        c.wait_send()
    for unit in (1, 2, 3):
        gone(unit)


def local(n_dom, flow_state, donor_index, donor_weight, span_count):
    shape = (NV, AX, T, S)
    padded = (NV, AX, T + 16, S)
    pieces = (2, NI, NV, SLAB, S)
    turned = (AX, NV, T + 16, S)
    f32 = jnp.float32
    anywhere = pl.BlockSpec(memory_space=pl.ANY)
    vmem = pl.BlockSpec(memory_space=pltpu.VMEM)
    new_state, last_update = pl.pallas_call(
        functools.partial(kernel, n_dom, n_dom * T),
        out_shape=[jax.ShapeDtypeStruct(shape, f32)] * 2,
        in_specs=[anywhere] * 4,
        out_specs=[vmem, vmem],
        scratch_shapes=[
            pltpu.SMEM((2, T), jnp.int32),
            pltpu.SMEM((1,), jnp.int32),
            pltpu.VMEM((2, T), jnp.int32),
            pltpu.VMEM((2, T), f32),
            pltpu.VMEM(shape, f32),
            pltpu.VMEM(pieces, f32),
            pltpu.VMEM((NI, NV, SLAB, S), f32),
            pltpu.VMEM(pieces, f32),
            pltpu.VMEM(pieces, f32),
            pltpu.VMEM((AX, NV, T, S), f32),
            pltpu.VMEM(turned, f32),
            pltpu.VMEM(shape, f32),
            pltpu.VMEM(shape, f32),
            pltpu.VMEM(turned, f32),
            pltpu.VMEM(padded, f32),
            pltpu.VMEM(padded, f32),
            pltpu.VMEM((2, 3, T, S), f32),
            pltpu.VMEM((ITERS, 2, NV, 2 * T, S), f32),
            pltpu.VMEM((ITERS, 2, NV + 1, AX, S), f32),
            pltpu.VMEM((ITERS, 2, NV + 1, AX, S), f32),
            pltpu.VMEM((2, 2, AX, NV, S), f32),
            pltpu.VMEM((2, 2, AX, NV, S), f32),
            pltpu.VMEM((2, 2, AX, NV, S), f32),
            pltpu.VMEM((2, 2, AX, NV, S), f32),
            pltpu.VMEM((2, 4, AX, NV, S), f32),
            pltpu.VMEM((2, 4, AX, NV, S), f32),
            pltpu.VMEM((NI, NV, SLAB, S), f32),
            pltpu.VMEM((NI, NV, SLAB + 8, S), f32),
            pltpu.VMEM((NI, NV, SLAB + 8, S), f32),
            pltpu.VMEM((2, NV, NI, S), f32),
            pltpu.VMEM((2, NV, NI, S), f32),
            pltpu.SemaphoreType.DMA((5,)),
            pltpu.SemaphoreType.DMA((4,)),
            pltpu.SemaphoreType.DMA((4, 2)),
            pltpu.SemaphoreType.DMA((22,)),
            pltpu.SemaphoreType.DMA((22,)),
        ],
        compiler_params=pltpu.CompilerParams(
            collective_id=0, has_side_effects=True, vmem_limit_bytes=52 * 1024 * 1024
        ),
        cost_estimate=pl.CostEstimate(
            flops=20_000_000, bytes_accessed=3 * PL * T * S * 4, transcendentals=0
        ),
    )(flow_state.reshape(shape), donor_index[0], donor_weight[0], span_count)
    whole = (1, NV, AX, T, S)
    return new_state.reshape(whole), last_update.reshape(whole)


def solution(mesh):
    placed = (
        P("inst", None, None, "dom", None),
        P("inst", None, "dom"),
        P("inst", None, "dom"),
        P("dom"),
    )
    return jax.shard_map(
        functools.partial(local, mesh.shape["dom"]),
        mesh=mesh,
        in_specs=placed,
        out_specs=(P("inst", None, None, "dom", None), P("inst", None, None, "dom", None)),
        check_vma=False,
    )
```

```python
import functools
import math

import jax
import jax.numpy as jnp
import numpy as np
from jax import lax
from jax.experimental import pallas as pl
from jax.experimental.pallas import tpu as pltpu
from jax.sharding import PartitionSpec as P

ITERS = 2
NI = 8
NV = 6
AX = 4
PL = NV * AX
T = 64
S = 128
ZN = 4
SLAB = T // ZN
ORDER = (1, 2, 0, 3)
MESH = pl.DeviceIdType.MESH


def spectral_row():
    k = np.arange(NI)[:, None] - np.arange(NI)[None, :]
    safe = np.where(k == 0, 1.0, np.sin(math.pi * k / NI))
    deriv = np.where(k == 0, 0.0, 0.5 * (-1.0) ** k * np.cos(math.pi * k / NI) / safe)
    return (deriv - 0.1 * deriv @ deriv)[:, 0]


def spectral_apply(x):
    row = spectral_row()
    even = [float(row[j] + row[j + 4]) / 2 for j in range(4)]
    odd = [float(row[j] - row[j + 4]) / 2 for j in range(4)]
    s = [x[z] + x[z + 4] for z in range(4)]
    d = [x[z] - x[z + 4] for z in range(4)]
    q0, q1 = s[0] - s[2], s[1] - s[3]
    s0 = even[0] * q0 + even[3] * q1
    s1 = even[1] * q0 + even[0] * q1
    sym = [s0, s1, -s0, -s1]
    out = [None] * NI
    for z in range(4):
        acc = None
        for y in range(4):
            coef = odd[z - y] if y <= z else -odd[4 + z - y]
            term = coef * d[y]
            acc = term if acc is None else acc + term
        out[z] = sym[z] + acc
        out[z + 4] = sym[z] - acc
    return out


def primitives(u):
    inv = 1.0 / u[0]
    vel = [u[1] * inv, u[2] * inv, u[3] * inv]
    nu = u[5] * inv
    pres = 0.4 * (u[4] - 0.5 * (u[1] * vel[0] + u[2] * vel[1] + u[3] * vel[2]))
    return vel, nu, pres


def centre_terms(u, vel, nu):
    return [
        0.1 * u[0],
        0.1 * u[1] + 0.02 * vel[0],
        0.1 * u[2] + 0.02 * vel[1],
        0.1 * u[3] + 0.02 * vel[2],
        0.1 * u[4],
        0.1 * u[5] + 0.02 * nu,
    ]


def half_flux(u, vel, pres, k):
    h = 0.5 * vel[k]
    f = [0.5 * u[1 + k], u[1] * h, u[2] * h, u[3] * h, (u[4] + pres) * h, u[5] * h]
    f[1 + k] = f[1 + k] + 0.5 * pres
    return f


def next_terms(u, k):
    vel, nu, pres = primitives(u)
    c = centre_terms(u, vel, nu)
    return [f - g for f, g in zip(half_flux(u, vel, pres, k), c)]


def prev_terms(u, k):
    vel, nu, pres = primitives(u)
    c = centre_terms(u, vel, nu)
    return [-(f + g) for f, g in zip(half_flux(u, vel, pres, k), c)]


def kernel(
    n_dom,
    n_cells,
    flow,
    idx,
    wgt,
    count,
    new_state,
    last_update,
    idx_s,
    count_s,
    idx_v,
    wgt_v,
    cur,
    in_u,
    in_n,
    w1,
    w2,
    ss,
    ww,
    n0,
    n1,
    rr,
    a2,
    b2,
    coef,
    win,
    edge,
    halo,
    redge,
    rhalo,
    qedge,
    qhalo,
    wedge,
    whalo,
    slab_n,
    slab_a,
    slab_b,
    slab_out,
    slab_in,
    load_sem,
    p_send,
    p_recv,
    d_send,
    d_recv,
):
    inst = lax.axis_index("inst")
    dom = lax.axis_index("dom")
    left = lax.rem(dom + n_dom - 1, n_dom)
    right = lax.rem(dom + 1, n_dom)

    others = [lax.rem(inst + n, NI) for n in range(1, NI)]
    body, place = inst // ZN, lax.rem(inst, ZN)
    at_start = jnp.where(place == 0, 1, 0)
    at_end = jnp.where(place == ZN - 1, 1, 0)
    before = lax.rem(dom + n_dom - at_start, n_dom)
    beyond = lax.rem(dom + at_end, n_dom)
    below = (body * ZN + lax.rem(place + ZN - 1, ZN), before)
    above = (body * ZN + lax.rem(place + 1, ZN), beyond)

    loads = [
        pltpu.make_async_copy(source, target, load_sem.at[n])
        for n, (source, target) in enumerate(
            ((flow, cur), (idx, idx_s), (idx, idx_v), (wgt, wgt_v), (count, count_s))
        )
    ]
    for c in loads:
        c.start()
    barrier = pltpu.get_barrier_semaphore()
    for j in others:
        pl.semaphore_signal(barrier, inc=1, device_id=(j, dom), device_id_type=MESH)
    for device in ((inst, left), (inst, right), below, above):
        pl.semaphore_signal(barrier, inc=1, device_id=device, device_id_type=MESH)

    def remote(source, target, send, recv, device):
        return pltpu.make_async_remote_copy(
            src_ref=source,
            dst_ref=target,
            send_sem=send,
            recv_sem=recv,
            device_id=device,
            device_id_type=MESH,
        )

    def source_of(unit, partner, part):
        side, slab = partner // ZN, lax.rem(partner, ZN)
        row = 1 + side if part == 0 else (AX - 1) * side
        mine = pl.ds(pl.multiple_of(SLAB * slab, SLAB), SLAB)
        if unit == 0:
            return flow.at[:, row, mine]
        if unit == 2:
            return n0.at[:, row, mine]
        return (w1 if unit == 1 else w2).at[part, partner]

    def target_of(unit, part, slot):
        spot = 2 * part + slot // ZN
        at = SLAB * lax.rem(slot, ZN)
        if unit == 0:
            return in_u.at[part, slot]
        if unit == 1:
            return ss.at[spot, :, pl.ds(pl.multiple_of(at, SLAB), SLAB)]
        if unit == 2:
            return in_n.at[slot]
        return ww.at[spot, :, pl.ds(pl.multiple_of(at + 8, 8), SLAB)]

    def send(unit, part):
        target = target_of(unit, part, inst)
        for j in others:
            remote(
                source_of(unit, j, part), target, p_send.at[unit], p_recv.at[unit, part], (j, dom)
            ).start()
        pltpu.make_async_copy(source_of(unit, inst, part), target, p_recv.at[unit, part]).start()

    def arrive(unit, part):
        spots = pl.ds(2 * part, 2)
        ref = (in_u.at[part], ss.at[spots], in_n, ww.at[spots, :, pl.ds(8, T)])[unit]
        pltpu.make_async_copy(ref, ref, p_recv.at[unit, part]).wait()

    def gone(unit):
        ref = in_n.at[0 : NI - 1] if unit == 2 else w1.at[:, 0 : NI - 1]
        pltpu.make_async_copy(ref, ref, p_send.at[unit]).wait()

    def near(slot, source, target, device):
        return remote(source, target, d_send.at[slot], d_recv.at[slot], (inst, device))

    def both(slot, out, back):
        return [near(slot, out(0), back(1), left), near(slot + 1, out(1), back(0), right)]

    def start(copies):
        for c in copies:
            c.start()
        return copies

    def over(n, body):
        def step(i, _):
            body(i)
            return 0

        lax.fori_loop(0, n, step, 0)

    lane = lax.broadcasted_iota(jnp.int32, (8, S), 1)
    first_lane = lane == 0
    last_lane = lane == S - 1

    def spanwise(f, c):
        out = []
        for g, h in zip(f, c):
            up, down = g - h, g + h
            after = jnp.where(last_lane, up, pltpu.roll(up, S - 1, 1))
            prior = jnp.where(first_lane, down, pltpu.roll(down, 1, 1))
            out.append(6.0 * h + (after - prior))
        return out

    def spectral(part, target, plus=None):
        def variable(v):
            for t0 in range(0, SLAB, 8):
                rows = slice(t0, t0 + 8)
                if plus is None:
                    x = [in_u[part, m, v, rows, :] for m in range(NI)]
                else:
                    x = [w1[part, m, v, rows, :] + plus(m, v, t0) for m in range(NI)]
                for m, g in enumerate(spectral_apply(x)):
                    target[part, m, v, rows, :] = g

        over(NV, variable)

    def inside(out, first_tile, last_tile):
        def tile(i, _):
            t0 = pl.multiple_of(8 * i, 8)
            total = []
            first = []
            second = []
            for a in range(AX):
                u = [cur[v, a, pl.ds(t0, 8), :] for v in range(NV)]
                vel, nu, pres = primitives(u)
                c = centre_terms(u, vel, nu)
                f1 = half_flux(u, vel, pres, 0)
                first.append([f - g for f, g in zip(f1, c)])
                second.append([f + g for f, g in zip(f1, c)])
                f2 = half_flux(u, vel, pres, 1)
                for v in range(NV):
                    a2[v, a, pl.ds(t0 + 8, 8), :] = f2[v] - c[v]
                    b2[v, a, pl.ds(t0 + 8, 8), :] = f2[v] + c[v]
                total.append(spanwise(half_flux(u, vel, pres, 2), c))
            for a in range(AX):
                for v in range(NV):
                    r = total[a][v]
                    if a == AX - 1:
                        r = r + first[a][v]
                    elif a != AX // 2 - 1:
                        r = r + first[a + 1][v]
                    if a == 0:
                        r = r - second[a][v]
                    elif a != AX // 2:
                        r = r - second[a - 1][v]
                    out[v, a, pl.ds(t0, 8), :] = r
            return 0

        lax.fori_loop(first_tile, last_tile, tile, 0)

    def around(out, it, layers):
        for c in layers:
            c.wait_recv()
        low = prev_terms([halo[it, 0, v] for v in range(NV)], 1)
        high = next_terms([halo[it, 1, v] for v in range(NV)], 1)
        for v in range(NV):
            for a in range(AX):
                b2[v, a, 7:8, :] = -low[v][a : a + 1]
                a2[v, a, T + 8 : T + 9, :] = high[v][a : a + 1]

        def variable(v):
            for a in range(AX):
                out[v, a] += a2[v, a, 9 : T + 9] - b2[v, a, 7 : T + 7]

        over(NV, variable)

    def interface(out, it, tiles):
        def ghosts(n):
            i = tiles[0] + n * tiles[2]
            t0 = pl.multiple_of(8 * i, 8)
            for side in range(2):
                taps = [coef[side, n, pl.ds(t0, 8), :] for n in range(3)]
                u = []
                for v in range(NV):
                    g = taps[0] * win[it, side, v, pl.ds(base[side] + t0, 8), :]
                    g = g + taps[1] * win[it, side, v, pl.ds(base[side] + t0 + 1, 8), :]
                    g = g + taps[2] * win[it, side, v, pl.ds(base[side] + t0 + 2, 8), :]
                    u.append(g)
                terms = next_terms(u, 0) if side == 0 else prev_terms(u, 0)
                for v in range(NV):
                    out[v, 1 + side, pl.ds(t0, 8), :] += terms[v]

        over(tiles[1], ghosts)

    def outer_layers(it):
        for side, t in enumerate((0, T - 1)):
            for v in range(NV):
                edge[it, side, v] = cur[v, :, t, :]
            edge[it, side, NV] = jnp.broadcast_to(active, (AX, S))
        return start(
            both(10 * it, lambda side: edge.at[it, side], lambda side: halo.at[it, side])
        )

    def interface_rows(it):
        for v in range(NV):
            win[it, 0, v, 0:T] = cur[v, 2]
            win[it, 1, v, T : 2 * T] = cur[v, 1]
        return start(
            [
                near(10 * it + 2, win.at[it, 0, :, 0:T], win.at[it, 0, :, T : 2 * T], left),
                near(10 * it + 3, win.at[it, 1, :, T : 2 * T], win.at[it, 1, :, 0:T], right),
            ]
        )

    def rim_of(slot, out, back, spots):
        return start(both(slot, lambda side: out.at[side, spots], lambda side: back.at[side, spots]))

    FRONT, REST = pl.ds(0, 2), pl.ds(2, 2)

    pl.semaphore_wait(barrier, NI + 3)
    for part in range(2):
        send(0, part)
    for c in loads:
        c.wait()
    active = jnp.where(lax.broadcasted_iota(jnp.int32, (1, S), 1) < count_s[0], 1.0, 0.0)
    layers = outer_layers(0)
    windows = interface_rows(0)

    def least(t, low):
        cell = dom * T + t
        gaps = (idx_s[0, t] - cell, cell - 1 - idx_s[1, t])
        gaps = [jnp.where(g < 0, g + n_cells, g) for g in gaps]
        return jnp.minimum(low[0], gaps[0]), jnp.minimum(low[1], gaps[1])

    most = (jnp.int32(n_cells), jnp.int32(n_cells))
    offset = [jnp.clip(x, 0, T - 2) for x in lax.fori_loop(0, T, least, most)]
    base = [offset[0], T - 2 - offset[1]]
    eye = lax.broadcasted_iota(jnp.int32, (T, T), 0) == lax.broadcasted_iota(
        jnp.int32, (T, T), 1
    )
    for side in range(2):
        cell = dom * T + lax.broadcasted_iota(jnp.int32, (1, T), 1)
        row = idx_v[side : side + 1, :]
        gap = row - cell if side == 0 else cell - 1 - row
        gap = jnp.where(gap < 0, gap + n_cells, gap)
        step = jnp.where(gap > offset[side], 1.0, 0.0)
        w = wgt_v[side : side + 1, :]
        taps = [(1.0 - step) * w, step * w + (1.0 - step) * (1.0 - w), step * (1.0 - w)]
        if side == 1:
            taps = [step * w, (1.0 - step) * w + step * (1.0 - w), (1.0 - step) * (1.0 - w)]
        for i, tap in enumerate(taps):
            column = jnp.sum(jnp.where(eye, tap, 0.0), axis=1, keepdims=True)
            coef[side, i] = jnp.broadcast_to(column, (T, S))

    half = T // 16
    arrive(0, 0)
    spectral(0, w1)
    send(1, 0)
    inside(n0, 0, half)
    arrive(0, 1)
    spectral(1, w1)
    send(1, 1)
    for v in range(NV):
        slab_out[0, v] = in_u[1, :, v, 0, :]
        slab_out[1, v] = in_u[1, :, v, SLAB - 1, :]
    slabs = start(
        [
            remote(slab_out.at[0], slab_in.at[1], d_send.at[18], d_recv.at[18], below),
            remote(slab_out.at[1], slab_in.at[0], d_send.at[19], d_recv.at[19], above),
        ]
    )
    inside(n0, half, 2 * half)
    around(n0, 0, layers)
    for c in windows:
        c.wait_recv()
    interface(n0, 0, (0, T // 8, 1))
    send(2, 0)

    toward = jnp.where(body == 0, 1.0, -1.0)

    def slab_inside(m):
        for t0 in range(0, SLAB, 8):
            rows = slice(t0, t0 + 8)
            u = [in_u[0, m, v, rows, :] for v in range(NV)]
            vel, nu, pres = primitives(u)
            c1 = centre_terms(u, vel, nu)
            f1 = half_flux(u, vel, pres, 0)
            u = [in_u[1, m, v, rows, :] for v in range(NV)]
            vel, nu, pres = primitives(u)
            c = centre_terms(u, vel, nu)
            f = half_flux(u, vel, pres, 0)
            f2 = half_flux(u, vel, pres, 1)
            r = spanwise(half_flux(u, vel, pres, 2), c)
            for v in range(NV):
                slab_a[m, v, t0 : t0 + 8, :] = f2[v] - c[v]
                slab_b[m, v, t0 + 8 : t0 + 16, :] = f2[v] + c[v]
                slab_n[m, v, rows, :] = r[v] + (toward * (f1[v] - f[v]) - (c1[v] + c[v]))

    over(NI, slab_inside)
    for c in slabs:
        c.wait()
    low = prev_terms([slab_in[0, v] for v in range(NV)], 1)
    high = next_terms([slab_in[1, v] for v in range(NV)], 1)
    for v in range(NV):
        slab_b[:, v, 7, :] = -low[v]
        slab_a[:, v, SLAB, :] = high[v]

    def outer(m, v, t0):
        return slab_n[m, v, t0 : t0 + 8, :] + (
            slab_a[m, v, t0 + 1 : t0 + 9, :] - slab_b[m, v, t0 + 7 : t0 + 15, :]
        )

    spectral(1, w2, outer)

    def keep_rows(out, spots, value):
        n = out.shape[3]
        for spot in spots:
            for v in range(NV):
                out[0, spot, v] = value(spot, v, 0, n)
                out[1, spot, v] = value(spot, v, T - n, T)

    def put_rows(back, spots):
        for spot in spots:
            for v in range(NV):
                rr[spot, v, 6:8, :] = back[0, spot, v]
                rr[spot, v, T + 8 : T + 10, :] = back[1, spot, v]

    def smoothed(ref, spot, v):
        return (
            0.625 * ref[spot, v, 8 : T + 8]
            + 0.125 * (ref[spot, v, 7 : T + 7] + ref[spot, v, 9 : T + 9])
            + 0.0625 * (ref[spot, v, 6 : T + 6] + ref[spot, v, 10 : T + 10])
        )

    def sums(spots):
        def variable(v):
            for spot in spots:
                rr[spot, v, 8 : T + 8] = n0[v, ORDER[spot]] + ss[spot, v]

        over(NV, variable)

    def first_update(spots):
        def variable(v):
            for spot in spots:
                a = ORDER[spot]
                cur[v, a] = cur[v, a] - 0.05 * (smoothed(rr, spot, v) * active)

        over(NV, variable)

    def first_sum(spot, v, t0, t1):
        return n0[v, ORDER[spot], t0:t1, :] + ss[spot, v, t0:t1, :]

    arrive(1, 0)
    keep_rows(redge, (0, 1), first_sum)
    rim = rim_of(4, redge, rhalo, FRONT)
    sums((0, 1))
    arrive(1, 1)
    keep_rows(redge, (2, 3), first_sum)
    rim2 = rim_of(6, redge, rhalo, REST)
    for c in rim:
        c.wait()
    put_rows(rhalo, (0, 1))
    gone(0)
    for c in layers + windows:
        c.wait_send()
    first_update((0, 1))
    windows = interface_rows(1)
    send(3, 1)
    sums((2, 3))
    for c in rim2:
        c.wait()
    put_rows(rhalo, (2, 3))
    first_update((2, 3))
    layers = outer_layers(1)

    inside(n1, 0, half)
    arrive(2, 0)
    spectral(0, w2, lambda m, v, t0: in_n[m, v, t0 : t0 + 8, :])
    send(3, 0)
    inside(n1, half, 2 * half)
    around(n1, 1, layers)

    def second_sum(spot, v, t0, t1):
        return n1[v, ORDER[spot], t0:t1, :] + ss[spot, v, t0:t1, :]

    keep_rows(qedge, (2, 3), second_sum)
    rim2 = rim_of(8, qedge, qhalo, REST)
    for c in windows:
        c.wait_recv()
    interface(n1, 1, (0, 2, T // 8 - 1))
    keep_rows(qedge, (0, 1), second_sum)
    rim = rim_of(12 + 2, qedge, qhalo, FRONT)
    interface(n1, 1, (1, T // 8 - 2, 1))

    def last_source(spot, v, t0, t1):
        return ww[spot, v, 8 + t0 : 8 + t1, :]

    arrive(3, 1)
    keep_rows(wedge, (2, 3), last_source)
    far2 = rim_of(16, wedge, whalo, REST)
    arrive(3, 0)
    keep_rows(wedge, (0, 1), last_source)
    far = rim_of(20, wedge, whalo, FRONT)

    masks = [halo[0, side, NV, 0:1, :] for side in range(2)]

    def second_update(spots):
        def variable(v):
            for spot in spots:
                a = ORDER[spot]
                ww[spot, v, 4:8, :] = whalo[0, spot, v]
                ww[spot, v, T + 8 : T + 12, :] = whalo[1, spot, v]
                for side, t in enumerate((6, T + 8)):
                    z = (
                        0.625 * ww[spot, v, t : t + 2, :]
                        + 0.125 * (ww[spot, v, t - 1 : t + 1, :] + ww[spot, v, t + 1 : t + 3, :])
                        + 0.0625 * (ww[spot, v, t - 2 : t, :] + ww[spot, v, t + 2 : t + 4, :])
                    )
                    rr[spot, v, t : t + 2, :] = qhalo[side, spot, v] - 0.05 * (z * masks[side])
                rr[spot, v, 8 : T + 8] = (
                    n1[v, a] + ss[spot, v] - 0.05 * (smoothed(ww, spot, v) * active)
                )
                update = smoothed(rr, spot, v) * active
                last_update[v, a] = update
                new_state[v, a] = cur[v, a] - 0.05 * update

        over(NV, variable)

    for c in rim2 + far2:
        c.wait()
    second_update((2, 3))
    for c in rim + far:
        c.wait()
    second_update((0, 1))

    for c in layers + windows:
        c.wait_send()
    for unit in (1, 2, 3):
        gone(unit)


def local(n_dom, flow_state, donor_index, donor_weight, span_count):
    shape = (NV, AX, T, S)
    padded = (NV, AX, T + 16, S)
    pieces = (2, NI, NV, SLAB, S)
    turned = (AX, NV, T + 16, S)
    f32 = jnp.float32
    anywhere = pl.BlockSpec(memory_space=pl.ANY)
    vmem = pl.BlockSpec(memory_space=pltpu.VMEM)
    new_state, last_update = pl.pallas_call(
        functools.partial(kernel, n_dom, n_dom * T),
        out_shape=[jax.ShapeDtypeStruct(shape, f32)] * 2,
        in_specs=[anywhere] * 4,
        out_specs=[vmem, vmem],
        scratch_shapes=[
            pltpu.SMEM((2, T), jnp.int32),
            pltpu.SMEM((1,), jnp.int32),
            pltpu.VMEM((2, T), jnp.int32),
            pltpu.VMEM((2, T), f32),
            pltpu.VMEM(shape, f32),
            pltpu.VMEM(pieces, f32),
            pltpu.VMEM((NI, NV, SLAB, S), f32),
            pltpu.VMEM(pieces, f32),
            pltpu.VMEM(pieces, f32),
            pltpu.VMEM((AX, NV, T, S), f32),
            pltpu.VMEM(turned, f32),
            pltpu.VMEM(shape, f32),
            pltpu.VMEM(shape, f32),
            pltpu.VMEM(turned, f32),
            pltpu.VMEM(padded, f32),
            pltpu.VMEM(padded, f32),
            pltpu.VMEM((2, 3, T, S), f32),
            pltpu.VMEM((ITERS, 2, NV, 2 * T, S), f32),
            pltpu.VMEM((ITERS, 2, NV + 1, AX, S), f32),
            pltpu.VMEM((ITERS, 2, NV + 1, AX, S), f32),
            pltpu.VMEM((2, AX, NV, 2, S), f32),
            pltpu.VMEM((2, AX, NV, 2, S), f32),
            pltpu.VMEM((2, AX, NV, 2, S), f32),
            pltpu.VMEM((2, AX, NV, 2, S), f32),
            pltpu.VMEM((2, AX, NV, 4, S), f32),
            pltpu.VMEM((2, AX, NV, 4, S), f32),
            pltpu.VMEM((NI, NV, SLAB, S), f32),
            pltpu.VMEM((NI, NV, SLAB + 8, S), f32),
            pltpu.VMEM((NI, NV, SLAB + 8, S), f32),
            pltpu.VMEM((2, NV, NI, S), f32),
            pltpu.VMEM((2, NV, NI, S), f32),
            pltpu.SemaphoreType.DMA((5,)),
            pltpu.SemaphoreType.DMA((4,)),
            pltpu.SemaphoreType.DMA((4, 2)),
            pltpu.SemaphoreType.DMA((22,)),
            pltpu.SemaphoreType.DMA((22,)),
        ],
        compiler_params=pltpu.CompilerParams(
            collective_id=0, has_side_effects=True, vmem_limit_bytes=52 * 1024 * 1024
        ),
        cost_estimate=pl.CostEstimate(
            flops=20_000_000, bytes_accessed=3 * PL * T * S * 4, transcendentals=0
        ),
    )(flow_state.reshape(shape), donor_index[0], donor_weight[0], span_count)
    whole = (1, NV, AX, T, S)
    return new_state.reshape(whole), last_update.reshape(whole)


def solution(mesh):
    placed = (
        P("inst", None, None, "dom", None),
        P("inst", None, "dom"),
        P("inst", None, "dom"),
        P("dom"),
    )
    return jax.shard_map(
        functools.partial(local, mesh.shape["dom"]),
        mesh=mesh,
        in_specs=placed,
        out_specs=(P("inst", None, None, "dom", None), P("inst", None, None, "dom", None)),
        check_vma=False,
    )
```
